32 devices in a mesh: dp: 8 (over z, x), mp: 4 (over y, core).
Axes of the slice: x: 2, y: 2, z: 4, core: 2. Of those that a mesh axis runs over, the one named last changes fastest.
Arguments:
- tokens: bfloat16 [8, 4, 512, 768], P('dp', None, 'mp'), may hold values from -6 to 6
- memory_init: bfloat16 [20, 768], P('mp', 'dp'), may hold values from -6 to 6
- query_weight: bfloat16 [768, 768], P('dp', 'mp'), may hold values from -0.21875 to 0.21875
- query_bias: bfloat16 [768], P(('mp', 'dp')), may hold values from -3 to 3
- key_weight: bfloat16 [768, 768], P('dp', 'mp'), may hold values from -0.21875 to 0.21875
- value_weight: bfloat16 [768, 768], P('dp', 'mp'), may hold values from -0.21875 to 0.21875
- value_bias: bfloat16 [768], P(('mp', 'dp')), may hold values from -3 to 3
- out_weight: bfloat16 [768, 768], P('mp', 'dp'), may hold values from -1.75 to 1.75
- out_bias: bfloat16 [768], P(('dp', 'mp')), may hold values from -2 to 2
- first_gain: bfloat16 [768], P(('dp', 'mp')), may hold values from 0.25 to 1.75
- first_shift: bfloat16 [768], P(('dp', 'mp')), may hold values from -2 to 2
- up_weight: bfloat16 [768, 3072], P('dp', 'mp'), may hold values from -0.21875 to 0.21875
- up_bias: bfloat16 [3072], P(('mp', 'dp')), may hold values from -3 to 3
- down_weight: bfloat16 [3072, 768], P('mp', 'dp'), may hold values from -0.109375 to 0.109375
- down_bias: bfloat16 [768], P(('dp', 'mp')), may hold values from -2 to 2
- second_gain: bfloat16 [768], P(('dp', 'mp')), may hold values from 0.25 to 1.75
- second_shift: bfloat16 [768], P(('dp', 'mp')), may hold values from -2 to 2
- cotangent: bfloat16 [8, 4, 512, 768], P('dp', None, 'mp'), may hold values from -6 to 6
- group_segs: int32 [6], replicated, may hold values from 1 to 4, as said below
- chain_group: int32 [8], P('dp'), may hold values from 0 to 5
Outputs:
- layer_out: bfloat16 [8, 4, 512, 768], P('dp', None, 'mp')
- input_grad: bfloat16 [8, 4, 512, 768], P('dp', None, 'mp')
- grad_memory_init: float32 [20, 768], P('mp', 'dp')
- grad_query_weight: float32 [768, 768], P('dp', 'mp')
- grad_query_bias: float32 [768], P(('mp', 'dp'))
- grad_key_weight: float32 [768, 768], P('dp', 'mp')
- grad_value_weight: float32 [768, 768], P('dp', 'mp')
- grad_value_bias: float32 [768], P(('mp', 'dp'))
- grad_out_weight: float32 [768, 768], P('mp', 'dp')
- grad_out_bias: float32 [768], P(('dp', 'mp'))
- grad_first_gain: float32 [768], P(('dp', 'mp'))
- grad_first_shift: float32 [768], P(('dp', 'mp'))
- grad_up_weight: float32 [768, 3072], P('dp', 'mp')
- grad_up_bias: float32 [3072], P(('mp', 'dp'))
- grad_down_weight: float32 [3072, 768], P('mp', 'dp')
- grad_down_bias: float32 [768], P(('dp', 'mp'))
- grad_second_gain: float32 [768], P(('dp', 'mp'))
- grad_second_shift: float32 [768], P(('dp', 'mp'))
- memory_norms: float32 [4], replicated
The draws below stay inside these ranges and needn't reach their ends.
Inputs may be any that keep to these rules, and one draw needn't show every extreme that they name: `group_segs`: in every draw the group of chain 0 has 4 segments; every group has 1 to 4 segments.
All inputs are finite; a program needn't handle non-finite values.
Results may differ from the reference program's by a relative error of at most 0.02.
Values may be sent and summed in bfloat16 or wider, within the bound.
No kernel may reach another device: no remote copies, remote signals or barrier semaphores. Data moves between devices by JAX's collectives and lax.ppermute only.
A program may use at most 192 MiB of HBM per device.

```python
import jax
import jax.numpy as jnp
from jax import lax

D = 768
FF = 3072
HEADS = 12
HD = 64
MEM = 20
SEG = 512
MAXSEG = 4
GROUPS = 6
CHAINS = 8


def chain_layout(key):
    base = jax.random.fold_in(key, 7)
    first, second = jax.random.split(base)
    groups = jax.random.randint(first, (CHAINS,), 0, GROUPS, dtype=jnp.int32)
    counts = jax.random.randint(second, (GROUPS,), 1, MAXSEG + 1, dtype=jnp.int32)
    counts = counts.at[groups[0]].set(MAXSEG)
    return (groups, counts)


def draw_group_segs(key, part):
    return chain_layout(key)[1]


def draw_chain_group(key, part):
    return chain_layout(key)[0]


def block_levels(own_key, extent, cuts, low, largest):
    level = 1.0
    for dim, blocks in cuts:
        draws = jax.random.uniform(jax.random.fold_in(jax.random.fold_in(own_key, 6), dim), (blocks,), jnp.float32, low / len(cuts), largest / len(cuts))
        level = level * jnp.repeat(jnp.exp(draws), extent[dim] // blocks).reshape((-1,) + (1,) * (len(extent) - 1 - dim))
    return level


def centred(own_key, dims, scale, limit, pieces=(), kind=jnp.bfloat16):
    level = block_levels(own_key, dims, pieces, -0.22, 0.18) if pieces else 1.0
    values = jax.random.normal(own_key, dims, jnp.float32) * scale * level
    return jnp.minimum(jnp.maximum(values, -limit), limit).astype(kind)


def setup_inputs(seed: int = 0) -> dict:
    seeds = jax.random.split(jax.random.key(seed), 21)
    tokens = centred(seeds[0], (CHAINS, MAXSEG, SEG, D), 1.0, 6.0, ((0, 8), (2, 4)))
    memory_init = centred(seeds[1], (MEM, D), 1.0, 6.0, ((0, 4), (1, 8)))
    query_weight = centred(seeds[2], (D, D), D ** -0.5, 0.21875, ((0, 8), (1, 4)))
    query_bias = centred(seeds[3], (D,), 0.5, 3.0, ((0, 32),))
    key_weight = centred(seeds[4], (D, D), D ** -0.5, 0.21875, ((0, 8), (1, 4)))
    value_weight = centred(seeds[5], (D, D), D ** -0.5, 0.21875, ((0, 8), (1, 4)))
    value_bias = centred(seeds[6], (D,), 0.5, 3.0, ((0, 32),))
    out_weight = centred(seeds[7], (D, D), (D // 64) ** -0.5, 1.75, ((0, 4), (1, 8)))
    out_bias = centred(seeds[8], (D,), 0.3, 2.0, ((0, 32),))
    first_gain = jnp.clip(1.0 + 0.15 * jax.random.normal(seeds[9], (D,), jnp.float32), 0.25, 1.75).astype(jnp.bfloat16)
    first_shift = centred(seeds[10], (D,), 0.3, 2.0, ((0, 32),))
    up_weight = centred(seeds[11], (D, FF), D ** -0.5, 0.21875, ((0, 8), (1, 4)))
    up_bias = centred(seeds[12], (FF,), 0.5, 3.0, ((0, 32),))
    down_weight = centred(seeds[13], (FF, D), FF ** -0.5, 0.109375, ((0, 4), (1, 8)))
    down_bias = centred(seeds[14], (D,), 0.3, 2.0, ((0, 32),))
    second_gain = jnp.clip(1.0 + 0.15 * jax.random.normal(seeds[15], (D,), jnp.float32), 0.25, 1.75).astype(jnp.bfloat16)
    second_shift = centred(seeds[16], (D,), 0.3, 2.0, ((0, 32),))
    cotangent = centred(seeds[17], (CHAINS, MAXSEG, SEG, D), 1.0, 6.0, ((0, 8), (2, 4)))
    group_segs = draw_group_segs(jax.random.fold_in(seeds[20], 71), 0)
    chain_group = draw_chain_group(jax.random.fold_in(seeds[20], 71), 0)
    return dict(tokens=tokens, memory_init=memory_init, query_weight=query_weight, query_bias=query_bias, key_weight=key_weight, value_weight=value_weight, value_bias=value_bias, out_weight=out_weight, out_bias=out_bias, first_gain=first_gain, first_shift=first_shift, up_weight=up_weight, up_bias=up_bias, down_weight=down_weight, down_bias=down_bias, second_gain=second_gain, second_shift=second_shift, cotangent=cotangent, group_segs=group_segs, chain_group=chain_group)


@jax.custom_vjp
def low(v):
    return lax.optimization_barrier(v.astype(jnp.bfloat16)).astype(jnp.float32)

@jax.custom_vjp
def low_back(v):
    return v

def low_keep(v):
    return (low(v), None)

def low_pass(kept, grad):
    return (grad,)

def back_keep(v):
    return (v, None)

def back_low(kept, grad):
    return (low(grad),)
low.defvjp(low_keep, low_pass)
low_back.defvjp(back_keep, back_low)
highest = lax.Precision.HIGHEST

def product(left, right):
    return jnp.dot(left, right, precision=highest, preferred_element_type=jnp.float32)

def layer_norm(resid, gain, shift):
    center = resid - lax.optimization_barrier(jnp.mean(resid, axis=-1, keepdims=True))
    spread = lax.optimization_barrier(jnp.mean(center * center, axis=-1, keepdims=True))
    return center * lax.rsqrt(spread + 1e-05) * gain + shift

def segment(hidden_in, params):
    query_weight, query_bias, key_weight, value_weight, value_bias, out_weight, out_bias, first_gain, first_shift, up_weight, up_bias, down_weight, down_bias, second_gain, second_shift = params
    count = hidden_in.shape[0]
    rounded = low(hidden_in)
    query = low(low_back(product(rounded, query_weight) + query_bias)).reshape(count, HEADS, HD)
    keys = low(low_back(product(rounded, key_weight))).reshape(count, HEADS, HD)
    values = low(low_back(product(rounded, value_weight) + value_bias)).reshape(count, HEADS, HD)
    scores = jnp.einsum('qhd,khd->hqk', query, keys, precision=highest) * HD ** (-0.5)
    scores = low_back(scores)
    probs = low(jax.nn.softmax(scores, axis=-1))
    attended = jnp.einsum('hqk,khd->qhd', probs, values, precision=highest).reshape(count, D)
    attended = low(low_back(attended))
    branch = low_back(product(attended, out_weight))
    normed = layer_norm(hidden_in + branch + out_bias, first_gain, first_shift)
    pre = low_back(product(low(normed), up_weight) + up_bias)
    inner = low(jax.nn.gelu(pre, approximate=False))
    branch_two = low_back(product(inner, down_weight))
    return layer_norm(normed + branch_two + down_bias, second_gain, second_shift)

def reference(tokens, memory_init, query_weight, query_bias, key_weight, value_weight, value_bias, out_weight, out_bias, first_gain, first_shift, up_weight, up_bias, down_weight, down_bias, second_gain, second_shift, cotangent, group_segs, chain_group):
    params = tuple((item.astype(jnp.float32) for item in (memory_init, query_weight, query_bias, key_weight, value_weight, value_bias, out_weight, out_bias, first_gain, first_shift, up_weight, up_bias, down_weight, down_bias, second_gain, second_shift)))
    match = chain_group[:, None] == jnp.arange(GROUPS, dtype=jnp.int32)[None, :]
    seg_count = lax.optimization_barrier(jnp.sum(jnp.where(match, group_segs[None, :], 0), axis=1))
    live = (jnp.arange(MAXSEG, dtype=jnp.int32)[None, :] < seg_count[:, None]).astype(jnp.float32)

    def forward(inputs, weights):

        def chain_fn(pair):
            chain_tokens, chain_live = pair
            memory = weights[0]
            outputs = []
            terms = []
            for index in range(MAXSEG):
                normed = segment(jnp.concatenate([memory, chain_tokens[index]], axis=0), weights[1:])
                memory = normed[:MEM]
                outputs.append(normed[MEM:] * chain_live[index])
                terms.append(chain_live[index] * jnp.mean(memory * memory))
            return (jnp.stack(outputs), jnp.stack(terms))
        result, terms = lax.map(jax.checkpoint(chain_fn), (inputs, live))
        return (result, terms)
    result, pullback, terms = jax.vjp(forward, tokens.astype(jnp.float32), params, has_aux=True)
    input_grad, grads = pullback(cotangent.astype(jnp.float32))
    norms = lax.optimization_barrier(jnp.sum(terms, axis=0)) / CHAINS
    return (result.astype(jnp.bfloat16), input_grad.astype(jnp.bfloat16), grads[0], grads[1], grads[2], grads[3], grads[4], grads[5], grads[6], grads[7], grads[8], grads[9], grads[10], grads[11], grads[12], grads[13], grads[14], grads[15], norms)
```

```python
import functools

import jax
import jax.numpy as jnp
from jax import lax
from jax.experimental import pallas as pl
from jax.experimental.pallas import tpu as pltpu
from jax.sharding import PartitionSpec as P

HD = 64
HPB = 3
BF = jnp.bfloat16
F32 = jnp.float32
VMEM_LIMIT = 60 * 1024 * 1024
NEG = -1e30


def nn(a, b):
    return lax.dot_general(a, b, (((1,), (0,)), ((), ())), preferred_element_type=F32)


def nt(a, b):
    return lax.dot_general(a, b, (((1,), (1,)), ((), ())), preferred_element_type=F32)


def norm_stats(r):
    mean = jnp.mean(r, axis=-1, keepdims=True)
    c = r - mean
    inv = lax.rsqrt(jnp.mean(c * c, axis=-1, keepdims=True) + 1e-05)
    return c * inv, inv


def norm_back(g, xh, inv):
    return inv * (
        g - jnp.mean(g, axis=-1, keepdims=True) - xh * jnp.mean(g * xh, axis=-1, keepdims=True)
    )


def gelu_both(f):
    cdf = 0.5 + 0.5 * lax.erf(f * (0.5**0.5))
    pdf = jnp.exp(-0.5 * f * f) * ((2.0 * jnp.pi) ** -0.5)
    return f * cdf, cdf + f * pdf


def rows_mask(shape, count):
    return lax.broadcasted_iota(jnp.int32, shape, 0) < count


def any_spec():
    return pl.BlockSpec(memory_space=pl.ANY)


def vm_spec():
    return pl.BlockSpec(memory_space=pltpu.VMEM)


def params():
    return pltpu.CompilerParams(vmem_limit_bytes=VMEM_LIMIT)


def qkv_kernel(tok_ref, w_ref, qkvb_ref, out_ref, wc, sem):
    nb = w_ref.shape[0]
    d = tok_ref.shape[1]
    copies = [
        pltpu.make_async_copy(w_ref.at[j, :, 0:d], wc.at[j], sem.at[j]) for j in range(nb)
    ]
    for c in copies:
        c.start()
    w3 = 3 * HPB * HD
    for j in range(nb):
        copies[j].wait()
        acc = nn(tok_ref[...], wc[j, :, 0:w3]) + qkvb_ref[j]
        out_ref[j, :, 0 : HPB * HD] = (acc[:, 0 : HPB * HD].astype(BF) * 0.125).astype(BF)
        out_ref[j, :, HPB * HD : w3] = acc[:, HPB * HD : w3].astype(BF)


def qkv_call(tok, w, qkvb):
    nb, d, _ = w.shape
    s = tok.shape[0]
    return pl.pallas_call(
        qkv_kernel,
        out_shape=jax.ShapeDtypeStruct((nb, s, 3 * HPB * HD), BF),
        in_specs=[vm_spec(), any_spec(), vm_spec()],
        out_specs=vm_spec(),
        scratch_shapes=[pltpu.VMEM((nb, d, d), BF), pltpu.SemaphoreType.DMA((nb,))],
        compiler_params=params(),
        cost_estimate=pl.CostEstimate(
            flops=2 * s * d * 3 * d, bytes_accessed=8 * d * d, transcendentals=0
        ),
        name="qkv",
    )(tok, w, qkvb)


def load_w(w_ref, wv, sem):
    nb = w_ref.shape[0]
    d = w_ref.shape[1]
    copies = {}
    for part in range(3):
        for j in range(nb):
            cols = slice(part * d, (part + 1) * d)
            copies[part, j] = pltpu.make_async_copy(
                w_ref.at[j, :, cols], wv.at[j, :, cols], sem.at[part, j]
            )
            copies[part, j].start()
    return copies


def mem_forward_kernel(
    nmem, save, m_ref, qkvt_ref, w_ref, qkvb_ref, ub_ref, vec_ref, *rest
):
    if save:
        (z2_ref, qkvm_ref, pm_ref, am_ref, z1b_ref, g_ref, gp_ref, xh1_ref, xh2_ref, inv_ref) = rest[:10]
        wv, qkv, sem, sem2 = rest[10:]
    else:
        z2_ref = rest[0]
        wv, qkv, sem, sem2 = rest[1:]
    nb = w_ref.shape[0]
    d = w_ref.shape[1]
    seg = qkvt_ref.shape[1]
    mp = m_ref.shape[0]
    w1 = HPB * HD
    tokcopy = pltpu.make_async_copy(qkvt_ref, qkv.at[:, 0:seg, :], sem2)
    tokcopy.start()
    copies = load_w(w_ref, wv, sem)
    mem = m_ref[...]
    mb = mem.astype(BF)
    tokcopy.wait()
    out = jnp.zeros((mp, d), F32)
    keep = lax.broadcasted_iota(jnp.int32, (mp, seg + mp), 1) < seg + nmem
    for j in range(nb):
        copies[0, j].wait()
        acc = nn(mb, wv[j, :, 0 : 3 * w1]) + qkvb_ref[j]
        qkv[j, seg : seg + mp, 0:w1] = (acc[:, 0:w1].astype(BF) * 0.125).astype(BF)
        qkv[j, seg : seg + mp, w1 : 3 * w1] = acc[:, w1 : 3 * w1].astype(BF)
        parts = [jnp.zeros((mp, HD), F32)]
        for i in range(HPB):
            q = qkv[j, seg : seg + mp, i * HD : (i + 1) * HD]
            k = qkv[j, :, w1 + i * HD : w1 + (i + 1) * HD]
            v = qkv[j, :, 2 * w1 + i * HD : 2 * w1 + (i + 1) * HD]
            s = jnp.where(keep, nt(q, k), NEG)
            e = jnp.exp(s - jnp.max(s, axis=-1, keepdims=True))
            p = (e / jnp.sum(e, axis=-1, keepdims=True)).astype(BF)
            if save:
                pm_ref[j * HPB + i] = p
            parts.append(nn(p, v))
        a = jnp.concatenate(parts, axis=1).astype(BF)
        if save:
            am_ref[j] = a
        out += nt(a, wv[j, :, d - 4 * HD : d])
    xh1, inv1 = norm_stats(mem + out + vec_ref[0:1])
    z1 = xh1 * vec_ref[1:2] + vec_ref[2:3]
    z1b = z1.astype(BF)
    y = jnp.zeros((mp, d), F32)
    for j in range(nb):
        copies[1, j].wait()
        copies[2, j].wait()
        f = nn(z1b, wv[j, :, d : 2 * d]) + ub_ref[j]
        g, gp = gelu_both(f)
        g = g.astype(BF)
        if save:
            g_ref[j] = g
            gp_ref[j] = gp
        y += nt(g, wv[j, :, 2 * d : 3 * d])
    xh2, inv2 = norm_stats(z1 + y + vec_ref[3:4])
    z2 = xh2 * vec_ref[4:5] + vec_ref[5:6]
    z2_ref[...] = jnp.where(rows_mask((mp, d), nmem), z2, 0.0)
    if save:
        qkvm_ref[...] = qkv[:, seg : seg + mp, :]
        z1b_ref[...] = z1b
        xh1_ref[...] = xh1
        xh2_ref[...] = xh2
        inv_ref[:, 0:128] = jnp.broadcast_to(inv1, (mp, 128))
        inv_ref[:, 128:256] = jnp.broadcast_to(inv2, (mp, 128))


def mem_forward(m, qkvt, w, qkvb, ub, vec, nmem, save):
    nb, d, _ = w.shape
    seg = qkvt.shape[1]
    mp = m.shape[0]
    sds = jax.ShapeDtypeStruct
    shapes = [sds((mp, d), F32)]
    if save:
        shapes += [
            sds((nb, mp, 3 * HPB * HD), BF),
            sds((nb * HPB, mp, seg + mp), BF),
            sds((nb, mp, 4 * HD), BF),
            sds((mp, d), BF),
            sds((nb, mp, d), BF),
            sds((nb, mp, d), F32),
            sds((mp, d), F32),
            sds((mp, d), F32),
            sds((mp, 256), F32),
        ]
    return pl.pallas_call(
        functools.partial(mem_forward_kernel, nmem, save),
        out_shape=shapes,
        in_specs=[vm_spec(), any_spec(), any_spec(), vm_spec(), vm_spec(), vm_spec()],
        out_specs=[vm_spec()] * len(shapes),
        scratch_shapes=[
            pltpu.VMEM((nb, d, 3 * d), BF),
            pltpu.VMEM((nb, seg + mp, 3 * HPB * HD), BF),
            pltpu.SemaphoreType.DMA((3, nb)),
            pltpu.SemaphoreType.DMA,
        ],
        compiler_params=params(),
        cost_estimate=pl.CostEstimate(
            flops=2 * mp * d * d * 12, bytes_accessed=24 * d * d, transcendentals=0
        ),
        name="mem_forward",
    )(m, qkvt, w, qkvb, ub, vec)


def colsum(x):
    return jnp.sum(x, axis=0, keepdims=True)


CH = 64


def token_kernel(
    nmem,
    tok_ref,
    ct_ref,
    live_ref,
    m_ref,
    qkvt_ref,
    w_ref,
    qkvb_ref,
    ub_ref,
    vec_ref,
    out_ref,
    z1b_ref,
    a_ref,
    g_ref,
    gf_ref,
    gr2b_ref,
    gr1_ref,
    gq_ref,
    gkv_ref,
    base_ref,
    small_ref,
    ubg_ref,
    wv,
    qkv,
    probs,
    big,
    one,
    xh1,
    xh2,
    inv,
    gp,
    sem,
    sem2,
):
    nb, d, _ = w_ref.shape
    seg = tok_ref.shape[0]
    mp = m_ref.shape[0]
    keys = seg + mp
    w1 = HPB * HD
    steps = seg // CH
    tokcopy = pltpu.make_async_copy(qkvt_ref, qkv.at[:, 0:seg, :], sem2)
    tokcopy.start()
    copies = load_w(w_ref, wv, sem)
    mb = m_ref[...].astype(BF)
    for j in range(nb):
        copies[0, j].wait()
        acc = nn(mb, wv[j, :, 0 : 3 * w1]) + qkvb_ref[j]
        qkv[j, seg:keys, 0:w1] = (acc[:, 0:w1].astype(BF) * 0.125).astype(BF)
        qkv[j, seg:keys, w1 : 3 * w1] = acc[:, w1 : 3 * w1].astype(BF)
    tokcopy.wait()
    one[...] = jnp.zeros_like(one)
    tail = seg + (nmem // 8) * 8

    def attend(j, _):
        vt = qkv[j, :, 2 * w1 : 3 * w1].astype(F32).T.astype(BF)
        parts = [jnp.zeros((HD, seg), F32)]
        for i in range(HPB):
            q = qkv[j, 0:seg, i * HD : (i + 1) * HD]
            k = qkv[j, :, w1 + i * HD : w1 + (i + 1) * HD]
            big[0:keys, 0:seg] = nt(k, q)
            big[tail:keys, 0:seg] = jnp.where(
                rows_mask((keys - tail, seg), seg + nmem - tail), big[tail:keys, 0:seg], NEG
            )
            for c in range(seg // 128):
                cols = slice(c * 128, (c + 1) * 128)
                s = big[0:keys, cols]
                e = jnp.exp(s - jnp.max(s, axis=0, keepdims=True))
                p = e * (1.0 / jnp.sum(e, axis=0, keepdims=True))
                probs[j * HPB + i, :, cols] = p.astype(BF)
            parts.append(nn(vt[i * HD : (i + 1) * HD], probs[j * HPB + i]))
        a = jnp.concatenate(parts, axis=0).T.astype(BF)
        a_ref[j] = a
        one[...] += nt(a, wv[j, :, d - 4 * HD : d])
        return 0

    lax.fori_loop(0, nb, attend, 0)

    def first(c, _):
        rows = pl.ds(pl.multiple_of(c * CH, CH), CH)
        r = tok_ref[rows, :].astype(F32) + one[rows, :] + vec_ref[0:1]
        x, v = norm_stats(r)
        xh1[rows, :] = x
        inv[rows, 0:128] = jnp.broadcast_to(v, (CH, 128))
        z1 = x * vec_ref[1:2] + vec_ref[2:3]
        z1b_ref[rows, :] = z1.astype(BF)
        one[rows, :] = z1 + vec_ref[3:4]
        return 0

    lax.fori_loop(0, steps, first, 0)
    for part in (1, 2):
        for j in range(nb):
            copies[part, j].wait()

    def feed(j, _):
        big[0:seg, 0:d] = nn(z1b_ref[...], wv[j, :, d : 2 * d])

        def act(c, _):
            rows = pl.ds(pl.multiple_of(c * 32, 32), 32)
            g, p = gelu_both(big[rows, 0:d] + ub_ref[j])
            g_ref[j, rows, :] = g.astype(BF)
            gp[j, rows, :] = p.astype(BF)
            return 0

        lax.fori_loop(0, seg // 32, act, 0)
        one[...] += nt(g_ref[j], wv[j, :, 2 * d : 3 * d])
        return 0

    lax.fori_loop(0, nb, feed, 0)
    zero = jnp.zeros((1, d), F32)

    def second(c, carry):
        sg, ss, sb = carry
        rows = pl.ds(pl.multiple_of(c * CH, CH), CH)
        x, v = norm_stats(one[rows, :])
        out_ref[rows, :] = ((x * vec_ref[4:5] + vec_ref[5:6]) * live_ref[0:1, 0:1]).astype(BF)
        gz = ct_ref[rows, :].astype(F32) * live_ref[0:1, 0:1]
        gr = norm_back(gz * vec_ref[4:5], x, v)
        one[rows, :] = gr
        gr2b_ref[rows, :] = gr.astype(BF)
        return (sg + colsum(gz * x), ss + colsum(gz), sb + colsum(gr))

    sg, ss, sb = lax.fori_loop(0, steps, second, (zero, zero, zero))
    small_ref[3:4] = sb
    small_ref[4:5] = sg
    small_ref[5:6] = ss

    def feed_back(j, _):
        big[0:seg, 0:d] = nn(gr2b_ref[...], wv[j, :, 2 * d : 3 * d])

        def act(c, total):
            rows = pl.ds(pl.multiple_of(c * CH, CH), CH)
            gf = (big[rows, 0:d] * gp[j, rows, :].astype(F32)).astype(BF)
            gf_ref[j, rows, :] = gf
            return total + colsum(gf.astype(F32))

        ubg_ref[j] = lax.fori_loop(0, steps, act, zero)
        one[...] += nt(gf_ref[j], wv[j, :, d : 2 * d])
        return 0

    lax.fori_loop(0, nb, feed_back, 0)

    def first_back(c, carry):
        sg, ss, sb = carry
        rows = pl.ds(pl.multiple_of(c * CH, CH), CH)
        gz = one[rows, :]
        x = xh1[rows, :]
        gr = norm_back(gz * vec_ref[1:2], x, inv[rows, 0:1])
        gr1_ref[rows, :] = gr
        xh2[rows, :] = gr.astype(BF)
        return (sg + colsum(gz * x), ss + colsum(gz), sb + colsum(gr))

    sg, ss, sb = lax.fori_loop(0, steps, first_back, (zero, zero, zero))
    small_ref[0:1] = sb
    small_ref[1:2] = sg
    small_ref[2:3] = ss
    small_ref[6:8] = jnp.zeros((2, d), F32)

    def attend_back(j, base):
        ga = nn(xh2[...], wv[j, :, d - 4 * HD : d])
        gab = ga.astype(BF)
        delta = (gab.astype(F32) * a_ref[j].astype(F32)).T
        kt = qkv[j, :, w1 : 2 * w1].astype(F32).T.astype(BF)
        gqs = []
        gks = []
        gvs = []
        for i in range(HPB):
            q = qkv[j, 0:seg, i * HD : (i + 1) * HD]
            v = qkv[j, :, 2 * w1 + i * HD : 2 * w1 + (i + 1) * HD]
            g = gab[:, (i + 1) * HD : (i + 2) * HD]
            p = probs[j * HPB + i]
            dl = jnp.sum(delta[(i + 1) * HD : (i + 2) * HD], axis=0, keepdims=True)
            gvs.append(nn(p, g))
            gs = (p.astype(F32) * (nt(v, g) - dl)).astype(BF)
            gks.append(nn(gs, q))
            gqs.append(nn(kt[i * HD : (i + 1) * HD], gs))
        gq_ref[j] = (jnp.concatenate(gqs, axis=0).T * 0.125).astype(BF)
        gkv = jnp.concatenate(gks + gvs, axis=1)
        gkv_ref[j] = gkv
        gm = jnp.concatenate([jnp.zeros((mp, w1), F32), gkv[seg:keys]], axis=1).astype(BF)
        return base + nt(gm, wv[j, :, 0 : 3 * w1])

    base_ref[...] = lax.fori_loop(0, nb, attend_back, jnp.zeros((mp, d), F32))


def token_call(tok, ct, live, m, qkvt, w, qkvb, ub, vec, nmem):
    nb, d, _ = w.shape
    seg = tok.shape[0]
    mp = m.shape[0]
    keys = seg + mp
    w1 = HPB * HD
    sds = jax.ShapeDtypeStruct
    shapes = [
        sds((seg, d), BF),
        sds((seg, d), BF),
        sds((nb, seg, 4 * HD), BF),
        sds((nb, seg, d), BF),
        sds((nb, seg, d), BF),
        sds((seg, d), BF),
        sds((seg, d), F32),
        sds((nb, seg, w1), BF),
        sds((nb, keys, 2 * w1), F32),
        sds((mp, d), F32),
        sds((8, d), F32),
        sds((nb, 1, d), F32),
    ]
    return pl.pallas_call(
        functools.partial(token_kernel, nmem),
        out_shape=shapes,
        in_specs=[vm_spec()] * 4 + [any_spec()] * 2 + [vm_spec()] * 3,
        out_specs=[vm_spec()] * len(shapes),
        scratch_shapes=[
            pltpu.VMEM((nb, d, 3 * d), BF),
            pltpu.VMEM((nb, keys, 3 * w1), BF),
            pltpu.VMEM((nb * HPB, keys, seg), BF),
            pltpu.VMEM((keys, d), F32),
            pltpu.VMEM((seg, d), F32),
            pltpu.VMEM((seg, d), F32),
            pltpu.VMEM((seg, d), BF),
            pltpu.VMEM((seg, 128), F32),
            pltpu.VMEM((nb, seg, d), BF),
            pltpu.SemaphoreType.DMA((3, nb)),
            pltpu.SemaphoreType.DMA,
        ],
        compiler_params=params(),
        cost_estimate=pl.CostEstimate(
            flops=5 * seg * d * d * 12, bytes_accessed=60 * d * d, transcendentals=0
        ),
        name="token_rows",
    )(tok, ct, live, m, qkvt, w, qkvb, ub, vec)


def mem_backward_kernel(nmem, full, *refs):
    refs = list(refs)
    (g_ref, qkvt_ref, w_ref, vec_ref, base_ref, qkvm_ref, pm_ref, am_ref, gp_ref, xh1_ref, xh2_ref, inv_ref) = refs[:12]
    refs = refs[12:]
    if full:
        (gq_ref, gkv_ref, gr1t_ref) = refs[:3]
        (gm_ref, gr2b_ref, gf_ref, gr1b_ref, gqkv_ref, ig_ref, small_ref, ubg_ref, qvb_ref) = refs[3:12]
        wv, qkv, one, sem, sem2 = refs[12:]
    else:
        gm_ref = refs[0]
        wv, qkv, sem, sem2 = refs[1:]
    nb, d, _ = w_ref.shape
    seg = qkvt_ref.shape[1]
    mp = g_ref.shape[0]
    keys = seg + mp
    w1 = HPB * HD
    tokcopy = pltpu.make_async_copy(qkvt_ref, qkv.at[:, 0:seg, :], sem2)
    tokcopy.start()
    copies = load_w(w_ref, wv, sem)
    qkv[:, seg:keys, :] = qkvm_ref[...]
    gz = g_ref[...]
    xh2 = xh2_ref[...]
    gr2 = norm_back(gz * vec_ref[4:5], xh2, inv_ref[:, 128:129])
    gr2b = gr2.astype(BF)
    acc = gr2
    for j in range(nb):
        copies[2, j].wait()
        copies[1, j].wait()
        gf = (nn(gr2b, wv[j, :, 2 * d : 3 * d]) * gp_ref[j]).astype(BF)
        if full:
            gf_ref[j] = gf
            ubg_ref[j] = colsum(gf.astype(F32))
        acc += nt(gf, wv[j, :, d : 2 * d])
    xh1 = xh1_ref[...]
    gr1 = norm_back(acc * vec_ref[1:2], xh1, inv_ref[:, 0:1])
    gr1b = gr1.astype(BF)
    if full:
        small_ref[0:1] = colsum(gr1)
        small_ref[1:2] = colsum(acc * xh1)
        small_ref[2:3] = colsum(acc)
        small_ref[3:4] = colsum(gr2)
        small_ref[4:5] = colsum(gz * xh2)
        small_ref[5:6] = colsum(gz)
        small_ref[6:8] = jnp.zeros((2, d), F32)
        gr2b_ref[...] = gr2b
        gr1b_ref[...] = gr1b
        one[...] = gr1t_ref[...]
    tokcopy.wait()
    out = gr1 if full else gr1 + base_ref[...]
    for j in range(nb):
        copies[0, j].wait()
        gab = nn(gr1b, wv[j, :, d - 4 * HD : d]).astype(BF)
        prod = gab.astype(F32) * am_ref[j].astype(F32)
        gqs = []
        gks = []
        gvs = []
        for i in range(HPB):
            q = qkv[j, seg:keys, i * HD : (i + 1) * HD]
            k = qkv[j, :, w1 + i * HD : w1 + (i + 1) * HD]
            v = qkv[j, :, 2 * w1 + i * HD : 2 * w1 + (i + 1) * HD]
            g = gab[:, (i + 1) * HD : (i + 2) * HD]
            p = pm_ref[j * HPB + i]
            pf = p.astype(F32)
            dl = jnp.sum(prod[:, (i + 1) * HD : (i + 2) * HD], axis=1, keepdims=True)
            gs = pf * (nt(g, v) - dl)
            gsb = gs.astype(BF)
            gqs.append(nn(gsb, k) * 0.125)
            if full:
                gks.append(nn(gsb.astype(F32).T.astype(BF), q))
                gvs.append(nn(pf.T.astype(BF), g))
            else:
                gks.append(nn(gsb[:, seg:keys].astype(F32).T.astype(BF), q))
                gvs.append(nn(pf[:, seg:keys].T.astype(BF), g))
        gq = jnp.concatenate(gqs, axis=1)
        gkv = jnp.concatenate(gks + gvs, axis=1)
        if full:
            gkv = gkv + gkv_ref[j]
            gqkv_ref[j, 0:seg, 0:w1] = gq_ref[j]
            gqkv_ref[j, seg:keys, 0:w1] = gq.astype(BF)
            gkvb = gkv.astype(BF)
            gqkv_ref[j, :, w1 : 3 * w1] = gkvb
            qvb_ref[j, :, 0 : 3 * w1] = jnp.concatenate(
                [
                    colsum(gq_ref[j].astype(F32)) + colsum(gq.astype(BF).astype(F32)),
                    colsum(gkvb.astype(F32)),
                ],
                axis=1,
            )
            one[...] += nt(gqkv_ref[j, 0:seg, :], wv[j, :, 0 : 3 * w1])
            out += nt(gqkv_ref[j, seg:keys, :], wv[j, :, 0 : 3 * w1])
        else:
            gm = jnp.concatenate([gq, gkv], axis=1).astype(BF)
            out += nt(gm, wv[j, :, 0 : 3 * w1])
    gm_ref[...] = out
    if full:
        ig_ref[...] = one[...].astype(BF)


def mem_backward(g, qkvt, w, vec, base, saved, nmem, extra=None):
    full = extra is not None
    nb, d, _ = w.shape
    seg = qkvt.shape[1]
    mp = g.shape[0]
    keys = seg + mp
    w1 = HPB * HD
    qkvm, pm, am, z1b, _, gp, xh1, xh2, inv = saved
    sds = jax.ShapeDtypeStruct
    shapes = [sds((mp, d), F32)]
    args = [g, qkvt, w, vec, base, qkvm, pm, am, gp, xh1, xh2, inv]
    specs = [vm_spec(), any_spec(), any_spec()] + [vm_spec()] * 9
    scratch = [
        pltpu.VMEM((nb, d, 3 * d), BF),
        pltpu.VMEM((nb, keys, 3 * w1), BF),
    ]
    if full:
        args += list(extra)
        specs += [vm_spec()] * 3
        shapes += [
            sds((mp, d), BF),
            sds((nb, mp, d), BF),
            sds((mp, d), BF),
            sds((nb, keys, 3 * w1), BF),
            sds((seg, d), BF),
            sds((8, d), F32),
            sds((nb, 1, d), F32),
            sds((nb, 1, 3 * w1), F32),
        ]
        scratch += [pltpu.VMEM((seg, d), F32)]
    scratch += [pltpu.SemaphoreType.DMA((3, nb)), pltpu.SemaphoreType.DMA]
    return pl.pallas_call(
        functools.partial(mem_backward_kernel, nmem, full),
        out_shape=shapes,
        in_specs=specs,
        out_specs=[vm_spec()] * len(shapes),
        scratch_shapes=scratch,
        compiler_params=params(),
        cost_estimate=pl.CostEstimate(
            flops=2 * mp * d * d * 12, bytes_accessed=24 * d * d, transcendentals=0
        ),
        name="mem_backward_full" if full else "mem_backward",
    )(*args)


def weight_grad_kernel(
    tok_ref, m_ref, gqkv_ref, gr1_ref, gr1m_ref, a_ref, am_ref, z1b_ref, z1m_ref, gf_ref, gfm_ref,
    gr2b_ref, gr2m_ref, g_ref, gm_ref, out_ref, lt
):
    seg, d = tok_ref.shape
    mp = m_ref.shape[0]
    keys = seg + mp
    w1 = HPB * HD

    @pl.when(pl.program_id(0) == 0)
    def _():
        pairs = (
            (tok_ref, m_ref),
            (gr1_ref, gr1m_ref),
            (z1b_ref, z1m_ref),
            (gr2b_ref, gr2m_ref),
        )
        for t, (a, b) in enumerate(pairs):
            lt[t, :, 0:seg] = a[...].astype(F32).T.astype(BF)
            lt[t, :, seg:keys] = b[...].astype(BF).astype(F32).T.astype(BF)

    out_ref[0, :, 0 : 3 * w1] = nn(lt[0], gqkv_ref[0]).astype(BF)
    go = nn(lt[1, :, 0:seg], a_ref[0]) + nn(lt[1, :, seg:keys], am_ref[0])
    out_ref[0, :, 3 * w1 : d] = go[:, HD : HD + w1].astype(BF)
    up = nn(lt[2, :, 0:seg], gf_ref[0]) + nn(lt[2, :, seg:keys], gfm_ref[0])
    out_ref[0, :, d : 2 * d] = up.astype(BF)
    dn = nn(lt[3, :, 0:seg], g_ref[0]) + nn(lt[3, :, seg:keys], gm_ref[0])
    out_ref[0, :, 2 * d : 3 * d] = dn.astype(BF)


def weight_grad(tok, m, gqkv, gr1, gr1m, a, am, z1b, z1m, gf, gfm, gr2b, gr2m, g, gm):
    seg, d = tok.shape
    mp = m.shape[0]
    nb = g.shape[0]
    args = (tok, m, gqkv, gr1, gr1m, a, am, z1b, z1m, gf, gfm, gr2b, gr2m, g, gm)
    specs = []
    for x in args:
        if x.ndim == 2:
            specs.append(pl.BlockSpec(x.shape, lambda j: (0, 0)))
        else:
            specs.append(pl.BlockSpec((1,) + x.shape[1:], lambda j: (j, 0, 0)))
    return pl.pallas_call(
        weight_grad_kernel,
        grid=(nb,),
        out_shape=jax.ShapeDtypeStruct((nb, d, 3 * d), BF),
        in_specs=specs,
        out_specs=pl.BlockSpec((1, d, 3 * d), lambda j: (j, 0, 0)),
        scratch_shapes=[pltpu.VMEM((4, d, seg + mp), BF)],
        compiler_params=params(),
        cost_estimate=pl.CostEstimate(
            flops=2 * seg * d * d * 12, bytes_accessed=48 * d * d, transcendentals=0
        ),
        name="weight_grad",
    )(*args)


def body(
    tokens, memory_init, query_weight, query_bias, key_weight, value_weight, value_bias, out_weight,
    out_bias, first_gain, first_shift, up_weight, up_bias, down_weight, down_bias, second_gain,
    second_shift, cotangent, group_segs, chain_group
):
    nd = lax.axis_size("dp")
    nb = lax.axis_size("mp")
    me = lax.axis_index("mp")
    segments = tokens.shape[1]
    d = tokens.shape[3]
    part = tokens.shape[2]
    seg = part * nb
    nmem = memory_init.shape[0] * nb
    pad = -(-nmem // 16) * 16
    both = ("mp", "dp")
    wl = jnp.concatenate(
        [query_weight, key_weight, value_weight, out_weight.T, up_weight, down_weight.T], axis=1
    )
    w = lax.all_gather(wl, both, axis=0).reshape(nb, d, 3 * d)
    vecs = (out_bias, first_gain, first_shift, down_bias, second_gain, second_shift)
    small = jnp.concatenate(
        (query_bias, value_bias, up_bias) + vecs + (memory_init.reshape(-1),)
    )
    n1 = query_bias.shape[0]
    n2 = up_bias.shape[0]
    sg = lax.all_gather(small, both, axis=0).reshape(nb, nd, -1)
    qb = sg[:, :, 0:n1].reshape(nb, 1, -1).astype(F32)
    vb = sg[:, :, n1 : 2 * n1].reshape(nb, 1, -1).astype(F32)
    qkvb = jnp.concatenate([qb, jnp.zeros_like(qb), vb], axis=2)
    ub = sg[:, :, 2 * n1 : 2 * n1 + n2].reshape(nb, 1, -1).astype(F32)
    at = 2 * n1 + n2
    vec = sg[:, :, at : at + 6 * n1].reshape(nb, nd, 6, n1).transpose(2, 1, 0, 3).reshape(6, d)
    vec = jnp.pad(vec.astype(F32), ((0, 2), (0, 0)))
    ml = memory_init.shape[0]
    m0 = sg[:, :, at + 6 * n1 :].reshape(nb, nd, ml, -1).transpose(0, 2, 1, 3).reshape(nmem, d)
    m0 = jnp.pad(m0.astype(F32), ((0, pad - nmem), (0, 0)))
    tok = lax.all_to_all(tokens[0], "mp", 0, 1, tiled=True).reshape(seg, d)
    ct = lax.all_to_all(cotangent[0], "mp", 0, 1, tiled=True).reshape(seg, d)
    match = chain_group[:, None] == jnp.arange(group_segs.shape[0], dtype=jnp.int32)[None, :]
    count = jnp.sum(jnp.where(match, group_segs[None, :], 0))
    live = (me < count).astype(F32)
    live2 = jnp.full((8, 128), live, F32)
    qkvt = qkv_call(tok, w, qkvb)
    m = jnp.where(me == 0, m0, 0.0)
    own = m
    for s in range(segments - 1):
        (z,) = mem_forward(m, qkvt, w, qkvb, ub, vec, nmem, False)
        m = lax.ppermute(z, "mp", [(s, s + 1)])
        own = own + m
    (out, z1b, a, g, gf, gr2b, gr1, gq, gkv, base, sm, ubg) = token_call(
        tok, ct, live2, own, qkvt, w, qkvb, ub, vec, nmem
    )
    z2m, *saved = mem_forward(own, qkvt, w, qkvb, ub, vec, nmem, True)
    send = base
    gin = jnp.zeros_like(base)
    gw = None
    for s in reversed(range(segments - 1)):
        recv = lax.ppermute(send, "mp", [(s + 1, s)])
        gin = gin + recv
        if s > 0:
            (send,) = mem_backward(recv, qkvt, w, vec, base, saved, nmem)
    gm, gr2m, gfm, gr1m, gqkv, ig, smm, ubgm, qvb = mem_backward(
        gin, qkvt, w, vec, base, saved, nmem, (gq, gkv, gr1)
    )
    qkvm, pm, am, z1m, g_m, gp_m, xh1, xh2, inv = saved
    wg = weight_grad(
        tok, own, gqkv, gr1.astype(BF), gr1m, a, am, z1b, z1m, gf, gfm, gr2b, gr2m, g, g_m
    )
    wg = lax.psum_scatter(
        wg.reshape(nb * nd, d // nd, 3 * d), both, scatter_dimension=0, tiled=False
    ).astype(F32)
    chains = nd * tokens.shape[0]
    norm = live * jnp.sum(z2m * z2m) / (nmem * d * chains)
    norms = jnp.where(jnp.arange(segments) == me, norm, 0.0)
    w1 = d // nb
    smt = (sm + smm)[0:6].reshape(6, nd, nb, n1).transpose(2, 1, 0, 3).reshape(nb, nd, 6 * n1)
    qbg = qvb[:, 0, 0:w1].reshape(nb, nd, n1)
    vbg = qvb[:, 0, 2 * w1 : 3 * w1].reshape(nb, nd, n1)
    ubt = (ubg + ubgm).reshape(nb, nd, n2)
    gmi = jnp.where(me == 0, gm[0:nmem], 0.0).reshape(nb, ml, nd, d // nd).transpose(0, 2, 1, 3)
    smalls = jnp.concatenate(
        [
            qbg, vbg, ubt, smt, gmi.reshape(nb, nd, -1),
            jnp.broadcast_to(norms, (nb, nd, segments)),
        ],
        axis=2,
    ).reshape(nb * nd, -1)
    sr = lax.psum_scatter(smalls, both, scatter_dimension=0, tiled=False)
    vg = sr[at : at + 6 * n1].reshape(6, n1)
    layer_out = lax.all_to_all(out.reshape(nb, part, d), "mp", 0, 0, tiled=True)
    input_grad = lax.all_to_all(ig.reshape(nb, part, d), "mp", 0, 0, tiled=True)
    return (
        layer_out[None],
        input_grad[None],
        sr[at + 6 * n1 : at + 6 * n1 + ml * (d // nd)].reshape(ml, d // nd),
        wg[:, 0:w1],
        sr[0:n1],
        wg[:, w1 : 2 * w1],
        wg[:, 2 * w1 : 3 * w1],
        sr[n1 : 2 * n1],
        wg[:, 3 * w1 : d].T,
        vg[0],
        vg[1],
        vg[2],
        wg[:, d : 2 * d],
        sr[2 * n1 : at],
        wg[:, 2 * d : 3 * d].T,
        vg[3],
        vg[4],
        vg[5],
        sr[at + 6 * n1 + ml * (d // nd) :],
    )


def solution(mesh):
    rows = P("dp", None, "mp", None)
    md, dm = P(("mp", "dp")), P(("dp", "mp"))
    win, wout = P("dp", "mp"), P("mp", "dp")
    in_specs = (
        rows, wout, win, md, win, win, md, wout, dm, dm, dm, win, md, wout, dm, dm, dm, rows, P(),
        P("dp"),
    )
    out_specs = (
        rows, rows, wout, win, md, win, win, md, wout, dm, dm, dm, win, md, wout, dm, dm, dm, P(),
    )
    return jax.shard_map(body, mesh=mesh, in_specs=in_specs, out_specs=out_specs, check_vma=False)
```

```python
import functools

import jax
import jax.numpy as jnp
from jax import lax
from jax.experimental import pallas as pl
from jax.experimental.pallas import tpu as pltpu
from jax.sharding import PartitionSpec as P

HD = 64
HPB = 3
BF = jnp.bfloat16
F32 = jnp.float32
VMEM_LIMIT = 60 * 1024 * 1024
NEG = -1e30


def nn(a, b):
    return lax.dot_general(a, b, (((1,), (0,)), ((), ())), preferred_element_type=F32)


def nt(a, b):
    return lax.dot_general(a, b, (((1,), (1,)), ((), ())), preferred_element_type=F32)


def norm_stats(r):
    mean = jnp.mean(r, axis=-1, keepdims=True)
    c = r - mean
    inv = lax.rsqrt(jnp.mean(c * c, axis=-1, keepdims=True) + 1e-05)
    return c * inv, inv


def norm_back(g, xh, inv):
    return inv * (
        g - jnp.mean(g, axis=-1, keepdims=True) - xh * jnp.mean(g * xh, axis=-1, keepdims=True)
    )


def gelu_both(f):
    cdf = 0.5 + 0.5 * lax.erf(f * (0.5**0.5))
    pdf = jnp.exp(-0.5 * f * f) * ((2.0 * jnp.pi) ** -0.5)
    return f * cdf, cdf + f * pdf


def rows_mask(shape, count):
    return lax.broadcasted_iota(jnp.int32, shape, 0) < count


def any_spec():
    return pl.BlockSpec(memory_space=pl.ANY)


def vm_spec():
    return pl.BlockSpec(memory_space=pltpu.VMEM)


def params():
    return pltpu.CompilerParams(vmem_limit_bytes=VMEM_LIMIT)


def sm_spec():
    return pl.BlockSpec(memory_space=pltpu.SMEM)


class Weights:
    def __init__(self, me, w_ref, wv, sem, order, depth=4):
        d = w_ref.shape[1]
        self.copies = []
        self.place = {}
        for n, (part, j) in enumerate(order):
            cols = slice(part * d, (part + 1) * d)
            self.place[part, j] = n
            self.copies.append(
                pltpu.make_async_copy(w_ref.at[j ^ me, :, cols], wv.at[j, :, cols], sem.at[n])
            )
        self.depth = depth
        self.done = 0
        for c in self.copies[:depth]:
            c.start()

    def wait(self, part, j):
        while self.done <= self.place[part, j]:
            self.copies[self.done].wait()
            if self.done + self.depth < len(self.copies):
                self.copies[self.done + self.depth].start()
            self.done += 1


def split_qkv(acc):
    w1 = HPB * HD
    zero = jnp.zeros((acc.shape[0], HD), BF)
    q = jnp.concatenate([(acc[:, 0:w1].astype(BF) * 0.125).astype(BF), zero], axis=1)
    k = jnp.concatenate([acc[:, w1 : 2 * w1].astype(BF), zero], axis=1)
    v = jnp.concatenate([acc[:, 2 * w1 : 3 * w1].astype(BF), zero], axis=1)
    return q, k, v


def head_cols(shape, i):
    c = lax.broadcasted_iota(jnp.int32, shape, len(shape) - 1)
    return (c >= i * HD) & (c < (i + 1) * HD)


def spread(x):
    return jnp.concatenate(
        [jnp.where(head_cols(x.shape, i), x, jnp.zeros_like(x)) for i in range(HPB)], axis=0
    )


def gather_heads(x):
    n = x.shape[0] // HPB
    out = jnp.zeros((n, x.shape[1]), x.dtype)
    for i in range(HPB):
        out = jnp.where(head_cols(out.shape, i), x[i * n : (i + 1) * n], out)
    return out


def out_cols(a):
    return jnp.concatenate([jnp.zeros((a.shape[0], HD), a.dtype), a[:, 0 : HPB * HD]], axis=1)


def qkv_kernel(me_ref, tok_ref, w_ref, qkvb_ref, q_ref, k_ref, v_ref, wc, sem):
    nb, d, _ = w_ref.shape
    me = me_ref[0]
    w = Weights(me, w_ref, wc, sem, [(0, j) for j in range(nb)])
    for j in range(nb):
        w.wait(0, j)
        acc = nn(tok_ref[...], wc[j, :, 0 : 3 * HPB * HD]) + qkvb_ref[j ^ me]
        q, k, v = split_qkv(acc)
        q_ref[j] = q
        k_ref[j] = k
        v_ref[j] = v


def qkv_call(me, tok, w, qkvb):
    nb, d, _ = w.shape
    s = tok.shape[0]
    return pl.pallas_call(
        qkv_kernel,
        out_shape=[jax.ShapeDtypeStruct((nb, s, 4 * HD), BF)] * 3,
        in_specs=[sm_spec(), vm_spec(), any_spec(), vm_spec()],
        out_specs=[vm_spec()] * 3,
        scratch_shapes=[pltpu.VMEM((nb, d, d), BF), pltpu.SemaphoreType.DMA((nb,))],
        compiler_params=params(),
        cost_estimate=pl.CostEstimate(
            flops=2 * s * d * 3 * d, bytes_accessed=8 * d * d, transcendentals=0
        ),
        name="qkv",
    )(me, tok, w, qkvb)


def mem_forward_kernel(
    nmem, save, me_ref, m_ref, k_hbm, v_hbm, w_ref, qkvb_ref, ub_ref, vec_ref, *rest
):
    if save:
        (
            z2_ref, qm_ref, km_ref, vm_ref, pm_ref, am_ref, z1b_ref, g_ref, gp_ref, xh1_ref,
            xh2_ref, inv_ref,
        ) = rest[:12]
        rest = rest[12:]
    else:
        z2_ref = rest[0]
        rest = rest[1:]
    wv, kk, vv, sc, sem, sem2 = rest
    nb, d, _ = w_ref.shape
    seg = k_hbm.shape[1]
    mp = m_ref.shape[0]
    keys = seg + mp
    w1 = HPB * HD
    me = me_ref[0]
    w = Weights(
        me, w_ref, wv, sem,
        [(0, j) for j in range(nb)] + [(p, j) for j in range(nb) for p in (1, 2)],
    )
    kc = pltpu.make_async_copy(k_hbm, kk.at[:, 0:seg, :], sem2.at[0])
    vc = pltpu.make_async_copy(v_hbm, vv.at[:, 0:seg, :], sem2.at[1])
    kc.start()
    vc.start()
    mem = m_ref[...]
    mb = mem.astype(BF)
    qs = []
    for j in range(nb):
        w.wait(0, j)
        acc = nn(mb, wv[j, :, 0 : 3 * w1]) + qkvb_ref[j ^ me]
        q, k, v = split_qkv(acc)
        qs.append(q)
        kk[j, seg:keys, :] = k
        vv[j, seg:keys, :] = v
        if save:
            qm_ref[j] = q
            km_ref[j] = k
            vm_ref[j] = v
    kc.wait()
    vc.wait()
    n = HPB * mp
    for j in range(nb):
        sc[j * n : (j + 1) * n, :] = nt(spread(qs[j]), kk[j])
    keep = lax.broadcasted_iota(jnp.int32, (n, keys), 1) < seg + nmem
    heads = []
    for j in range(nb):
        s = jnp.where(keep, sc[j * n : (j + 1) * n, :], NEG)
        e = jnp.exp(s - jnp.max(s, axis=-1, keepdims=True))
        p = (e / jnp.sum(e, axis=-1, keepdims=True)).astype(BF)
        if save:
            pm_ref[j] = p
        heads.append(p)
    out = jnp.zeros((mp, d), F32)
    for j in range(nb):
        a = gather_heads(nn(heads[j], vv[j])).astype(BF)
        if save:
            am_ref[j] = a
        out += nt(out_cols(a), wv[j, :, d - 4 * HD : d])
    xh1, inv1 = norm_stats(mem + out + vec_ref[0:1])
    z1 = xh1 * vec_ref[1:2] + vec_ref[2:3]
    z1b = z1.astype(BF)
    y = jnp.zeros((mp, d), F32)
    for j in range(nb):
        w.wait(1, j)
        f = nn(z1b, wv[j, :, d : 2 * d]) + ub_ref[j ^ me]
        g, gp = gelu_both(f)
        g = g.astype(BF)
        if save:
            g_ref[j] = g
            gp_ref[j] = gp
        w.wait(2, j)
        y += nt(g, wv[j, :, 2 * d : 3 * d])
    xh2, inv2 = norm_stats(z1 + y + vec_ref[3:4])
    z2 = xh2 * vec_ref[4:5] + vec_ref[5:6]
    z2_ref[...] = jnp.where(rows_mask((mp, d), nmem), z2, 0.0)
    if save:
        z1b_ref[...] = z1b
        xh1_ref[...] = xh1
        xh2_ref[...] = xh2
        inv_ref[:, 0:128] = jnp.broadcast_to(inv1, (mp, 128))
        inv_ref[:, 128:256] = jnp.broadcast_to(inv2, (mp, 128))


def mem_forward(me, m, k, v, w, qkvb, ub, vec, nmem, save):
    nb, d, _ = w.shape
    seg = k.shape[1]
    mp = m.shape[0]
    keys = seg + mp
    sds = jax.ShapeDtypeStruct
    shapes = [sds((mp, d), F32)]
    if save:
        shapes += [sds((nb, mp, 4 * HD), BF)] * 3
        shapes += [
            sds((nb, HPB * mp, keys), BF),
            sds((nb, mp, 4 * HD), BF),
            sds((mp, d), BF),
            sds((nb, mp, d), BF),
            sds((nb, mp, d), F32),
            sds((mp, d), F32),
            sds((mp, d), F32),
            sds((mp, 256), F32),
        ]
    return pl.pallas_call(
        functools.partial(mem_forward_kernel, nmem, save),
        out_shape=shapes,
        in_specs=[sm_spec(), vm_spec()] + [any_spec()] * 3 + [vm_spec()] * 3,
        out_specs=[vm_spec()] * len(shapes),
        scratch_shapes=[
            pltpu.VMEM((nb, d, 3 * d), BF),
            pltpu.VMEM((nb, keys, 4 * HD), BF),
            pltpu.VMEM((nb, keys, 4 * HD), BF),
            pltpu.VMEM((nb * HPB * mp, keys), F32),
            pltpu.SemaphoreType.DMA((3 * nb,)),
            pltpu.SemaphoreType.DMA((2,)),
        ],
        compiler_params=params(),
        cost_estimate=pl.CostEstimate(
            flops=2 * mp * d * d * 12, bytes_accessed=24 * d * d, transcendentals=0
        ),
        name="mem_forward_save" if save else "mem_forward",
    )(me, m, k, v, w, qkvb, ub, vec)


def colsum(x):
    return jnp.sum(x, axis=0, keepdims=True)


CH = 64


def token_kernel(
    nmem,
    me_ref,
    tok_ref,
    ct_ref,
    live_ref,
    m_ref,
    q_hbm,
    k_hbm,
    v_hbm,
    w_ref,
    qkvb_ref,
    ub_ref,
    vec_ref,
    out_ref,
    z1b_ref,
    a_ref,
    g_ref,
    gf_ref,
    gr2b_ref,
    gr1_ref,
    gq_ref,
    gk_ref,
    gv_ref,
    base_ref,
    small_ref,
    ubg_ref,
    wv,
    qq,
    kk,
    vv,
    probs,
    big,
    one,
    xh1,
    g1b,
    inv,
    gp,
    sem,
    sem2,
):
    nb, d, _ = w_ref.shape
    seg = tok_ref.shape[0]
    mp = m_ref.shape[0]
    keys = seg + mp
    w1 = HPB * HD
    steps = seg // CH
    me = me_ref[0]
    w = Weights(me, w_ref, wv, sem, [(p, j) for p in range(3) for j in range(nb)])
    loads = [
        pltpu.make_async_copy(q_hbm, qq, sem2.at[0]),
        pltpu.make_async_copy(k_hbm, kk.at[:, 0:seg, :], sem2.at[1]),
        pltpu.make_async_copy(v_hbm, vv.at[:, 0:seg, :], sem2.at[2]),
    ]
    for c in loads:
        c.start()
    mb = m_ref[...].astype(BF)
    for j in range(nb):
        w.wait(0, j)
        _, k, v = split_qkv(nn(mb, wv[j, :, 0 : 3 * w1]) + qkvb_ref[j ^ me])
        kk[j, seg:keys, :] = k
        vv[j, seg:keys, :] = v
    for c in loads:
        c.wait()
    one[...] = jnp.zeros_like(one)
    tail = seg + (nmem // 8) * 8

    def attend(j, _):
        vt = vv[j].astype(F32).T.astype(BF)
        parts = []
        for i in range(HPB):
            cols = slice(i * HD, (i + 1) * HD)
            big[0:keys, 0:seg] = nt(kk[j, :, cols], qq[j, :, cols])
            big[tail:keys, 0:seg] = jnp.where(
                rows_mask((keys - tail, seg), seg + nmem - tail), big[tail:keys, 0:seg], NEG
            )
            for c in range(seg // 128):
                cols = slice(c * 128, (c + 1) * 128)
                s = big[0:keys, cols]
                e = jnp.exp(s - jnp.max(s, axis=0, keepdims=True))
                p = e * (1.0 / jnp.sum(e, axis=0, keepdims=True))
                probs[j * HPB + i, :, cols] = p.astype(BF)
            parts.append(nn(vt[i * HD : (i + 1) * HD], probs[j * HPB + i]))
        parts.append(jnp.zeros((HD, seg), F32))
        a = jnp.concatenate(parts, axis=0).T.astype(BF)
        a_ref[j] = a
        one[...] += nt(out_cols(a), wv[j, :, d - 4 * HD : d])
        return 0

    lax.fori_loop(0, nb, attend, 0)

    def first(c, _):
        rows = pl.ds(pl.multiple_of(c * CH, CH), CH)
        r = tok_ref[rows, :].astype(F32) + one[rows, :] + vec_ref[0:1]
        x, v = norm_stats(r)
        xh1[rows, :] = x
        inv[rows, 0:128] = jnp.broadcast_to(v, (CH, 128))
        z1 = x * vec_ref[1:2] + vec_ref[2:3]
        z1b_ref[rows, :] = z1.astype(BF)
        one[rows, :] = z1 + vec_ref[3:4]
        return 0

    lax.fori_loop(0, steps, first, 0)
    w.wait(2, nb - 1)

    def feed(j, _):
        big[0:seg, 0:d] = nn(z1b_ref[...], wv[j, :, d : 2 * d])

        def act(c, _):
            rows = pl.ds(pl.multiple_of(c * 32, 32), 32)
            g, p = gelu_both(big[rows, 0:d] + ub_ref[j ^ me])
            g_ref[j, rows, :] = g.astype(BF)
            gp[j, rows, :] = p.astype(BF)
            return 0

        lax.fori_loop(0, seg // 32, act, 0)
        one[...] += nt(g_ref[j], wv[j, :, 2 * d : 3 * d])
        return 0

    lax.fori_loop(0, nb, feed, 0)
    zero = jnp.zeros((1, d), F32)

    def second(c, carry):
        sg, ss, sb = carry
        rows = pl.ds(pl.multiple_of(c * CH, CH), CH)
        x, v = norm_stats(one[rows, :])
        out_ref[rows, :] = ((x * vec_ref[4:5] + vec_ref[5:6]) * live_ref[0:1, 0:1]).astype(BF)
        gz = ct_ref[rows, :].astype(F32) * live_ref[0:1, 0:1]
        gr = norm_back(gz * vec_ref[4:5], x, v)
        one[rows, :] = gr
        gr2b_ref[rows, :] = gr.astype(BF)
        return (sg + colsum(gz * x), ss + colsum(gz), sb + colsum(gr))

    sg, ss, sb = lax.fori_loop(0, steps, second, (zero, zero, zero))
    small_ref[3:4] = sb
    small_ref[4:5] = sg
    small_ref[5:6] = ss

    def feed_back(j, _):
        big[0:seg, 0:d] = nn(gr2b_ref[...], wv[j, :, 2 * d : 3 * d])

        def act(c, total):
            rows = pl.ds(pl.multiple_of(c * CH, CH), CH)
            gf = (big[rows, 0:d] * gp[j, rows, :].astype(F32)).astype(BF)
            gf_ref[j, rows, :] = gf
            return total + colsum(gf.astype(F32))

        ubg_ref[j] = lax.fori_loop(0, steps, act, zero)
        one[...] += nt(gf_ref[j], wv[j, :, d : 2 * d])
        return 0

    lax.fori_loop(0, nb, feed_back, 0)

    def first_back(c, carry):
        sg, ss, sb = carry
        rows = pl.ds(pl.multiple_of(c * CH, CH), CH)
        gz = one[rows, :]
        x = xh1[rows, :]
        gr = norm_back(gz * vec_ref[1:2], x, inv[rows, 0:1])
        gr1_ref[rows, :] = gr
        g1b[rows, :] = gr.astype(BF)
        return (sg + colsum(gz * x), ss + colsum(gz), sb + colsum(gr))

    sg, ss, sb = lax.fori_loop(0, steps, first_back, (zero, zero, zero))
    small_ref[0:1] = sb
    small_ref[1:2] = sg
    small_ref[2:3] = ss
    small_ref[6:8] = jnp.zeros((2, d), F32)

    def attend_back(j, base):
        ga = nn(g1b[...], wv[j, :, d - 4 * HD : d])[:, HD:]
        gab = ga.astype(BF)
        delta = (gab.astype(F32) * a_ref[j, :, 0:w1].astype(F32)).T
        kt = kk[j].astype(F32).T.astype(BF)
        gqs = []
        gks = []
        gvs = []
        for i in range(HPB):
            cols = slice(i * HD, (i + 1) * HD)
            g = gab[:, cols]
            p = probs[j * HPB + i]
            dl = jnp.sum(delta[cols], axis=0, keepdims=True)
            gvs.append(nn(p, g))
            gs = (p.astype(F32) * (nt(vv[j, :, cols], g) - dl)).astype(BF)
            gks.append(nn(gs, qq[j, :, cols]))
            gqs.append(nn(kt[cols], gs))
        zq = jnp.zeros((HD, seg), F32)
        zk = jnp.zeros((keys, HD), F32)
        gq_ref[j] = (jnp.concatenate(gqs + [zq], axis=0).T * 0.125).astype(BF)
        gk = jnp.concatenate(gks + [zk], axis=1)
        gv = jnp.concatenate(gvs + [zk], axis=1)
        gk_ref[j] = gk
        gv_ref[j] = gv
        gm = jnp.concatenate(
            [jnp.zeros((mp, w1), F32), gk[seg:keys, 0:w1], gv[seg:keys, 0:w1]], axis=1
        ).astype(BF)
        return base + nt(gm, wv[j, :, 0 : 3 * w1])

    base_ref[...] = lax.fori_loop(0, nb, attend_back, jnp.zeros((mp, d), F32))


def token_call(me, tok, ct, live, m, q, k, v, w, qkvb, ub, vec, nmem):
    nb, d, _ = w.shape
    seg = tok.shape[0]
    mp = m.shape[0]
    keys = seg + mp
    sds = jax.ShapeDtypeStruct
    shapes = [
        sds((seg, d), BF),
        sds((seg, d), BF),
        sds((nb, seg, 4 * HD), BF),
        sds((nb, seg, d), BF),
        sds((nb, seg, d), BF),
        sds((seg, d), BF),
        sds((seg, d), F32),
        sds((nb, seg, 4 * HD), BF),
        sds((nb, keys, 4 * HD), F32),
        sds((nb, keys, 4 * HD), F32),
        sds((mp, d), F32),
        sds((8, d), F32),
        sds((nb, 1, d), F32),
    ]
    return pl.pallas_call(
        functools.partial(token_kernel, nmem),
        out_shape=shapes,
        in_specs=[sm_spec()] + [vm_spec()] * 4 + [any_spec()] * 4 + [vm_spec()] * 3,
        out_specs=[vm_spec()] * len(shapes),
        scratch_shapes=[
            pltpu.VMEM((nb, d, 3 * d), BF),
            pltpu.VMEM((nb, seg, 4 * HD), BF),
            pltpu.VMEM((nb, keys, 4 * HD), BF),
            pltpu.VMEM((nb, keys, 4 * HD), BF),
            pltpu.VMEM((nb * HPB, keys, seg), BF),
            pltpu.VMEM((keys, d), F32),
            pltpu.VMEM((seg, d), F32),
            pltpu.VMEM((seg, d), F32),
            pltpu.VMEM((seg, d), BF),
            pltpu.VMEM((seg, 128), F32),
            pltpu.VMEM((nb, seg, d), BF),
            pltpu.SemaphoreType.DMA((3 * nb,)),
            pltpu.SemaphoreType.DMA((3,)),
        ],
        compiler_params=params(),
        cost_estimate=pl.CostEstimate(
            flops=5 * seg * d * d * 12, bytes_accessed=60 * d * d, transcendentals=0
        ),
        name="token_rows",
    )(me, tok, ct, live, m, q, k, v, w, qkvb, ub, vec)


def back_feed(w, wv, nb, d, gz, vec_ref, gp_ref, xh1, xh2, inv_ref, gf_ref=None, ubg_ref=None):
    gr2 = norm_back(gz * vec_ref[4:5], xh2, inv_ref[:, 128:129])
    gr2b = gr2.astype(BF)
    acc = gr2
    for j in range(nb):
        w.wait(2, j)
        gf = (nn(gr2b, wv[j, :, 2 * d : 3 * d]) * gp_ref[j]).astype(BF)
        if gf_ref is not None:
            gf_ref[j] = gf
            ubg_ref[j] = colsum(gf.astype(F32))
        w.wait(1, j)
        acc += nt(gf, wv[j, :, d : 2 * d])
    return gr2, acc, norm_back(acc * vec_ref[1:2], xh1, inv_ref[:, 0:1])


def back_scores(j, gab, am_ref, pm_ref, vv, delta_rows):
    n = HPB * delta_rows
    gs3 = spread(gab)
    a3 = jnp.concatenate([am_ref[j]] * HPB, axis=0)
    dl = jnp.sum(gs3.astype(F32) * a3.astype(F32), axis=1, keepdims=True)
    p = pm_ref[j].astype(F32)
    return gs3, p, (p * (nt(gs3, vv[j]) - dl)).astype(BF)


def mem_backward_kernel(
    nmem, me_ref, g_ref, k_hbm, v_hbm, w_ref, vec_ref, base_ref, qm_ref, km_ref, vm_ref, pm_ref,
    am_ref, gp_ref, xh1_ref, xh2_ref, inv_ref, gm_ref, wv, kk, vv, sem, sem2
):
    nb, d, _ = w_ref.shape
    seg = k_hbm.shape[1]
    mp = g_ref.shape[0]
    keys = seg + mp
    w1 = HPB * HD
    w = Weights(
        me_ref[0], w_ref, wv, sem,
        [(p, j) for j in range(nb) for p in (2, 1)] + [(0, j) for j in range(nb)],
    )
    kc = pltpu.make_async_copy(k_hbm, kk.at[:, 0:seg, :], sem2.at[0])
    vc = pltpu.make_async_copy(v_hbm, vv.at[:, 0:seg, :], sem2.at[1])
    kc.start()
    vc.start()
    kk[:, seg:keys, :] = km_ref[...]
    vv[:, seg:keys, :] = vm_ref[...]
    _, _, gr1 = back_feed(
        w, wv, nb, d, g_ref[...], vec_ref, gp_ref, xh1_ref[...], xh2_ref[...], inv_ref
    )
    gr1b = gr1.astype(BF)
    kc.wait()
    vc.wait()
    gabs = []
    for j in range(nb):
        w.wait(0, j)
        ga = nn(gr1b, wv[j, :, d - 4 * HD : d]).astype(BF)
        gabs.append(jnp.concatenate([ga[:, HD:], jnp.zeros((mp, HD), BF)], axis=1))
    scores = [back_scores(j, gabs[j], am_ref, pm_ref, vv, mp) for j in range(nb)]
    out = gr1 + base_ref[...]
    for j in range(nb):
        gs3, p, gs = scores[j]
        gq = gather_heads(nn(gs, kk[j])) * 0.125
        gk = nn(gs[:, seg:keys].astype(F32).T.astype(BF), spread(qm_ref[j]))
        gv = nn(p[:, seg:keys].T.astype(BF), gs3)
        gm = jnp.concatenate([gq[:, 0:w1], gk[:, 0:w1], gv[:, 0:w1]], axis=1).astype(BF)
        out += nt(gm, wv[j, :, 0 : 3 * w1])
    gm_ref[...] = out


def mem_backward(me, g, k, v, w, vec, base, saved):
    nb, d, _ = w.shape
    seg = k.shape[1]
    mp = g.shape[0]
    keys = seg + mp
    qm, km, vm, pm, am, _, _, gp, xh1, xh2, inv = saved
    args = (me, g, k, v, w, vec, base, qm, km, vm, pm, am, gp, xh1, xh2, inv)
    return pl.pallas_call(
        functools.partial(mem_backward_kernel, 0),
        out_shape=jax.ShapeDtypeStruct((mp, d), F32),
        in_specs=[sm_spec(), vm_spec()] + [any_spec()] * 3 + [vm_spec()] * 11,
        out_specs=vm_spec(),
        scratch_shapes=[
            pltpu.VMEM((nb, d, 3 * d), BF),
            pltpu.VMEM((nb, keys, 4 * HD), BF),
            pltpu.VMEM((nb, keys, 4 * HD), BF),
            pltpu.SemaphoreType.DMA((3 * nb,)),
            pltpu.SemaphoreType.DMA((2,)),
        ],
        compiler_params=params(),
        cost_estimate=pl.CostEstimate(
            flops=2 * mp * d * d * 12, bytes_accessed=24 * d * d, transcendentals=0
        ),
        name="mem_backward",
    )(*args)


def last_feed_kernel(
    me_ref, g_ref, w_ref, vec_ref, gp_ref, xh1_ref, xh2_ref, inv_ref, gr2b_ref, gf_ref, gr1_ref,
    small_ref, ubg_ref, wv, sem
):
    nb, d, _ = w_ref.shape
    w = Weights(me_ref[0], w_ref, wv, sem, [(p, j) for j in range(nb) for p in (2, 1)])
    gz = g_ref[...]
    xh1 = xh1_ref[...]
    xh2 = xh2_ref[...]
    gr2, gz1, gr1 = back_feed(
        w, wv, nb, d, gz, vec_ref, gp_ref, xh1, xh2, inv_ref, gf_ref, ubg_ref
    )
    gr2b_ref[...] = gr2.astype(BF)
    gr1_ref[...] = gr1
    small_ref[0:1] = colsum(gr1)
    small_ref[1:2] = colsum(gz1 * xh1)
    small_ref[2:3] = colsum(gz1)
    small_ref[3:4] = colsum(gr2)
    small_ref[4:5] = colsum(gz * xh2)
    small_ref[5:6] = colsum(gz)
    small_ref[6:8] = jnp.zeros((2, d), F32)


def last_feed(me, g, w, vec, saved):
    nb, d, _ = w.shape
    mp = g.shape[0]
    _, _, _, _, _, _, _, gp, xh1, xh2, inv = saved
    sds = jax.ShapeDtypeStruct
    shapes = [
        sds((mp, d), BF),
        sds((nb, mp, d), BF),
        sds((mp, d), F32),
        sds((8, d), F32),
        sds((nb, 1, d), F32),
    ]
    return pl.pallas_call(
        last_feed_kernel,
        out_shape=shapes,
        in_specs=[sm_spec(), vm_spec(), any_spec()] + [vm_spec()] * 5,
        out_specs=[vm_spec()] * len(shapes),
        scratch_shapes=[pltpu.VMEM((nb, d, 3 * d), BF), pltpu.SemaphoreType.DMA((2 * nb,))],
        compiler_params=params(),
        cost_estimate=pl.CostEstimate(
            flops=2 * mp * d * d * 8, bytes_accessed=16 * d * d, transcendentals=0
        ),
        name="last_feed",
    )(me, g, w, vec, gp, xh1, xh2, inv)


def last_attention_kernel(
    me_ref, gr1m_ref, k_hbm, v_hbm, w_ref, qm_ref, km_ref, vm_ref, pm_ref, am_ref, gq_ref, gk_ref,
    gv_ref, gr1_ref, gm_ref, gqkv_ref, ig_ref, qvb_ref, wv, kk, vv, one, sem, sem2
):
    nb, d, _ = w_ref.shape
    seg = k_hbm.shape[1]
    mp = gr1m_ref.shape[0]
    keys = seg + mp
    w1 = HPB * HD
    w = Weights(me_ref[0], w_ref, wv, sem, [(0, j) for j in range(nb)])
    kc = pltpu.make_async_copy(k_hbm, kk.at[:, 0:seg, :], sem2.at[0])
    vc = pltpu.make_async_copy(v_hbm, vv.at[:, 0:seg, :], sem2.at[1])
    kc.start()
    vc.start()
    kk[:, seg:keys, :] = km_ref[...]
    vv[:, seg:keys, :] = vm_ref[...]
    gr1 = gr1m_ref[...]
    gr1b = gr1.astype(BF)
    kc.wait()
    vc.wait()
    gabs = []
    for j in range(nb):
        w.wait(0, j)
        ga = nn(gr1b, wv[j, :, d - 4 * HD : d]).astype(BF)
        gabs.append(jnp.concatenate([ga[:, HD:], jnp.zeros((mp, HD), BF)], axis=1))
    scores = [back_scores(j, gabs[j], am_ref, pm_ref, vv, mp) for j in range(nb)]
    out = gr1
    for j in range(nb):
        gs3, p, gs = scores[j]
        gq = (gather_heads(nn(gs, kk[j])) * 0.125).astype(BF)
        gk = (gk_ref[j] + nn(gs.astype(F32).T.astype(BF), spread(qm_ref[j]))).astype(BF)
        gv = (gv_ref[j] + nn(p.T.astype(BF), gs3)).astype(BF)
        gqt = gq_ref[j]
        gqkv_ref[j, 0:seg, 0:w1] = gqt[:, 0:w1]
        gqkv_ref[j, seg:keys, 0:w1] = gq[:, 0:w1]
        gqkv_ref[j, :, w1 : 2 * w1] = gk[:, 0:w1]
        gqkv_ref[j, :, 2 * w1 : 3 * w1] = gv[:, 0:w1]
        qvb_ref[j, 0:1, :] = colsum(gqt.astype(F32)) + colsum(gq.astype(F32))
        qvb_ref[j, 1:2, :] = colsum(gv.astype(F32))
        x = nt(gqkv_ref[j, 0:seg, :], wv[j, :, 0 : 3 * w1])
        if j == 0:
            one[...] = gr1_ref[...] + x
        else:
            one[...] += x
        out += nt(gqkv_ref[j, seg:keys, :], wv[j, :, 0 : 3 * w1])
    gm_ref[...] = out
    ig_ref[...] = one[...].astype(BF)


def last_attention(me, gr1m, k, v, w, saved, gq, gk, gv, gr1):
    nb, d, _ = w.shape
    seg = k.shape[1]
    mp = gr1m.shape[0]
    keys = seg + mp
    w1 = HPB * HD
    qm, km, vm, pm, am, _, _, _, _, _, _ = saved
    sds = jax.ShapeDtypeStruct
    shapes = [
        sds((mp, d), F32),
        sds((nb, keys, 3 * w1), BF),
        sds((seg, d), BF),
        sds((nb, 2, 4 * HD), F32),
    ]
    return pl.pallas_call(
        last_attention_kernel,
        out_shape=shapes,
        in_specs=[sm_spec(), vm_spec()] + [any_spec()] * 3 + [vm_spec()] * 9,
        out_specs=[vm_spec()] * len(shapes),
        scratch_shapes=[
            pltpu.VMEM((nb, d, d), BF),
            pltpu.VMEM((nb, keys, 4 * HD), BF),
            pltpu.VMEM((nb, keys, 4 * HD), BF),
            pltpu.VMEM((seg, d), F32),
            pltpu.SemaphoreType.DMA((nb,)),
            pltpu.SemaphoreType.DMA((2,)),
        ],
        compiler_params=params(),
        cost_estimate=pl.CostEstimate(
            flops=2 * seg * d * d * 4, bytes_accessed=30 * d * d, transcendentals=0
        ),
        name="last_attention",
    )(me, gr1m, k, v, w, qm, km, vm, pm, am, gq, gk, gv, gr1)


def turn(dst, t, a_ref, b_ref):
    seg = a_ref.shape[0]
    dst[t, :, 0:seg] = a_ref[...].astype(F32).T.astype(BF)
    dst[t, :, seg:] = b_ref[...].astype(F32).T.astype(BF)


def feed_grad_kernel(l_ref, lm_ref, r_ref, rm_ref, keep_ref, send_ref, lt):
    seg = l_ref.shape[0]

    @pl.when(pl.program_id(0) == 0)
    def _():
        turn(lt, 0, l_ref, lm_ref)

    for c, o in enumerate((keep_ref, send_ref)):
        o[0] = (nn(lt[0, :, 0:seg], r_ref[c]) + nn(lt[0, :, seg:], rm_ref[c])).astype(BF)


def feed_grad(left, left_m, right, right_m):
    seg, d = left.shape
    mp = left_m.shape[0]
    nb, _, cols = right.shape
    whole = lambda y: (0, 0)
    block = lambda y: (y, 0, 0)
    return pl.pallas_call(
        feed_grad_kernel,
        grid=(nb // 2,),
        out_shape=[jax.ShapeDtypeStruct((nb // 2, d, cols), BF)] * 2,
        in_specs=[
            pl.BlockSpec((seg, d), whole),
            pl.BlockSpec((mp, d), whole),
            pl.BlockSpec((2, seg, cols), block),
            pl.BlockSpec((2, mp, cols), block),
        ],
        out_specs=[pl.BlockSpec((1, d, cols), block)] * 2,
        scratch_shapes=[pltpu.VMEM((1, d, seg + mp), BF)],
        compiler_params=params(),
        cost_estimate=pl.CostEstimate(
            flops=2 * seg * d * cols * nb, bytes_accessed=16 * d * d, transcendentals=0
        ),
        name="feed_grad",
    )(left, left_m, right, right_m)


def attention_grad_kernel(
    tok_ref, m_ref, gqkv_ref, gr1_ref, gr1m_ref, a_ref, am_ref, small_ref, keep_ref, send_ref, lt
):
    seg, d = tok_ref.shape
    w1 = HPB * HD
    _, nd, n, _ = keep_ref.shape
    chunk = d // nd

    @pl.when(pl.program_id(0) == 0)
    def _():
        turn(lt, 0, tok_ref, m_ref)
        turn(lt, 1, gr1_ref, gr1m_ref)

    for c, o in enumerate((keep_ref, send_ref)):
        x = nn(lt[0], gqkv_ref[c])
        y = nn(lt[1, :, 0:seg], a_ref[c]) + nn(lt[1, :, seg:], am_ref[c])
        x = jnp.concatenate([x, y[:, 0:w1]], axis=1).astype(BF)
        for i in range(nd):
            o[0, i, 0:chunk, :] = x[i * chunk : (i + 1) * chunk]
            if n > chunk:
                o[0, i, chunk:n, :] = small_ref[c, i]


def attention_grad(tok, m, gqkv, gr1, gr1m, a, am, small):
    seg, d = tok.shape
    mp = m.shape[0]
    nb, keys, w3 = gqkv.shape
    _, nd, extra, _ = small.shape
    n = d // nd + extra
    whole = lambda y: (0, 0)
    block = lambda y: (y, 0, 0)
    block4 = lambda y: (y, 0, 0, 0)
    return pl.pallas_call(
        attention_grad_kernel,
        grid=(nb // 2,),
        out_shape=[jax.ShapeDtypeStruct((nb // 2, nd, n, d), BF)] * 2,
        in_specs=[
            pl.BlockSpec((seg, d), whole),
            pl.BlockSpec((mp, d), whole),
            pl.BlockSpec((2, keys, w3), block),
            pl.BlockSpec((seg, d), whole),
            pl.BlockSpec((mp, d), whole),
            pl.BlockSpec((2, seg, 4 * HD), block),
            pl.BlockSpec((2, mp, 4 * HD), block),
            pl.BlockSpec((2, nd, extra, d), block4),
        ],
        out_specs=[pl.BlockSpec((1, nd, n, d), block4)] * 2,
        scratch_shapes=[pltpu.VMEM((2, d, keys), BF)],
        compiler_params=params(),
        cost_estimate=pl.CostEstimate(
            flops=2 * seg * d * d * 4, bytes_accessed=16 * d * d, transcendentals=0
        ),
        name="attention_grad",
    )(tok, m, gqkv, gr1, gr1m, a, am, small)


def pack_kernel(q_ref, k_ref, v_ref, o_ref, u_ref, d_ref, out_ref):
    n, w1 = q_ref.shape
    d = u_ref.shape[1]
    for i, r in enumerate((q_ref, k_ref, v_ref)):
        out_ref[:, i * w1 : (i + 1) * w1] = r[...]
    out_ref[:, 3 * w1 : 4 * w1] = o_ref[...].astype(F32).T.astype(BF)
    out_ref[:, d : 2 * d] = u_ref[...]
    out_ref[:, 2 * d : 3 * d] = d_ref[...].astype(F32).T.astype(BF)


def pack(*weights):
    n = weights[0].shape[0]
    d = weights[4].shape[1]
    return pl.pallas_call(
        pack_kernel,
        out_shape=jax.ShapeDtypeStruct((n, 3 * d), BF),
        in_specs=[vm_spec()] * 6,
        out_specs=vm_spec(),
        name="pack",
    )(*weights)


def flip(a, axis, bit):
    return lax.ppermute(a, axis, [(i, i ^ bit) for i in range(lax.axis_size(axis))])


def shift(a, by):
    n = lax.axis_size("dp")
    return lax.ppermute(a, "dp", [(i, (i + by) % n) for i in range(n)])


def add(*xs):
    total = xs[0].astype(F32)
    for x in xs[1:]:
        total = total + x.astype(F32)
    return total.astype(BF)


def pick(a, i, axis):
    return lax.dynamic_index_in_dim(a, i, axis, keepdims=False)


def y_half(a):
    return add(a[0], flip(a[1], "mp", 2))


def x_half(a, axis):
    b = lax.axis_index("dp") % 2
    return add(pick(a, b, axis), flip(pick(a, 1 - b, axis), "dp", 1))


def z_quarter(a):
    z = lax.axis_index("dp") // 2
    part = [pick(a, (z + i) % 4, 0) for i in range(4)]
    return add(part[0], shift(part[1], 2), shift(part[3], -2), shift(part[2], 4))


def reduce_blocks(keep, send):
    _, _, n, c = keep.shape
    t = add(keep, flip(send, "mp", 1)).reshape(2, 4, 2, n, c)
    half = c // 2
    first = y_half(x_half(t[..., :half], 2))
    second = x_half(y_half(t[..., half:]), 1)
    s = z_quarter(jnp.stack([first, second], 1))
    return jnp.concatenate([s[0], s[1]], axis=1)


def relative(x):
    me = lax.axis_index("mp")
    v = x.reshape((2, 2) + x.shape[1:])
    v = jnp.where(me % 2 == 1, v[:, ::-1], v)
    v = jnp.where(me // 2 == 1, v[::-1], v)
    return v.reshape(x.shape)


def gather_small(x):
    nd = lax.axis_size("dp")
    nb = lax.axis_size("mp")
    if nd != 8:
        return lax.all_gather(x, ("mp", "dp"), axis=0).reshape(nb, nd, -1)
    k = x.shape[0]
    t = x.reshape(1, k)
    me = lax.axis_index("dp")
    b = me % 2
    z = me // 2
    o = flip(t, "mp", 1)
    c = lax.axis_index("mp") % 2
    t = jnp.where(c == 0, jnp.concatenate([t, o]), jnp.concatenate([o, t]))
    o = flip(t, "mp", 2)
    y = lax.axis_index("mp") // 2
    t = jnp.where(y == 0, jnp.concatenate([t, o]), jnp.concatenate([o, t]))
    o = flip(t, "dp", 1)
    t = jnp.where(b == 0, jnp.stack([t, o]), jnp.stack([o, t]))
    up, down, far = shift(t, -2), shift(t, 2), shift(t, 4)
    ring = jnp.stack([t, up, far, down, t, up, far])
    t = lax.dynamic_slice_in_dim(ring, (4 - z) % 4, 4, 0)
    return t.reshape(nd, nb, k).transpose(1, 0, 2)


def body(
    tokens, memory_init, query_weight, query_bias, key_weight, value_weight, value_bias, out_weight,
    out_bias, first_gain, first_shift, up_weight, up_bias, down_weight, down_bias, second_gain,
    second_shift, cotangent, group_segs, chain_group
):
    nd = lax.axis_size("dp")
    nb = lax.axis_size("mp")
    me = lax.axis_index("mp")
    me1 = me.astype(jnp.int32).reshape(1)
    segments = tokens.shape[1]
    d = tokens.shape[3]
    part = tokens.shape[2]
    seg = part * nb
    nmem = memory_init.shape[0] * nb
    pad = -(-nmem // 16) * 16
    both = ("mp", "dp")
    wl = pack(query_weight, key_weight, value_weight, out_weight, up_weight, down_weight)
    w = lax.all_gather(wl, both, axis=0).reshape(nb, d, 3 * d)
    vecs = (out_bias, first_gain, first_shift, down_bias, second_gain, second_shift)
    small = jnp.concatenate(
        (query_bias, value_bias, up_bias) + vecs + (memory_init.reshape(-1),)
    )
    n1 = query_bias.shape[0]
    n2 = up_bias.shape[0]
    sg = gather_small(small)
    qb = sg[:, :, 0:n1].reshape(nb, 1, -1).astype(F32)
    vb = sg[:, :, n1 : 2 * n1].reshape(nb, 1, -1).astype(F32)
    qkvb = jnp.concatenate([qb, jnp.zeros_like(qb), vb], axis=2)
    ub = sg[:, :, 2 * n1 : 2 * n1 + n2].reshape(nb, 1, -1).astype(F32)
    at = 2 * n1 + n2
    vec = sg[:, :, at : at + 6 * n1].reshape(nb, nd, 6, n1).transpose(2, 1, 0, 3).reshape(6, d)
    vec = jnp.pad(vec.astype(F32), ((0, 2), (0, 0)))
    ml = memory_init.shape[0]
    m0 = sg[:, :, at + 6 * n1 :].reshape(nb, nd, ml, -1).transpose(0, 2, 1, 3).reshape(nmem, d)
    m0 = jnp.pad(m0.astype(F32), ((0, pad - nmem), (0, 0)))
    tok = lax.all_to_all(tokens[0], "mp", 0, 1, tiled=True).reshape(seg, d)
    ct = lax.all_to_all(cotangent[0], "mp", 0, 1, tiled=True).reshape(seg, d)
    match = chain_group[:, None] == jnp.arange(group_segs.shape[0], dtype=jnp.int32)[None, :]
    count = jnp.sum(jnp.where(match, group_segs[None, :], 0))
    live = (me < count).astype(F32)
    live2 = jnp.full((8, 128), live, F32)
    q, k, v = qkv_call(me1, tok, w, qkvb)
    m = jnp.where(me == 0, m0, 0.0)
    own = m
    for s in range(segments - 1):
        (z,) = mem_forward(me1, m, k, v, w, qkvb, ub, vec, nmem, False)
        m = lax.ppermute(z, "mp", [(s, s + 1)])
        own = own + m
    (out, z1b, a, g, gf, gr2b, gr1, gq, gk, gv, base, sm, ubg) = token_call(
        me1, tok, ct, live2, own, q, k, v, w, qkvb, ub, vec, nmem
    )
    z2m, *saved = mem_forward(me1, own, k, v, w, qkvb, ub, vec, nmem, True)
    am, z1m, g_m = saved[4:7]
    send = base
    gin = jnp.zeros_like(base)
    for s in reversed(range(segments - 1)):
        recv = lax.ppermute(send, "mp", [(s + 1, s)])
        gin = gin + recv
        if s > 0:
            send = mem_backward(me1, recv, k, v, w, vec, base, saved)
    gr2m, gfm, gr1m, smm, ubgm = last_feed(me1, gin, w, vec, saved)
    up_g = feed_grad(z1b, z1m, gf, gfm)
    down_g = feed_grad(gr2b, gr2m, g, g_m)
    gm, gqkv, ig, qvb = last_attention(me1, gr1m, k, v, w, saved, gq, gk, gv, gr1)
    chains = nd * tokens.shape[0]
    norm = live * jnp.sum(z2m * z2m) / (nmem * d * chains)
    norms = jnp.where(jnp.arange(segments) == me, norm, 0.0)
    w1 = d // nb
    smt = (sm + smm)[0:6].reshape(6, nd, nb, n1).transpose(2, 1, 0, 3).reshape(nb, nd, 6 * n1)
    gmi = jnp.where(me == 0, gm[0:nmem], 0.0).reshape(nb, ml, nd, d // nd).transpose(0, 2, 1, 3)
    moved = relative(jnp.concatenate([smt, gmi.reshape(nb, nd, -1)], axis=2))
    qbg = qvb[:, 0, 0:w1].reshape(nb, nd, n1)
    vbg = qvb[:, 1, 0:w1].reshape(nb, nd, n1)
    ubt = (ubg + ubgm).reshape(nb, nd, n2)
    smalls = jnp.concatenate([qbg, vbg, ubt, moved], axis=2)
    count_small = smalls.shape[2]
    tuned = nd == 8
    if tuned:
        rows = jnp.stack(
            [smalls, jnp.zeros_like(smalls).at[:, :, 0:segments].set(norms)], axis=2
        )
        rows = jnp.pad(rows, ((0, 0), (0, 0), (0, 6), (0, 0))).astype(BF)
    else:
        rows = jnp.zeros((nb, 8, 8, d), BF)
    att_g = attention_grad(tok, own, gqkv, gr1, gr1m, a, am, rows)
    chunk = d // nd
    if tuned:
        wup = reduce_blocks(*[x.reshape(2, nd, chunk, d) for x in up_g]).astype(F32)
        wdn = reduce_blocks(*[x.reshape(2, nd, chunk, d) for x in down_g]).astype(F32)
        watt = reduce_blocks(*att_g).astype(F32)
        sr = watt[chunk]
        norms = watt[chunk + 1, 0:segments]
        watt = watt[0:chunk]
    else:

        def scatter(keep, send):
            x = relative(jnp.stack([keep, send], axis=1).reshape(nb, d, d))
            x = x.reshape(nb * nd, chunk, d)
            return lax.psum_scatter(x, both, scatter_dimension=0, tiled=False).astype(F32)

        att_g = [x[:, :, 0 : d // 8] for x in att_g]
        wup, wdn, watt = scatter(*up_g), scatter(*down_g), scatter(*att_g)
        sr = jnp.concatenate(
            [relative(smalls), jnp.broadcast_to(norms, (nb, nd, segments))], axis=2
        ).reshape(nb * nd, -1)
        sr = lax.psum_scatter(sr, both, scatter_dimension=0, tiled=False)
        norms = sr[count_small:]
    vg = sr[at : at + 6 * n1].reshape(6, n1)
    layer_out = lax.all_to_all(out.reshape(nb, part, d), "mp", 0, 0, tiled=True)
    input_grad = lax.all_to_all(ig.reshape(nb, part, d), "mp", 0, 0, tiled=True)
    return (
        layer_out[None],
        input_grad[None],
        sr[at + 6 * n1 : count_small].reshape(ml, d // nd),
        watt[:, 0:w1],
        sr[0:n1],
        watt[:, w1 : 2 * w1],
        watt[:, 2 * w1 : 3 * w1],
        sr[n1 : 2 * n1],
        watt[:, 3 * w1 : d].T,
        vg[0],
        vg[1],
        vg[2],
        wup,
        sr[2 * n1 : at],
        wdn.T,
        vg[3],
        vg[4],
        vg[5],
        norms,
    )


def solution(mesh):
    rows = P("dp", None, "mp", None)
    md, dm = P(("mp", "dp")), P(("dp", "mp"))
    win, wout = P("dp", "mp"), P("mp", "dp")
    in_specs = (
        rows, wout, win, md, win, win, md, wout, dm, dm, dm, win, md, wout, dm, dm, dm, rows, P(),
        P("dp"),
    )
    out_specs = (
        rows, rows, wout, win, md, win, win, md, wout, dm, dm, dm, win, md, wout, dm, dm, dm, P(),
    )
    return jax.shard_map(body, mesh=mesh, in_specs=in_specs, out_specs=out_specs, check_vma=False)
```

```python
import functools

import jax
import jax.numpy as jnp
from jax import lax
from jax.experimental import pallas as pl
from jax.experimental.pallas import tpu as pltpu
from jax.sharding import PartitionSpec as P

HD = 64
HPB = 3
BF = jnp.bfloat16
F32 = jnp.float32
MIB = 1024 * 1024
NEG = -1e30


def nn(a, b):
    return lax.dot_general(a, b, (((1,), (0,)), ((), ())), preferred_element_type=F32)


def nt(a, b):
    return lax.dot_general(a, b, (((1,), (1,)), ((), ())), preferred_element_type=F32)


def norm_stats(r):
    mean = jnp.mean(r, axis=-1, keepdims=True)
    c = r - mean
    inv = lax.rsqrt(jnp.mean(c * c, axis=-1, keepdims=True) + 1e-05)
    return c * inv, inv


def norm_back(g, xh, inv):
    return inv * (
        g - jnp.mean(g, axis=-1, keepdims=True) - xh * jnp.mean(g * xh, axis=-1, keepdims=True)
    )


def gelu_both(f):
    cdf = 0.5 + 0.5 * lax.erf(f * (0.5**0.5))
    pdf = jnp.exp(-0.5 * f * f) * ((2.0 * jnp.pi) ** -0.5)
    return f * cdf, cdf + f * pdf


def rows_mask(shape, count):
    return lax.broadcasted_iota(jnp.int32, shape, 0) < count


def any_spec():
    return pl.BlockSpec(memory_space=pl.ANY)


def vm_spec():
    return pl.BlockSpec(memory_space=pltpu.VMEM)


def params(mib):
    return pltpu.CompilerParams(vmem_limit_bytes=mib * MIB)


def sm_spec():
    return pl.BlockSpec(memory_space=pltpu.SMEM)


def after(kernel, n_in, n_dep):
    def run(*refs):
        kernel(*refs[:n_in], *refs[n_in + n_dep :])

    return run


def split_qkv(acc):
    w1 = HPB * HD
    zero = jnp.zeros((acc.shape[0], HD), BF)
    q = jnp.concatenate([(acc[:, 0:w1].astype(BF) * 0.125).astype(BF), zero], axis=1)
    k = jnp.concatenate([acc[:, w1 : 2 * w1].astype(BF), zero], axis=1)
    v = jnp.concatenate([acc[:, 2 * w1 : 3 * w1].astype(BF), zero], axis=1)
    return q, k, v


def head_cols(shape, i):
    c = lax.broadcasted_iota(jnp.int32, shape, len(shape) - 1)
    return (c >= i * HD) & (c < (i + 1) * HD)


def spread(x):
    return jnp.concatenate(
        [jnp.where(head_cols(x.shape, i), x, jnp.zeros_like(x)) for i in range(HPB)], axis=0
    )


def gather_heads(x):
    n = x.shape[0] // HPB
    out = jnp.zeros((n, x.shape[1]), x.dtype)
    for i in range(HPB):
        out = jnp.where(head_cols(out.shape, i), x[i * n : (i + 1) * n], out)
    return out


def out_cols(a):
    return jnp.concatenate([jnp.zeros((a.shape[0], HD), a.dtype), a[:, 0 : HPB * HD]], axis=1)


def qkv_kernel(me_ref, tok_ref, w_ref, qkvb_ref, q_ref, k_ref, v_ref):
    nb, d, _ = w_ref.shape
    me = me_ref[0]
    for j in range(nb):
        acc = nn(tok_ref[...], w_ref[j ^ me, :, 0 : 3 * HPB * HD]) + qkvb_ref[j ^ me]
        q, k, v = split_qkv(acc)
        q_ref[j] = q
        k_ref[j] = k
        v_ref[j] = v


def qkv_call(me, tok, w, qkvb):
    nb, d, _ = w.shape
    s = tok.shape[0]
    return pl.pallas_call(
        qkv_kernel,
        out_shape=[jax.ShapeDtypeStruct((nb, s, 4 * HD), BF)] * 3,
        in_specs=[sm_spec(), vm_spec(), vm_spec(), vm_spec()],
        out_specs=[vm_spec()] * 3,
        compiler_params=params(20),
        cost_estimate=pl.CostEstimate(
            flops=2 * s * d * 3 * d, bytes_accessed=8 * d * d, transcendentals=0
        ),
        name="qkv",
    )(me, tok, w, qkvb)


def mem_forward_kernel(
    nmem, save, me_ref, m_ref, k_hbm, v_hbm, w_ref, qkvb_ref, ub_ref, vec_ref, *rest
):
    if save:
        (
            z2_ref, qm_ref, km_ref, vm_ref, pm_ref, am_ref, z1b_ref, g_ref, gp_ref, xh1_ref,
            xh2_ref, inv_ref,
        ) = rest[:12]
        rest = rest[12:]
    else:
        z2_ref = rest[0]
        rest = rest[1:]
    kk, vv, sc, sem2 = rest
    nb, d, _ = w_ref.shape
    seg = k_hbm.shape[1]
    mp = m_ref.shape[0]
    keys = seg + mp
    w1 = HPB * HD
    me = me_ref[0]
    kc = pltpu.make_async_copy(k_hbm, kk.at[:, 0:seg, :], sem2.at[0])
    vc = pltpu.make_async_copy(v_hbm, vv.at[:, 0:seg, :], sem2.at[1])
    kc.start()
    vc.start()
    mem = m_ref[...]
    mb = mem.astype(BF)
    qs = []
    for j in range(nb):
        acc = nn(mb, w_ref[j ^ me, :, 0 : 3 * w1]) + qkvb_ref[j ^ me]
        q, k, v = split_qkv(acc)
        qs.append(q)
        kk[j, seg:keys, :] = k
        vv[j, seg:keys, :] = v
        if save:
            qm_ref[j] = q
            km_ref[j] = k
            vm_ref[j] = v
    kc.wait()
    vc.wait()
    n = HPB * mp
    for j in range(nb):
        sc[j * n : (j + 1) * n, :] = nt(spread(qs[j]), kk[j])
    keep = lax.broadcasted_iota(jnp.int32, (n, keys), 1) < seg + nmem
    heads = []
    for j in range(nb):
        s = jnp.where(keep, sc[j * n : (j + 1) * n, :], NEG)
        e = jnp.exp(s - jnp.max(s, axis=-1, keepdims=True))
        p = (e / jnp.sum(e, axis=-1, keepdims=True)).astype(BF)
        if save:
            pm_ref[j] = p
        heads.append(p)
    out = jnp.zeros((mp, d), F32)
    for j in range(nb):
        a = gather_heads(nn(heads[j], vv[j])).astype(BF)
        if save:
            am_ref[j] = a
        out += nt(out_cols(a), w_ref[j ^ me, :, d - 4 * HD : d])
    xh1, inv1 = norm_stats(mem + out + vec_ref[0:1])
    z1 = xh1 * vec_ref[1:2] + vec_ref[2:3]
    z1b = z1.astype(BF)
    y = jnp.zeros((mp, d), F32)
    for j in range(nb):
        f = nn(z1b, w_ref[j ^ me, :, d : 2 * d]) + ub_ref[j ^ me]
        g, gp = gelu_both(f)
        g = g.astype(BF)
        if save:
            g_ref[j] = g
            gp_ref[j] = gp
        y += nt(g, w_ref[j ^ me, :, 2 * d : 3 * d])
    xh2, inv2 = norm_stats(z1 + y + vec_ref[3:4])
    z2 = xh2 * vec_ref[4:5] + vec_ref[5:6]
    z2_ref[...] = jnp.where(rows_mask((mp, d), nmem), z2, 0.0)
    if save:
        z1b_ref[...] = z1b
        xh1_ref[...] = xh1
        xh2_ref[...] = xh2
        inv_ref[:, 0:128] = jnp.broadcast_to(inv1, (mp, 128))
        inv_ref[:, 128:256] = jnp.broadcast_to(inv2, (mp, 128))


def mem_forward(me, m, k, v, w, qkvb, ub, vec, nmem, save, deps=()):
    nb, d, _ = w.shape
    seg = k.shape[1]
    mp = m.shape[0]
    keys = seg + mp
    sds = jax.ShapeDtypeStruct
    shapes = [sds((mp, d), F32)]
    if save:
        shapes += [sds((nb, mp, 4 * HD), BF)] * 3
        shapes += [
            sds((nb, HPB * mp, keys), BF),
            sds((nb, mp, 4 * HD), BF),
            sds((mp, d), BF),
            sds((nb, mp, d), BF),
            sds((nb, mp, d), F32),
            sds((mp, d), F32),
            sds((mp, d), F32),
            sds((mp, 256), F32),
        ]
    return pl.pallas_call(
        after(functools.partial(mem_forward_kernel, nmem, save), 8, len(deps)),
        out_shape=shapes,
        in_specs=[sm_spec(), vm_spec()]
        + [any_spec()] * 2
        + [vm_spec()] * 4
        + [any_spec()] * len(deps),
        out_specs=[vm_spec()] * len(shapes),
        scratch_shapes=[
            pltpu.VMEM((nb, keys, 4 * HD), BF),
            pltpu.VMEM((nb, keys, 4 * HD), BF),
            pltpu.VMEM((nb * HPB * mp, keys), F32),
            pltpu.SemaphoreType.DMA((2,)),
        ],
        compiler_params=params(24),
        cost_estimate=pl.CostEstimate(
            flops=2 * mp * d * d * 12, bytes_accessed=24 * d * d, transcendentals=0
        ),
        name="mem_forward_save" if save else "mem_forward",
    )(me, m, k, v, w, qkvb, ub, vec, *deps)


def colsum(x):
    return jnp.sum(x, axis=0, keepdims=True)


CH = 64


def token_kernel(
    nmem,
    me_ref,
    tok_ref,
    ct_ref,
    live_ref,
    m_ref,
    q_hbm,
    k_hbm,
    v_hbm,
    w_ref,
    qkvb_ref,
    ub_ref,
    vec_ref,
    out_ref,
    z1b_ref,
    a_ref,
    g_ref,
    gf_ref,
    gr2b_ref,
    gr1_ref,
    gq_ref,
    gk_ref,
    gv_ref,
    base_ref,
    small_ref,
    ubg_ref,
    qq,
    kk,
    vv,
    probs,
    big,
    one,
    xh1,
    g1b,
    inv,
    gp,
    sem2,
):
    nb, d, _ = w_ref.shape
    seg = tok_ref.shape[0]
    mp = m_ref.shape[0]
    keys = seg + mp
    w1 = HPB * HD
    steps = seg // CH
    me = me_ref[0]
    loads = [
        pltpu.make_async_copy(q_hbm, qq, sem2.at[0]),
        pltpu.make_async_copy(k_hbm, kk.at[:, 0:seg, :], sem2.at[1]),
        pltpu.make_async_copy(v_hbm, vv.at[:, 0:seg, :], sem2.at[2]),
    ]
    for c in loads:
        c.start()
    mb = m_ref[...].astype(BF)
    for j in range(nb):
        _, k, v = split_qkv(nn(mb, w_ref[j ^ me, :, 0 : 3 * w1]) + qkvb_ref[j ^ me])
        kk[j, seg:keys, :] = k
        vv[j, seg:keys, :] = v
    for c in loads:
        c.wait()
    one[...] = jnp.zeros_like(one)
    tail = seg + (nmem // 8) * 8

    def attend(j, _):
        vt = vv[j].astype(F32).T.astype(BF)
        parts = []
        for i in range(HPB):
            cols = slice(i * HD, (i + 1) * HD)
            big[0:keys, 0:seg] = nt(kk[j, :, cols], qq[j, :, cols])
            big[tail:keys, 0:seg] = jnp.where(
                rows_mask((keys - tail, seg), seg + nmem - tail), big[tail:keys, 0:seg], NEG
            )
            for c in range(seg // 128):
                cols = slice(c * 128, (c + 1) * 128)
                s = big[0:keys, cols]
                e = jnp.exp(s - jnp.max(s, axis=0, keepdims=True))
                p = e * (1.0 / jnp.sum(e, axis=0, keepdims=True))
                probs[j * HPB + i, :, cols] = p.astype(BF)
            parts.append(nn(vt[i * HD : (i + 1) * HD], probs[j * HPB + i]))
        parts.append(jnp.zeros((HD, seg), F32))
        a = jnp.concatenate(parts, axis=0).T.astype(BF)
        a_ref[j] = a
        one[...] += nt(out_cols(a), w_ref[j ^ me, :, d - 4 * HD : d])
        return 0

    lax.fori_loop(0, nb, attend, 0)

    def first(c, _):
        rows = pl.ds(pl.multiple_of(c * CH, CH), CH)
        r = tok_ref[rows, :].astype(F32) + one[rows, :] + vec_ref[0:1]
        x, v = norm_stats(r)
        xh1[rows, :] = x
        inv[rows, 0:128] = jnp.broadcast_to(v, (CH, 128))
        z1 = x * vec_ref[1:2] + vec_ref[2:3]
        z1b_ref[rows, :] = z1.astype(BF)
        one[rows, :] = z1 + vec_ref[3:4]
        return 0

    lax.fori_loop(0, steps, first, 0)

    def feed(j, _):
        big[0:seg, 0:d] = nn(z1b_ref[...], w_ref[j ^ me, :, d : 2 * d])

        def act(c, _):
            rows = pl.ds(pl.multiple_of(c * 32, 32), 32)
            g, p = gelu_both(big[rows, 0:d] + ub_ref[j ^ me])
            g_ref[j, rows, :] = g.astype(BF)
            gp[j, rows, :] = p.astype(BF)
            return 0

        lax.fori_loop(0, seg // 32, act, 0)
        one[...] += nt(g_ref[j], w_ref[j ^ me, :, 2 * d : 3 * d])
        return 0

    lax.fori_loop(0, nb, feed, 0)
    zero = jnp.zeros((1, d), F32)

    def second(c, carry):
        sg, ss, sb = carry
        rows = pl.ds(pl.multiple_of(c * CH, CH), CH)
        x, v = norm_stats(one[rows, :])
        out_ref[rows, :] = ((x * vec_ref[4:5] + vec_ref[5:6]) * live_ref[0:1, 0:1]).astype(BF)
        gz = ct_ref[rows, :].astype(F32) * live_ref[0:1, 0:1]
        gr = norm_back(gz * vec_ref[4:5], x, v)
        one[rows, :] = gr
        gr2b_ref[rows, :] = gr.astype(BF)
        return (sg + colsum(gz * x), ss + colsum(gz), sb + colsum(gr))

    sg, ss, sb = lax.fori_loop(0, steps, second, (zero, zero, zero))
    small_ref[3:4] = sb
    small_ref[4:5] = sg
    small_ref[5:6] = ss

    def feed_back(j, _):
        big[0:seg, 0:d] = nn(gr2b_ref[...], w_ref[j ^ me, :, 2 * d : 3 * d])

        def act(c, total):
            rows = pl.ds(pl.multiple_of(c * CH, CH), CH)
            gf = (big[rows, 0:d] * gp[j, rows, :].astype(F32)).astype(BF)
            gf_ref[j, rows, :] = gf
            return total + colsum(gf.astype(F32))

        ubg_ref[j] = lax.fori_loop(0, steps, act, zero)
        one[...] += nt(gf_ref[j], w_ref[j ^ me, :, d : 2 * d])
        return 0

    lax.fori_loop(0, nb, feed_back, 0)

    def first_back(c, carry):
        sg, ss, sb = carry
        rows = pl.ds(pl.multiple_of(c * CH, CH), CH)
        gz = one[rows, :]
        x = xh1[rows, :]
        gr = norm_back(gz * vec_ref[1:2], x, inv[rows, 0:1])
        gr1_ref[rows, :] = gr
        g1b[rows, :] = gr.astype(BF)
        return (sg + colsum(gz * x), ss + colsum(gz), sb + colsum(gr))

    sg, ss, sb = lax.fori_loop(0, steps, first_back, (zero, zero, zero))
    small_ref[0:1] = sb
    small_ref[1:2] = sg
    small_ref[2:3] = ss
    small_ref[6:8] = jnp.zeros((2, d), F32)

    def attend_back(j, base):
        ga = nn(g1b[...], w_ref[j ^ me, :, d - 4 * HD : d])[:, HD:]
        gab = ga.astype(BF)
        delta = (gab.astype(F32) * a_ref[j, :, 0:w1].astype(F32)).T
        kt = kk[j].astype(F32).T.astype(BF)
        gqs = []
        gks = []
        gvs = []
        for i in range(HPB):
            cols = slice(i * HD, (i + 1) * HD)
            g = gab[:, cols]
            p = probs[j * HPB + i]
            dl = jnp.sum(delta[cols], axis=0, keepdims=True)
            gvs.append(nn(p, g))
            gs = (p.astype(F32) * (nt(vv[j, :, cols], g) - dl)).astype(BF)
            gks.append(nn(gs, qq[j, :, cols]))
            gqs.append(nn(kt[cols], gs))
        zq = jnp.zeros((HD, seg), F32)
        zk = jnp.zeros((keys, HD), F32)
        gq_ref[j] = (jnp.concatenate(gqs + [zq], axis=0).T * 0.125).astype(BF)
        gk = jnp.concatenate(gks + [zk], axis=1)
        gv = jnp.concatenate(gvs + [zk], axis=1)
        gk_ref[j] = gk.astype(BF)
        gv_ref[j] = gv.astype(BF)
        gm = jnp.concatenate(
            [jnp.zeros((mp, w1), F32), gk[seg:keys, 0:w1], gv[seg:keys, 0:w1]], axis=1
        ).astype(BF)
        return base + nt(gm, w_ref[j ^ me, :, 0 : 3 * w1])

    base_ref[...] = lax.fori_loop(0, nb, attend_back, jnp.zeros((mp, d), F32))


def token_call(me, tok, ct, live, m, q, k, v, w, qkvb, ub, vec, nmem):
    nb, d, _ = w.shape
    seg = tok.shape[0]
    mp = m.shape[0]
    keys = seg + mp
    sds = jax.ShapeDtypeStruct
    shapes = [
        sds((seg, d), BF),
        sds((seg, d), BF),
        sds((nb, seg, 4 * HD), BF),
        sds((nb, seg, d), BF),
        sds((nb, seg, d), BF),
        sds((seg, d), BF),
        sds((seg, d), F32),
        sds((nb, seg, 4 * HD), BF),
        sds((nb, keys, 4 * HD), BF),
        sds((nb, keys, 4 * HD), BF),
        sds((mp, d), F32),
        sds((8, d), F32),
        sds((nb, 1, d), F32),
    ]
    return pl.pallas_call(
        functools.partial(token_kernel, nmem),
        out_shape=shapes,
        in_specs=[sm_spec()] + [vm_spec()] * 4 + [any_spec()] * 3 + [vm_spec()] * 4,
        out_specs=[vm_spec()] * len(shapes),
        scratch_shapes=[
            pltpu.VMEM((nb, seg, 4 * HD), BF),
            pltpu.VMEM((nb, keys, 4 * HD), BF),
            pltpu.VMEM((nb, keys, 4 * HD), BF),
            pltpu.VMEM((nb * HPB, keys, seg), BF),
            pltpu.VMEM((keys, d), F32),
            pltpu.VMEM((seg, d), F32),
            pltpu.VMEM((seg, d), F32),
            pltpu.VMEM((seg, d), BF),
            pltpu.VMEM((seg, 128), F32),
            pltpu.VMEM((nb, seg, d), BF),
            pltpu.SemaphoreType.DMA((3,)),
        ],
        compiler_params=params(45),
        cost_estimate=pl.CostEstimate(
            flops=5 * seg * d * d * 12, bytes_accessed=60 * d * d, transcendentals=0
        ),
        name="token_rows",
    )(me, tok, ct, live, m, q, k, v, w, qkvb, ub, vec)


def back_feed(w_ref, me, nb, d, gz, vec_ref, gp_ref, xh1, xh2, inv_ref, gf_ref=None, ubg_ref=None):
    gr2 = norm_back(gz * vec_ref[4:5], xh2, inv_ref[:, 128:129])
    gr2b = gr2.astype(BF)
    acc = gr2
    for j in range(nb):
        gf = (nn(gr2b, w_ref[j ^ me, :, 2 * d : 3 * d]) * gp_ref[j]).astype(BF)
        if gf_ref is not None:
            gf_ref[j] = gf
            ubg_ref[j] = colsum(gf.astype(F32))
        acc += nt(gf, w_ref[j ^ me, :, d : 2 * d])
    return gr2, acc, norm_back(acc * vec_ref[1:2], xh1, inv_ref[:, 0:1])


def back_scores(j, gab, am_ref, pm_ref, vv, delta_rows):
    n = HPB * delta_rows
    gs3 = spread(gab)
    a3 = jnp.concatenate([am_ref[j]] * HPB, axis=0)
    dl = jnp.sum(gs3.astype(F32) * a3.astype(F32), axis=1, keepdims=True)
    p = pm_ref[j].astype(F32)
    return gs3, p, (p * (nt(gs3, vv[j]) - dl)).astype(BF)


def mem_backward_kernel(
    nmem, me_ref, g_ref, k_hbm, v_hbm, w_ref, vec_ref, base_ref, qm_ref, km_ref, vm_ref, pm_ref,
    am_ref, gp_ref, xh1_ref, xh2_ref, inv_ref, gm_ref, kk, vv, sem2
):
    nb, d, _ = w_ref.shape
    seg = k_hbm.shape[1]
    mp = g_ref.shape[0]
    keys = seg + mp
    w1 = HPB * HD
    me = me_ref[0]
    kc = pltpu.make_async_copy(k_hbm, kk.at[:, 0:seg, :], sem2.at[0])
    vc = pltpu.make_async_copy(v_hbm, vv.at[:, 0:seg, :], sem2.at[1])
    kc.start()
    vc.start()
    kk[:, seg:keys, :] = km_ref[...]
    vv[:, seg:keys, :] = vm_ref[...]
    _, _, gr1 = back_feed(
        w_ref, me, nb, d, g_ref[...], vec_ref, gp_ref, xh1_ref[...], xh2_ref[...], inv_ref
    )
    gr1b = gr1.astype(BF)
    kc.wait()
    vc.wait()
    gabs = []
    for j in range(nb):
        ga = nn(gr1b, w_ref[j ^ me, :, d - 4 * HD : d]).astype(BF)
        gabs.append(jnp.concatenate([ga[:, HD:], jnp.zeros((mp, HD), BF)], axis=1))
    scores = [back_scores(j, gabs[j], am_ref, pm_ref, vv, mp) for j in range(nb)]
    out = gr1 + base_ref[...]
    for j in range(nb):
        gs3, p, gs = scores[j]
        gq = gather_heads(nn(gs, kk[j])) * 0.125
        gk = nn(gs[:, seg:keys].astype(F32).T.astype(BF), spread(qm_ref[j]))
        gv = nn(p[:, seg:keys].T.astype(BF), gs3)
        gm = jnp.concatenate([gq[:, 0:w1], gk[:, 0:w1], gv[:, 0:w1]], axis=1).astype(BF)
        out += nt(gm, w_ref[j ^ me, :, 0 : 3 * w1])
    gm_ref[...] = out


def mem_backward(me, g, k, v, w, vec, base, saved):
    nb, d, _ = w.shape
    seg = k.shape[1]
    mp = g.shape[0]
    keys = seg + mp
    qm, km, vm, pm, am, _, _, gp, xh1, xh2, inv = saved
    args = (me, g, k, v, w, vec, base, qm, km, vm, pm, am, gp, xh1, xh2, inv)
    return pl.pallas_call(
        functools.partial(mem_backward_kernel, 0),
        out_shape=jax.ShapeDtypeStruct((mp, d), F32),
        in_specs=[sm_spec(), vm_spec()] + [any_spec()] * 2 + [vm_spec()] * 12,
        out_specs=vm_spec(),
        scratch_shapes=[
            pltpu.VMEM((nb, keys, 4 * HD), BF),
            pltpu.VMEM((nb, keys, 4 * HD), BF),
            pltpu.SemaphoreType.DMA((2,)),
        ],
        compiler_params=params(24),
        cost_estimate=pl.CostEstimate(
            flops=2 * mp * d * d * 12, bytes_accessed=24 * d * d, transcendentals=0
        ),
        name="mem_backward",
    )(*args)


def last_feed_kernel(
    me_ref, g_ref, w_ref, vec_ref, gp_ref, xh1_ref, xh2_ref, inv_ref, gr2b_ref, gf_ref, gr1_ref,
    small_ref, ubg_ref
):
    nb, d, _ = w_ref.shape
    me = me_ref[0]
    gz = g_ref[...]
    xh1 = xh1_ref[...]
    xh2 = xh2_ref[...]
    gr2, gz1, gr1 = back_feed(
        w_ref, me, nb, d, gz, vec_ref, gp_ref, xh1, xh2, inv_ref, gf_ref, ubg_ref
    )
    gr2b_ref[...] = gr2.astype(BF)
    gr1_ref[...] = gr1
    small_ref[0:1] = colsum(gr1)
    small_ref[1:2] = colsum(gz1 * xh1)
    small_ref[2:3] = colsum(gz1)
    small_ref[3:4] = colsum(gr2)
    small_ref[4:5] = colsum(gz * xh2)
    small_ref[5:6] = colsum(gz)
    small_ref[6:8] = jnp.zeros((2, d), F32)


def last_feed(me, g, w, vec, saved, deps=()):
    nb, d, _ = w.shape
    mp = g.shape[0]
    _, _, _, _, _, _, _, gp, xh1, xh2, inv = saved
    sds = jax.ShapeDtypeStruct
    shapes = [
        sds((mp, d), BF),
        sds((nb, mp, d), BF),
        sds((mp, d), F32),
        sds((8, d), F32),
        sds((nb, 1, d), F32),
    ]
    return pl.pallas_call(
        after(last_feed_kernel, 8, len(deps)),
        out_shape=shapes,
        in_specs=[sm_spec()] + [vm_spec()] * 7 + [any_spec()] * len(deps),
        out_specs=[vm_spec()] * len(shapes),
        compiler_params=params(20),
        cost_estimate=pl.CostEstimate(
            flops=2 * mp * d * d * 8, bytes_accessed=16 * d * d, transcendentals=0
        ),
        name="last_feed",
    )(me, g, w, vec, gp, xh1, xh2, inv, *deps)


def last_attention_kernel(
    nmem, me_ref, gr1m_ref, k_hbm, v_hbm, w_ref, qm_ref, km_ref, vm_ref, pm_ref, am_ref, gq_ref, gk_ref,
    gv_ref, gr1_ref, gm_ref, gqkv_ref, ig_ref, qvb_ref, kk, vv, one, sem2
):
    nb, d, _ = w_ref.shape
    seg = k_hbm.shape[1]
    mp = gr1m_ref.shape[0]
    keys = seg + mp
    w1 = HPB * HD
    me = me_ref[0]
    kc = pltpu.make_async_copy(k_hbm, kk.at[:, 0:seg, :], sem2.at[0])
    vc = pltpu.make_async_copy(v_hbm, vv.at[:, 0:seg, :], sem2.at[1])
    kc.start()
    vc.start()
    kk[:, seg:keys, :] = km_ref[...]
    vv[:, seg:keys, :] = vm_ref[...]
    gr1 = gr1m_ref[...]
    gr1b = gr1.astype(BF)
    kc.wait()
    vc.wait()
    gabs = []
    for j in range(nb):
        ga = nn(gr1b, w_ref[j ^ me, :, d - 4 * HD : d]).astype(BF)
        gabs.append(jnp.concatenate([ga[:, HD:], jnp.zeros((mp, HD), BF)], axis=1))
    scores = [back_scores(j, gabs[j], am_ref, pm_ref, vv, mp) for j in range(nb)]
    out = gr1
    for j in range(nb):
        gs3, p, gs = scores[j]
        gq = (gather_heads(nn(gs, kk[j])) * 0.125).astype(BF)
        gk = (gk_ref[j] + nn(gs.astype(F32).T.astype(BF), spread(qm_ref[j]))).astype(BF)
        gv = (gv_ref[j] + nn(p.T.astype(BF), gs3)).astype(BF)
        gqt = gq_ref[j]
        gqkv_ref[j, 0:seg, 0:w1] = gqt[:, 0:w1]
        gqkv_ref[j, seg:keys, 0:w1] = gq[:, 0:w1]
        gqkv_ref[j, :, w1 : 2 * w1] = gk[:, 0:w1]
        gqkv_ref[j, :, 2 * w1 : 3 * w1] = gv[:, 0:w1]
        qvb_ref[j, 0:1, :] = colsum(gqt.astype(F32)) + colsum(gq.astype(F32))
        qvb_ref[j, 1:2, :] = colsum(gv.astype(F32))
        x = nt(gqkv_ref[j, 0:seg, :], w_ref[j ^ me, :, 0 : 3 * w1])
        if j == 0:
            one[...] = gr1_ref[...] + x
        else:
            one[...] += x
        out += nt(gqkv_ref[j, seg:keys, :], w_ref[j ^ me, :, 0 : 3 * w1])
    gm_ref[...] = jnp.zeros_like(gm_ref)
    for i in range(nb):
        gm_ref[i, 0 : nmem // nb, :] = out[i * nmem // nb : (i + 1) * nmem // nb]
    ig_ref[...] = one[...].astype(BF)


def last_attention(me, gr1m, k, v, w, saved, gq, gk, gv, gr1, nmem, deps=()):
    nb, d, _ = w.shape
    seg = k.shape[1]
    mp = gr1m.shape[0]
    keys = seg + mp
    w1 = HPB * HD
    qm, km, vm, pm, am, _, _, _, _, _, _ = saved
    sds = jax.ShapeDtypeStruct
    shapes = [
        sds((nb, 8, d), F32),
        sds((nb, keys, 3 * w1), BF),
        sds((seg, d), BF),
        sds((nb, 2, 4 * HD), F32),
    ]
    return pl.pallas_call(
        after(functools.partial(last_attention_kernel, nmem), 14, len(deps)),
        out_shape=shapes,
        in_specs=[sm_spec(), vm_spec()]
        + [any_spec()] * 2
        + [vm_spec()] * 10
        + [any_spec()] * len(deps),
        out_specs=[vm_spec()] * len(shapes),
        scratch_shapes=[
            pltpu.VMEM((nb, keys, 4 * HD), BF),
            pltpu.VMEM((nb, keys, 4 * HD), BF),
            pltpu.VMEM((seg, d), F32),
            pltpu.SemaphoreType.DMA((2,)),
        ],
        compiler_params=params(28),
        cost_estimate=pl.CostEstimate(
            flops=2 * seg * d * d * 4, bytes_accessed=30 * d * d, transcendentals=0
        ),
        name="last_attention",
    )(me, gr1m, k, v, w, qm, km, vm, pm, am, gq, gk, gv, gr1, *deps)


def turn(dst, t, a_ref, b_ref):
    seg = a_ref.shape[0]
    dst[t, :, 0:seg] = a_ref[...].astype(F32).T.astype(BF)
    dst[t, :, seg:] = b_ref[...].astype(F32).T.astype(BF)


def feed_grad_kernel(l_ref, lm_ref, r_ref, rm_ref, keep_ref, send_ref, lt):
    seg = l_ref.shape[0]

    @pl.when(pl.program_id(0) == 0)
    def _():
        turn(lt, 0, l_ref, lm_ref)

    for c, o in enumerate((keep_ref, send_ref)):
        o[0] = (nn(lt[0, :, 0:seg], r_ref[c]) + nn(lt[0, :, seg:], rm_ref[c])).astype(BF)


def feed_grad(left, left_m, right, right_m, deps=()):
    seg, d = left.shape
    mp = left_m.shape[0]
    nb, _, cols = right.shape
    whole = lambda y: (0, 0)
    block = lambda y: (y, 0, 0)
    return pl.pallas_call(
        after(feed_grad_kernel, 4, len(deps)),
        grid=(nb // 2,),
        out_shape=[jax.ShapeDtypeStruct((nb // 2, d, cols), BF)] * 2,
        in_specs=[
            pl.BlockSpec((seg, d), whole),
            pl.BlockSpec((mp, d), whole),
            pl.BlockSpec((2, seg, cols), block),
            pl.BlockSpec((2, mp, cols), block),
        ]
        + [any_spec()] * len(deps),
        out_specs=[pl.BlockSpec((1, d, cols), block)] * 2,
        scratch_shapes=[pltpu.VMEM((1, d, seg + mp), BF)],
        compiler_params=params(20),
        cost_estimate=pl.CostEstimate(
            flops=2 * seg * d * cols * nb, bytes_accessed=16 * d * d, transcendentals=0
        ),
        name="feed_grad",
    )(left, left_m, right, right_m, *deps)


def attention_grad_kernel(
    nmem, chains, me_ref, tok_ref, m_ref, gqkv_ref, gr1_ref, gr1m_ref, a_ref, am_ref, sm_ref, smm_ref,
    ubg_ref, ubgm_ref, qvb_ref, gm_ref, z2m_ref, live_ref, keep_ref, send_ref, lt
):
    seg, d = tok_ref.shape
    w1 = HPB * HD
    _, nd, n, _ = keep_ref.shape
    chunk = d // nd
    me = me_ref[0]
    y = pl.program_id(0)

    @pl.when(y == 0)
    def _():
        turn(lt, 0, tok_ref, m_ref)
        turn(lt, 1, gr1_ref, gr1m_ref)

    vecs = sm_ref[...] + smm_ref[...]
    norm = jnp.sum(z2m_ref[...] * z2m_ref[...]) * (live_ref[0:1, 0:1] / (nmem * d * chains))
    lane = lax.broadcasted_iota(jnp.int32, (1, d - w1), 1)
    norms = jnp.where(lane == me, norm, 0.0)
    first = jnp.where(me == 0, 1.0, 0.0)
    for c, o in enumerate((keep_ref, send_ref)):
        x = nn(lt[0], gqkv_ref[c])
        r = nn(lt[1, :, 0:seg], a_ref[c]) + nn(lt[1, :, seg:], am_ref[c])
        x = jnp.concatenate([x, r[:, 0:w1]], axis=1).astype(BF)
        j = 2 * y + c
        second = jnp.concatenate([qvb_ref[j, 1:2, 0:w1], norms], axis=1)
        third = ubg_ref[j] + ubgm_ref[j]
        rest = gm_ref[j ^ me][0:5] * first
        for i in range(nd):
            o[0, i, 0:chunk, :] = x[i * chunk : (i + 1) * chunk]
            part = [vecs[t : t + 1, i * chunk : (i + 1) * chunk] for t in range(6)]
            top = jnp.concatenate(part + [qvb_ref[j, 0:1, 0:w1]], axis=1)
            o[0, i, chunk:n, :] = jnp.concatenate([top, second, third, rest], axis=0).astype(BF)


def attention_grad(
    me, tok, m, gqkv, gr1, gr1m, a, am, sm, smm, ubg, ubgm, qvb, gm, z2m, live, nmem, chains, deps=()
):
    seg, d = tok.shape
    mp = m.shape[0]
    nb, keys, w3 = gqkv.shape
    nd = 8
    n = d // nd + 8
    block = lambda y: (y, 0, 0)
    block4 = lambda y: (y, 0, 0, 0)
    flat = lambda x: pl.BlockSpec(x.shape, lambda y: (0,) * x.ndim)
    return pl.pallas_call(
        after(functools.partial(attention_grad_kernel, nmem, chains), 16, len(deps)),
        grid=(nb // 2,),
        out_shape=[jax.ShapeDtypeStruct((nb // 2, nd, n, d), BF)] * 2,
        in_specs=[
            sm_spec(),
            flat(tok),
            flat(m),
            pl.BlockSpec((2, keys, w3), block),
            flat(gr1),
            flat(gr1m),
            pl.BlockSpec((2, seg, 4 * HD), block),
            pl.BlockSpec((2, mp, 4 * HD), block),
        ]
        + [flat(x) for x in (sm, smm, ubg, ubgm, qvb, gm, z2m, live)]
        + [any_spec()] * len(deps),
        out_specs=[pl.BlockSpec((1, nd, n, d), block4)] * 2,
        scratch_shapes=[pltpu.VMEM((2, d, keys), BF)],
        compiler_params=params(26),
        cost_estimate=pl.CostEstimate(
            flops=2 * seg * d * d * 4, bytes_accessed=16 * d * d, transcendentals=0
        ),
        name="attention_grad",
    )(me, tok, m, gqkv, gr1, gr1m, a, am, sm, smm, ubg, ubgm, qvb, gm, z2m, live, *deps)


def hold_kernel(*refs):
    pass


def hold(xs, deps=()):
    args = [*xs, *deps]
    return pl.pallas_call(
        hold_kernel,
        out_shape=[jax.ShapeDtypeStruct(x.shape, x.dtype) for x in xs],
        in_specs=[any_spec()] * len(args),
        out_specs=[any_spec()] * len(xs),
        input_output_aliases={i: i for i in range(len(xs))},
        compiler_params=params(1),
        name="hold",
    )(*args)


def pack_kernel(q_ref, k_ref, v_ref, o_ref, u_ref, d_ref, out_ref):
    n, w1 = q_ref.shape
    d = u_ref.shape[1]
    for i, r in enumerate((q_ref, k_ref, v_ref)):
        out_ref[:, i * w1 : (i + 1) * w1] = r[...]
    out_ref[:, 3 * w1 : 4 * w1] = o_ref[...].astype(F32).T.astype(BF)
    out_ref[:, d : 2 * d] = u_ref[...]
    out_ref[:, 2 * d : 3 * d] = d_ref[...].astype(F32).T.astype(BF)


def pack(*weights):
    n = weights[0].shape[0]
    d = weights[4].shape[1]
    return pl.pallas_call(
        pack_kernel,
        out_shape=jax.ShapeDtypeStruct((n, 3 * d), BF),
        in_specs=[vm_spec()] * 6,
        out_specs=vm_spec(),
        name="pack",
    )(*weights)


def flip(a, axis, bit):
    return lax.ppermute(a, axis, [(i, i ^ bit) for i in range(lax.axis_size(axis))])


def shift(a, by):
    n = lax.axis_size("dp")
    return lax.ppermute(a, "dp", [(i, (i + by) % n) for i in range(n)])


def add(*xs):
    total = xs[0].astype(F32)
    for x in xs[1:]:
        total = total + x.astype(F32)
    return total.astype(BF)


def pick(a, i, axis):
    return lax.dynamic_index_in_dim(a, i, axis, keepdims=False)


def y_half(a):
    return add(a[0], flip(a[1], "mp", 2))


def x_half(a, axis):
    b = lax.axis_index("dp") % 2
    return add(pick(a, b, axis), flip(pick(a, 1 - b, axis), "dp", 1))


def z_quarter(a):
    z = lax.axis_index("dp") // 2
    part = [pick(a, (z + i) % 4, 0) for i in range(4)]
    return add(part[0], shift(part[1], 2), shift(part[3], -2), shift(part[2], 4))


def reduce_core(keep, send):
    _, _, n, c = keep.shape
    return add(keep, flip(send, "mp", 1)).reshape(2, 4, 2, n, c)


def reduce_xy1(t):
    half = t.shape[-1] // 2
    return x_half(t[..., :half], 2), y_half(t[..., half:])


def reduce_xy2(first, second):
    return jnp.stack([y_half(first), x_half(second, 1)], 1)


def reduce_z(t):
    s = z_quarter(t)
    return jnp.concatenate([s[0], s[1]], axis=1)


def exchange(x):
    me = lax.axis_index("mp")
    nb = x.shape[0]
    got = [pick(x, me, 0)]
    for i in range(1, nb):
        got.append(flip(pick(x, me ^ i, 0), "mp", i))
    return relative(jnp.stack(got))


def relative(x):
    me = lax.axis_index("mp")
    v = x.reshape((2, 2) + x.shape[1:])
    v = jnp.where(me % 2 == 1, v[:, ::-1], v)
    v = jnp.where(me // 2 == 1, v[::-1], v)
    return v.reshape(x.shape)


def gather_small(x):
    nd = lax.axis_size("dp")
    nb = lax.axis_size("mp")
    if nd != 8:
        return lax.all_gather(x, ("mp", "dp"), axis=0).reshape(nb, nd, -1)
    k = x.shape[0]
    t = x.reshape(1, k)
    me = lax.axis_index("dp")
    b = me % 2
    z = me // 2
    o = flip(t, "mp", 1)
    c = lax.axis_index("mp") % 2
    t = jnp.where(c == 0, jnp.concatenate([t, o]), jnp.concatenate([o, t]))
    o = flip(t, "mp", 2)
    y = lax.axis_index("mp") // 2
    t = jnp.where(y == 0, jnp.concatenate([t, o]), jnp.concatenate([o, t]))
    o = flip(t, "dp", 1)
    t = jnp.where(b == 0, jnp.stack([t, o]), jnp.stack([o, t]))
    up, down, far = shift(t, -2), shift(t, 2), shift(t, 4)
    ring = jnp.stack([t, up, far, down, t, up, far])
    t = lax.dynamic_slice_in_dim(ring, (4 - z) % 4, 4, 0)
    return t.reshape(nd, nb, k).transpose(1, 0, 2)


def body(
    tokens, memory_init, query_weight, query_bias, key_weight, value_weight, value_bias, out_weight,
    out_bias, first_gain, first_shift, up_weight, up_bias, down_weight, down_bias, second_gain,
    second_shift, cotangent, group_segs, chain_group
):
    nd = lax.axis_size("dp")
    nb = lax.axis_size("mp")
    me = lax.axis_index("mp")
    me1 = me.astype(jnp.int32).reshape(1)
    segments = tokens.shape[1]
    d = tokens.shape[3]
    part = tokens.shape[2]
    seg = part * nb
    nmem = memory_init.shape[0] * nb
    pad = -(-nmem // 16) * 16
    both = ("mp", "dp")
    wl = pack(query_weight, key_weight, value_weight, out_weight, up_weight, down_weight)
    w = lax.all_gather(wl, both, axis=0).reshape(nb, d, 3 * d)
    vecs = (out_bias, first_gain, first_shift, down_bias, second_gain, second_shift)
    small = jnp.concatenate(
        (query_bias, value_bias, up_bias) + vecs + (memory_init.reshape(-1),)
    )
    n1 = query_bias.shape[0]
    n2 = up_bias.shape[0]
    sg = gather_small(small)
    qb = sg[:, :, 0:n1].reshape(nb, 1, -1).astype(F32)
    vb = sg[:, :, n1 : 2 * n1].reshape(nb, 1, -1).astype(F32)
    qkvb = jnp.concatenate([qb, jnp.zeros_like(qb), vb], axis=2)
    ub = sg[:, :, 2 * n1 : 2 * n1 + n2].reshape(nb, 1, -1).astype(F32)
    at = 2 * n1 + n2
    vec = sg[:, :, at : at + 6 * n1].reshape(nb, nd, 6, n1).transpose(2, 1, 0, 3).reshape(6, d)
    vec = jnp.pad(vec.astype(F32), ((0, 2), (0, 0)))
    ml = memory_init.shape[0]
    m0 = sg[:, :, at + 6 * n1 :].reshape(nb, nd, ml, -1).transpose(0, 2, 1, 3).reshape(nmem, d)
    m0 = jnp.pad(m0.astype(F32), ((0, pad - nmem), (0, 0)))
    tok = exchange(tokens[0]).reshape(seg, d)
    ct = exchange(cotangent[0]).reshape(seg, d)
    match = chain_group[:, None] == jnp.arange(group_segs.shape[0], dtype=jnp.int32)[None, :]
    count = jnp.sum(jnp.where(match, group_segs[None, :], 0))
    live = (me < count).astype(F32)
    live2 = jnp.full((8, 128), live, F32)
    q, k, v = qkv_call(me1, tok, w, qkvb)
    m = jnp.where(me == 0, m0, 0.0)
    own = m
    for s in range(segments - 1):
        (z,) = mem_forward(me1, m, k, v, w, qkvb, ub, vec, nmem, False)
        m = lax.ppermute(z, "mp", [(s, s + 1)])
        own = own + m
    (out, z1b, a, g, gf, gr2b, gr1, gq, gk, gv, base, sm, ubg) = token_call(
        me1, tok, ct, live2, own, q, k, v, w, qkvb, ub, vec, nmem
    )
    z2m, *saved = mem_forward(me1, own, k, v, w, qkvb, ub, vec, nmem, True, (base,))
    am, z1m, g_m = saved[4:7]
    send = base
    gin = jnp.zeros_like(base)
    for s in reversed(range(segments - 1)):
        recv = lax.ppermute(send, "mp", [(s + 1, s)])
        gin = gin + recv
        if s > 0:
            send = mem_backward(me1, recv, k, v, w, vec, base, saved)
    layer_out = exchange(out.reshape(nb, part, d))
    gr2m, gfm, gr1m, smm, ubgm = last_feed(me1, gin, w, vec, saved, (layer_out,))
    tuned = nd == 8
    chunk = d // nd
    blocks = lambda pair: [x.reshape(2, nd, chunk, d) for x in pair]
    up_g = feed_grad(z1b, z1m, gf, gfm)
    down_g = feed_grad(gr2b, gr2m, g, g_m, (up_g[0],))
    deps = ()
    if tuned:
        up_s = reduce_core(*blocks(up_g))
        deps = (up_s, down_g[0])
    gm, gqkv, ig, qvb = last_attention(
        me1, gr1m, k, v, w, saved, gq, gk, gv, gr1, nmem, deps
    )
    if tuned:
        down_s = reduce_core(*blocks(down_g))
        up_s = reduce_xy1(up_s)
        deps = (down_s,) + up_s
    chains = nd * tokens.shape[0]
    w1 = d // nb
    att_g = attention_grad(
        me1, tok, own, gqkv, gr1, gr1m, a, am, sm, smm, ubg, ubgm, qvb, gm, z2m, live2, nmem, chains, deps
    )
    if tuned:
        keep, send, up_s, d1, d2, ig = hold(
            [*att_g, reduce_xy2(*up_s), *reduce_xy1(down_s), ig.reshape(nb, part, d)]
        )
        att_s = reduce_core(keep, send)
        wup = reduce_z(up_s)
        down_s = reduce_xy2(d1, d2)
        input_grad = exchange(ig)
        att_s, down_s = hold([att_s, down_s], (wup, input_grad))
        wup = wup.astype(F32)
        wdn = reduce_z(down_s)
        t1, t2 = hold(reduce_xy1(att_s), (wdn,))
        wdn = wdn.astype(F32)
        watt = reduce_z(reduce_xy2(t1, t2)).astype(F32)
        extra = watt[chunk:]
        vg = lax.dynamic_slice(
            extra[0, 0 : 6 * chunk].reshape(6, chunk), (0, me * n1), (6, n1)
        )
        at_dp = lax.axis_index("dp")
        qbg = lax.dynamic_slice(extra[0, 6 * chunk :], (at_dp * n1,), (n1,))
        vbg = lax.dynamic_slice(extra[1, 0:w1], (at_dp * n1,), (n1,))
        ubt = lax.dynamic_slice(extra[2], (at_dp * n2,), (n2,))
        gmi = lax.dynamic_slice(extra[3 : 3 + ml], (0, at_dp * chunk), (ml, chunk))
        norms = extra[1, w1 : w1 + segments]
        watt = watt[0:chunk]
    else:
        input_grad = exchange(ig.reshape(nb, part, d))

        def scatter(keep, send):
            x = relative(jnp.stack([keep, send], axis=1).reshape(nb, d, d))
            x = x.reshape(nb * nd, chunk, d)
            return lax.psum_scatter(x, both, scatter_dimension=0, tiled=False).astype(F32)

        att_g = [x[:, :, 0 : d // 8] for x in att_g]
        wup, wdn, watt = scatter(*up_g), scatter(*down_g), scatter(*att_g)
        norm = live * jnp.sum(z2m * z2m) / (nmem * d * chains)
        norms = jnp.where(jnp.arange(segments) == me, norm, 0.0)
        smt = (sm + smm)[0:6].reshape(6, nd, nb, n1).transpose(2, 1, 0, 3).reshape(nb, nd, -1)
        gmi = jnp.where(me == 0, gm[:, 0:ml], 0.0).reshape(nb, ml, nd, -1).transpose(0, 2, 1, 3)
        smalls = jnp.concatenate(
            [
                relative(qvb[:, 0, 0:w1]).reshape(nb, nd, n1),
                relative(qvb[:, 1, 0:w1]).reshape(nb, nd, n1),
                relative(ubg + ubgm).reshape(nb, nd, n2),
                smt,
                gmi.reshape(nb, nd, -1),
                jnp.broadcast_to(norms, (nb, nd, segments)),
            ],
            axis=2,
        ).reshape(nb * nd, -1)
        sr = lax.psum_scatter(smalls, both, scatter_dimension=0, tiled=False)
        qbg = sr[0:n1]
        vbg = sr[n1 : 2 * n1]
        ubt = sr[2 * n1 : at]
        vg = sr[at : at + 6 * n1].reshape(6, n1)
        norms = sr[-segments:]
        gmi = sr[at + 6 * n1 : -segments].reshape(ml, d // nd)
    return (
        layer_out[None],
        input_grad[None],
        gmi,
        watt[:, 0:w1],
        qbg,
        watt[:, w1 : 2 * w1],
        watt[:, 2 * w1 : 3 * w1],
        vbg,
        watt[:, 3 * w1 : d].T,
        vg[0],
        vg[1],
        vg[2],
        wup,
        ubt,
        wdn.T,
        vg[3],
        vg[4],
        vg[5],
        norms,
    )


def solution(mesh):
    rows = P("dp", None, "mp", None)
    md, dm = P(("mp", "dp")), P(("dp", "mp"))
    win, wout = P("dp", "mp"), P("mp", "dp")
    in_specs = (
        rows, wout, win, md, win, win, md, wout, dm, dm, dm, win, md, wout, dm, dm, dm, rows, P(),
        P("dp"),
    )
    out_specs = (
        rows, rows, wout, win, md, win, win, md, wout, dm, dm, dm, win, md, wout, dm, dm, dm, P(),
    )
    return jax.shard_map(body, mesh=mesh, in_specs=in_specs, out_specs=out_specs, check_vma=False)
```

```python
import functools

import jax
import jax.numpy as jnp
from jax import lax
from jax.experimental import pallas as pl
from jax.experimental.pallas import tpu as pltpu
from jax.sharding import PartitionSpec as P

HD = 64
HPB = 3
BF = jnp.bfloat16
F32 = jnp.float32
MIB = 1024 * 1024
NEG = -1e30


def nn(a, b):
    return lax.dot_general(a, b, (((1,), (0,)), ((), ())), preferred_element_type=F32)


def nt(a, b):
    return lax.dot_general(a, b, (((1,), (1,)), ((), ())), preferred_element_type=F32)


def norm_stats(r):
    mean = jnp.mean(r, axis=-1, keepdims=True)
    c = r - mean
    inv = lax.rsqrt(jnp.mean(c * c, axis=-1, keepdims=True) + 1e-05)
    return c * inv, inv


def norm_back(g, xh, inv):
    return inv * (
        g - jnp.mean(g, axis=-1, keepdims=True) - xh * jnp.mean(g * xh, axis=-1, keepdims=True)
    )


def gelu_both(f):
    cdf = 0.5 + 0.5 * lax.erf(f * (0.5**0.5))
    pdf = jnp.exp(-0.5 * f * f) * ((2.0 * jnp.pi) ** -0.5)
    return f * cdf, cdf + f * pdf


def rows_mask(shape, count):
    return lax.broadcasted_iota(jnp.int32, shape, 0) < count


def any_spec():
    return pl.BlockSpec(memory_space=pl.ANY)


def vm_spec():
    return pl.BlockSpec(memory_space=pltpu.VMEM)


def params(mib):
    return pltpu.CompilerParams(vmem_limit_bytes=mib * MIB)


def sm_spec():
    return pl.BlockSpec(memory_space=pltpu.SMEM)


def after(kernel, n_in, n_dep):
    def run(*refs):
        kernel(*refs[:n_in], *refs[n_in + n_dep :])

    return run


def split_qkv(acc):
    w1 = HPB * HD
    zero = jnp.zeros((acc.shape[0], HD), BF)
    q = jnp.concatenate([(acc[:, 0:w1].astype(BF) * 0.125).astype(BF), zero], axis=1)
    k = jnp.concatenate([acc[:, w1 : 2 * w1].astype(BF), zero], axis=1)
    v = jnp.concatenate([acc[:, 2 * w1 : 3 * w1].astype(BF), zero], axis=1)
    return q, k, v


def head_cols(shape, i):
    c = lax.broadcasted_iota(jnp.int32, shape, len(shape) - 1)
    return (c >= i * HD) & (c < (i + 1) * HD)


def spread(x):
    return jnp.concatenate(
        [jnp.where(head_cols(x.shape, i), x, jnp.zeros_like(x)) for i in range(HPB)], axis=0
    )


def gather_heads(x):
    n = x.shape[0] // HPB
    out = jnp.zeros((n, x.shape[1]), x.dtype)
    for i in range(HPB):
        out = jnp.where(head_cols(out.shape, i), x[i * n : (i + 1) * n], out)
    return out


def out_cols(a):
    return jnp.concatenate([jnp.zeros((a.shape[0], HD), a.dtype), a[:, 0 : HPB * HD]], axis=1)


def qkv_kernel(me_ref, tok_ref, w_ref, qkvb_ref, q_ref, k_ref, v_ref):
    nb, d, _ = w_ref.shape
    me = me_ref[0]
    for j in range(nb):
        acc = nn(tok_ref[...], w_ref[j ^ me, :, 0 : 3 * HPB * HD]) + qkvb_ref[j ^ me]
        q, k, v = split_qkv(acc)
        q_ref[j] = q
        k_ref[j] = k
        v_ref[j] = v


def qkv_call(me, tok, w, qkvb):
    nb, d, _ = w.shape
    s = tok.shape[0]
    return pl.pallas_call(
        qkv_kernel,
        out_shape=[jax.ShapeDtypeStruct((nb, s, 4 * HD), BF)] * 3,
        in_specs=[sm_spec(), vm_spec(), vm_spec(), vm_spec()],
        out_specs=[vm_spec()] * 3,
        compiler_params=params(20),
        cost_estimate=pl.CostEstimate(
            flops=2 * s * d * 3 * d, bytes_accessed=8 * d * d, transcendentals=0
        ),
        name="qkv",
    )(me, tok, w, qkvb)


def mem_forward_kernel(
    nmem, save, me_ref, m_ref, k_hbm, v_hbm, w_ref, qkvb_ref, ub_ref, vec_ref, *rest
):
    if save:
        (
            z2_ref, qm_ref, km_ref, vm_ref, pm_ref, am_ref, z1b_ref, g_ref, gp_ref, xh1_ref,
            xh2_ref, inv_ref,
        ) = rest[:12]
        rest = rest[12:]
    else:
        z2_ref = rest[0]
        rest = rest[1:]
    kk, vv, sc, sem2 = rest
    nb, d, _ = w_ref.shape
    seg = k_hbm.shape[1]
    mp = m_ref.shape[0]
    keys = seg + mp
    w1 = HPB * HD
    me = me_ref[0]
    kc = pltpu.make_async_copy(k_hbm, kk.at[:, 0:seg, :], sem2.at[0])
    vc = pltpu.make_async_copy(v_hbm, vv.at[:, 0:seg, :], sem2.at[1])
    kc.start()
    vc.start()
    mem = m_ref[...]
    mb = mem.astype(BF)
    qs = []
    for j in range(nb):
        acc = nn(mb, w_ref[j ^ me, :, 0 : 3 * w1]) + qkvb_ref[j ^ me]
        q, k, v = split_qkv(acc)
        qs.append(q)
        kk[j, seg:keys, :] = k
        vv[j, seg:keys, :] = v
        if save:
            qm_ref[j] = q
            km_ref[j] = k
            vm_ref[j] = v
    kc.wait()
    vc.wait()
    n = HPB * mp
    for j in range(nb):
        sc[j * n : (j + 1) * n, :] = nt(spread(qs[j]), kk[j])
    keep = lax.broadcasted_iota(jnp.int32, (n, keys), 1) < seg + nmem
    heads = []
    for j in range(nb):
        s = jnp.where(keep, sc[j * n : (j + 1) * n, :], NEG)
        e = jnp.exp(s - jnp.max(s, axis=-1, keepdims=True))
        p = (e / jnp.sum(e, axis=-1, keepdims=True)).astype(BF)
        if save:
            pm_ref[j] = p
        heads.append(p)
    out = jnp.zeros((mp, d), F32)
    for j in range(nb):
        a = gather_heads(nn(heads[j], vv[j])).astype(BF)
        if save:
            am_ref[j] = a
        out += nt(out_cols(a), w_ref[j ^ me, :, d - 4 * HD : d])
    xh1, inv1 = norm_stats(mem + out + vec_ref[0:1])
    z1 = xh1 * vec_ref[1:2] + vec_ref[2:3]
    z1b = z1.astype(BF)
    y = jnp.zeros((mp, d), F32)
    for j in range(nb):
        f = nn(z1b, w_ref[j ^ me, :, d : 2 * d]) + ub_ref[j ^ me]
        g, gp = gelu_both(f)
        g = g.astype(BF)
        if save:
            g_ref[j] = g
            gp_ref[j] = gp
        y += nt(g, w_ref[j ^ me, :, 2 * d : 3 * d])
    xh2, inv2 = norm_stats(z1 + y + vec_ref[3:4])
    z2 = xh2 * vec_ref[4:5] + vec_ref[5:6]
    z2_ref[...] = jnp.where(rows_mask((mp, d), nmem), z2, 0.0)
    if save:
        z1b_ref[...] = z1b
        xh1_ref[...] = xh1
        xh2_ref[...] = xh2
        inv_ref[:, 0:128] = jnp.broadcast_to(inv1, (mp, 128))
        inv_ref[:, 128:256] = jnp.broadcast_to(inv2, (mp, 128))


def mem_forward(me, m, k, v, w, qkvb, ub, vec, nmem, save, deps=()):
    nb, d, _ = w.shape
    seg = k.shape[1]
    mp = m.shape[0]
    keys = seg + mp
    sds = jax.ShapeDtypeStruct
    shapes = [sds((mp, d), F32)]
    if save:
        shapes += [sds((nb, mp, 4 * HD), BF)] * 3
        shapes += [
            sds((nb, HPB * mp, keys), BF),
            sds((nb, mp, 4 * HD), BF),
            sds((mp, d), BF),
            sds((nb, mp, d), BF),
            sds((nb, mp, d), F32),
            sds((mp, d), F32),
            sds((mp, d), F32),
            sds((mp, 256), F32),
        ]
    return pl.pallas_call(
        after(functools.partial(mem_forward_kernel, nmem, save), 8, len(deps)),
        out_shape=shapes,
        in_specs=[sm_spec(), vm_spec()]
        + [any_spec()] * 2
        + [vm_spec()] * 4
        + [any_spec()] * len(deps),
        out_specs=[vm_spec()] * len(shapes),
        scratch_shapes=[
            pltpu.VMEM((nb, keys, 4 * HD), BF),
            pltpu.VMEM((nb, keys, 4 * HD), BF),
            pltpu.VMEM((nb * HPB * mp, keys), F32),
            pltpu.SemaphoreType.DMA((2,)),
        ],
        compiler_params=params(24),
        cost_estimate=pl.CostEstimate(
            flops=2 * mp * d * d * 12, bytes_accessed=24 * d * d, transcendentals=0
        ),
        name="mem_forward_save" if save else "mem_forward",
    )(me, m, k, v, w, qkvb, ub, vec, *deps)


def colsum(x):
    return jnp.sum(x, axis=0, keepdims=True)


CH = 64


def token_kernel(
    nmem,
    me_ref,
    tok_ref,
    ct_ref,
    live_ref,
    m_ref,
    q_hbm,
    k_hbm,
    v_hbm,
    w_ref,
    qkvb_ref,
    ub_ref,
    vec_ref,
    out_ref,
    z1b_ref,
    a0_ref,
    a1_ref,
    g0_ref,
    g1_ref,
    gf0_ref,
    gf1_ref,
    gr2b_ref,
    gr1_ref,
    g1b,
    gq_ref,
    gk_ref,
    gv_ref,
    base_ref,
    small_ref,
    ubg_ref,
    qq,
    kk,
    vv,
    probs,
    big,
    one,
    xh1,
    inv,
    gp,
    sem2,
):
    nb, d, _ = w_ref.shape
    seg = tok_ref.shape[0]
    mp = m_ref.shape[0]
    keys = seg + mp
    w1 = HPB * HD
    steps = seg // CH
    me = me_ref[0]
    loads = [
        pltpu.make_async_copy(q_hbm, qq, sem2.at[0]),
        pltpu.make_async_copy(k_hbm, kk.at[:, 0:seg, :], sem2.at[1]),
        pltpu.make_async_copy(v_hbm, vv.at[:, 0:seg, :], sem2.at[2]),
    ]
    for c in loads:
        c.start()
    mb = m_ref[...].astype(BF)
    for j in range(nb):
        _, k, v = split_qkv(nn(mb, w_ref[j ^ me, :, 0 : 3 * w1]) + qkvb_ref[j ^ me])
        kk[j, seg:keys, :] = k
        vv[j, seg:keys, :] = v
    for c in loads:
        c.wait()
    one[...] = jnp.zeros_like(one)
    tail = seg + (nmem // 8) * 8

    a_refs = (a0_ref, a1_ref)
    g_refs = (g0_ref, g1_ref)
    gf_refs = (gf0_ref, gf1_ref)

    def attend_one(j, y, c):
        vt = vv[j].astype(F32).T.astype(BF)
        parts = []
        for i in range(HPB):
            cols = slice(i * HD, (i + 1) * HD)
            big[0:keys, 0:seg] = nt(kk[j, :, cols], qq[j, :, cols])
            big[tail:keys, 0:seg] = jnp.where(
                rows_mask((keys - tail, seg), seg + nmem - tail), big[tail:keys, 0:seg], NEG
            )
            for t in range(seg // 128):
                cols = slice(t * 128, (t + 1) * 128)
                s = big[0:keys, cols]
                e = jnp.exp(s - jnp.max(s, axis=0, keepdims=True))
                p = e * (1.0 / jnp.sum(e, axis=0, keepdims=True))
                probs[j * HPB + i, :, cols] = p.astype(BF)
            parts.append(nn(vt[i * HD : (i + 1) * HD], probs[j * HPB + i]))
        parts.append(jnp.zeros((HD, seg), F32))
        a = jnp.concatenate(parts, axis=0).T.astype(BF)
        a_refs[c][y] = a
        one[...] += nt(out_cols(a), w_ref[j ^ me, :, d - 4 * HD : d])

    def attend(y, _):
        for c in range(2):
            attend_one(2 * y + c, y, c)
        return 0

    lax.fori_loop(0, nb // 2, attend, 0)

    def first(c, _):
        rows = pl.ds(pl.multiple_of(c * CH, CH), CH)
        r = tok_ref[rows, :].astype(F32) + one[rows, :] + vec_ref[0:1]
        x, v = norm_stats(r)
        xh1[rows, :] = x
        inv[rows, 0:128] = jnp.broadcast_to(v, (CH, 128))
        z1 = x * vec_ref[1:2] + vec_ref[2:3]
        z1b_ref[rows, :] = z1.astype(BF)
        one[rows, :] = z1 + vec_ref[3:4]
        return 0

    lax.fori_loop(0, steps, first, 0)

    def feed_one(j, y, c):
        big[0:seg, 0:d] = nn(z1b_ref[...], w_ref[j ^ me, :, d : 2 * d])

        def act(r, _):
            rows = pl.ds(pl.multiple_of(r * 32, 32), 32)
            g, p = gelu_both(big[rows, 0:d] + ub_ref[j ^ me])
            g_refs[c][y, rows, :] = g.astype(BF)
            gp[j, rows, :] = p.astype(BF)
            return 0

        lax.fori_loop(0, seg // 32, act, 0)
        one[...] += nt(g_refs[c][y], w_ref[j ^ me, :, 2 * d : 3 * d])

    def feed(y, _):
        for c in range(2):
            feed_one(2 * y + c, y, c)
        return 0

    lax.fori_loop(0, nb // 2, feed, 0)
    zero = jnp.zeros((1, d), F32)

    def second(c, carry):
        sg, ss, sb = carry
        rows = pl.ds(pl.multiple_of(c * CH, CH), CH)
        x, v = norm_stats(one[rows, :])
        out_ref[rows, :] = ((x * vec_ref[4:5] + vec_ref[5:6]) * live_ref[0:1, 0:1]).astype(BF)
        gz = ct_ref[rows, :].astype(F32) * live_ref[0:1, 0:1]
        gr = norm_back(gz * vec_ref[4:5], x, v)
        one[rows, :] = gr
        gr2b_ref[rows, :] = gr.astype(BF)
        return (sg + colsum(gz * x), ss + colsum(gz), sb + colsum(gr))

    sg, ss, sb = lax.fori_loop(0, steps, second, (zero, zero, zero))
    small_ref[3:4] = sb
    small_ref[4:5] = sg
    small_ref[5:6] = ss

    def feed_back_one(j, y, c):
        big[0:seg, 0:d] = nn(gr2b_ref[...], w_ref[j ^ me, :, 2 * d : 3 * d])

        def act(r, total):
            rows = pl.ds(pl.multiple_of(r * CH, CH), CH)
            gf = (big[rows, 0:d] * gp[j, rows, :].astype(F32)).astype(BF)
            gf_refs[c][y, rows, :] = gf
            return total + colsum(gf.astype(F32))

        ubg_ref[j] = lax.fori_loop(0, steps, act, zero)
        one[...] += nt(gf_refs[c][y], w_ref[j ^ me, :, d : 2 * d])

    def feed_back(y, _):
        for c in range(2):
            feed_back_one(2 * y + c, y, c)
        return 0

    lax.fori_loop(0, nb // 2, feed_back, 0)

    def first_back(c, carry):
        sg, ss, sb = carry
        rows = pl.ds(pl.multiple_of(c * CH, CH), CH)
        gz = one[rows, :]
        x = xh1[rows, :]
        gr = norm_back(gz * vec_ref[1:2], x, inv[rows, 0:1])
        gr1_ref[rows, :] = gr
        g1b[rows, :] = gr.astype(BF)
        return (sg + colsum(gz * x), ss + colsum(gz), sb + colsum(gr))

    sg, ss, sb = lax.fori_loop(0, steps, first_back, (zero, zero, zero))
    small_ref[0:1] = sb
    small_ref[1:2] = sg
    small_ref[2:3] = ss
    small_ref[6:8] = jnp.zeros((2, d), F32)

    def attend_back_one(j, y, c, base):
        ga = nn(g1b[...], w_ref[j ^ me, :, d - 4 * HD : d])[:, HD:]
        gab = ga.astype(BF)
        delta = (gab.astype(F32) * a_refs[c][y, :, 0:w1].astype(F32)).T
        kt = kk[j].astype(F32).T.astype(BF)
        gqs = []
        gks = []
        gvs = []
        for i in range(HPB):
            cols = slice(i * HD, (i + 1) * HD)
            g = gab[:, cols]
            p = probs[j * HPB + i]
            dl = jnp.sum(delta[cols], axis=0, keepdims=True)
            gvs.append(nn(p, g))
            gs = (p.astype(F32) * (nt(vv[j, :, cols], g) - dl)).astype(BF)
            gks.append(nn(gs, qq[j, :, cols]))
            gqs.append(nn(kt[cols], gs))
        zq = jnp.zeros((HD, seg), F32)
        zk = jnp.zeros((keys, HD), F32)
        gq_ref[j] = (jnp.concatenate(gqs + [zq], axis=0).T * 0.125).astype(BF)
        gk = jnp.concatenate(gks + [zk], axis=1)
        gv = jnp.concatenate(gvs + [zk], axis=1)
        gk_ref[j] = gk.astype(BF)
        gv_ref[j] = gv.astype(BF)
        gm = jnp.concatenate(
            [jnp.zeros((mp, w1), F32), gk[seg:keys, 0:w1], gv[seg:keys, 0:w1]], axis=1
        ).astype(BF)
        return base + nt(gm, w_ref[j ^ me, :, 0 : 3 * w1])

    def attend_back(y, base):
        for c in range(2):
            base = attend_back_one(2 * y + c, y, c, base)
        return base

    base_ref[...] = lax.fori_loop(0, nb // 2, attend_back, jnp.zeros((mp, d), F32))


def token_call(me, tok, ct, live, m, q, k, v, w, qkvb, ub, vec, nmem):
    nb, d, _ = w.shape
    seg = tok.shape[0]
    mp = m.shape[0]
    keys = seg + mp
    sds = jax.ShapeDtypeStruct
    shapes = [
        sds((seg, d), BF),
        sds((seg, d), BF),
        sds((nb // 2, seg, 4 * HD), BF),
        sds((nb // 2, seg, 4 * HD), BF),
        sds((nb // 2, seg, d), BF),
        sds((nb // 2, seg, d), BF),
        sds((nb // 2, seg, d), BF),
        sds((nb // 2, seg, d), BF),
        sds((seg, d), BF),
        sds((seg, d), F32),
        sds((seg, d), BF),
        sds((nb, seg, 4 * HD), BF),
        sds((nb, keys, 4 * HD), BF),
        sds((nb, keys, 4 * HD), BF),
        sds((mp, d), F32),
        sds((8, d), F32),
        sds((nb, 1, d), F32),
    ]
    return pl.pallas_call(
        functools.partial(token_kernel, nmem),
        out_shape=shapes,
        in_specs=[sm_spec()] + [vm_spec()] * 4 + [any_spec()] * 3 + [vm_spec()] * 4,
        out_specs=[vm_spec()] * len(shapes),
        scratch_shapes=[
            pltpu.VMEM((nb, seg, 4 * HD), BF),
            pltpu.VMEM((nb, keys, 4 * HD), BF),
            pltpu.VMEM((nb, keys, 4 * HD), BF),
            pltpu.VMEM((nb * HPB, keys, seg), BF),
            pltpu.VMEM((keys, d), F32),
            pltpu.VMEM((seg, d), F32),
            pltpu.VMEM((seg, d), F32),
            pltpu.VMEM((seg, 128), F32),
            pltpu.VMEM((nb, seg, d), BF),
            pltpu.SemaphoreType.DMA((3,)),
        ],
        compiler_params=params(48),
        cost_estimate=pl.CostEstimate(
            flops=5 * seg * d * d * 12, bytes_accessed=60 * d * d, transcendentals=0
        ),
        name="token_rows",
    )(me, tok, ct, live, m, q, k, v, w, qkvb, ub, vec)


def back_feed(w_ref, me, nb, d, gz, vec_ref, gp_ref, xh1, xh2, inv_ref, gf_ref=None, ubg_ref=None):
    gr2 = norm_back(gz * vec_ref[4:5], xh2, inv_ref[:, 128:129])
    gr2b = gr2.astype(BF)
    acc = gr2
    for j in range(nb):
        gf = (nn(gr2b, w_ref[j ^ me, :, 2 * d : 3 * d]) * gp_ref[j]).astype(BF)
        if gf_ref is not None:
            gf_ref[j] = gf
            ubg_ref[j] = colsum(gf.astype(F32))
        acc += nt(gf, w_ref[j ^ me, :, d : 2 * d])
    return gr2, acc, norm_back(acc * vec_ref[1:2], xh1, inv_ref[:, 0:1])


def back_scores(j, gab, am_ref, pm_ref, vv, delta_rows):
    n = HPB * delta_rows
    gs3 = spread(gab)
    a3 = jnp.concatenate([am_ref[j]] * HPB, axis=0)
    dl = jnp.sum(gs3.astype(F32) * a3.astype(F32), axis=1, keepdims=True)
    p = pm_ref[j].astype(F32)
    return gs3, p, (p * (nt(gs3, vv[j]) - dl)).astype(BF)


def mem_backward_kernel(
    nmem, me_ref, g_ref, k_hbm, v_hbm, w_ref, vec_ref, base_ref, qm_ref, km_ref, vm_ref, pm_ref,
    am_ref, gp_ref, xh1_ref, xh2_ref, inv_ref, gm_ref, kk, vv, sem2
):
    nb, d, _ = w_ref.shape
    seg = k_hbm.shape[1]
    mp = g_ref.shape[0]
    keys = seg + mp
    w1 = HPB * HD
    me = me_ref[0]
    kc = pltpu.make_async_copy(k_hbm, kk.at[:, 0:seg, :], sem2.at[0])
    vc = pltpu.make_async_copy(v_hbm, vv.at[:, 0:seg, :], sem2.at[1])
    kc.start()
    vc.start()
    kk[:, seg:keys, :] = km_ref[...]
    vv[:, seg:keys, :] = vm_ref[...]
    _, _, gr1 = back_feed(
        w_ref, me, nb, d, g_ref[...], vec_ref, gp_ref, xh1_ref[...], xh2_ref[...], inv_ref
    )
    gr1b = gr1.astype(BF)
    kc.wait()
    vc.wait()
    gabs = []
    for j in range(nb):
        ga = nn(gr1b, w_ref[j ^ me, :, d - 4 * HD : d]).astype(BF)
        gabs.append(jnp.concatenate([ga[:, HD:], jnp.zeros((mp, HD), BF)], axis=1))
    scores = [back_scores(j, gabs[j], am_ref, pm_ref, vv, mp) for j in range(nb)]
    out = gr1 + base_ref[...]
    for j in range(nb):
        gs3, p, gs = scores[j]
        gq = gather_heads(nn(gs, kk[j])) * 0.125
        gk = nn(gs[:, seg:keys].astype(F32).T.astype(BF), spread(qm_ref[j]))
        gv = nn(p[:, seg:keys].T.astype(BF), gs3)
        gm = jnp.concatenate([gq[:, 0:w1], gk[:, 0:w1], gv[:, 0:w1]], axis=1).astype(BF)
        out += nt(gm, w_ref[j ^ me, :, 0 : 3 * w1])
    gm_ref[...] = out


def mem_backward(me, g, k, v, w, vec, base, saved):
    nb, d, _ = w.shape
    seg = k.shape[1]
    mp = g.shape[0]
    keys = seg + mp
    qm, km, vm, pm, am, _, _, gp, xh1, xh2, inv = saved
    args = (me, g, k, v, w, vec, base, qm, km, vm, pm, am, gp, xh1, xh2, inv)
    return pl.pallas_call(
        functools.partial(mem_backward_kernel, 0),
        out_shape=jax.ShapeDtypeStruct((mp, d), F32),
        in_specs=[sm_spec(), vm_spec()] + [any_spec()] * 2 + [vm_spec()] * 12,
        out_specs=vm_spec(),
        scratch_shapes=[
            pltpu.VMEM((nb, keys, 4 * HD), BF),
            pltpu.VMEM((nb, keys, 4 * HD), BF),
            pltpu.SemaphoreType.DMA((2,)),
        ],
        compiler_params=params(24),
        cost_estimate=pl.CostEstimate(
            flops=2 * mp * d * d * 12, bytes_accessed=24 * d * d, transcendentals=0
        ),
        name="mem_backward",
    )(*args)


def last_feed_kernel(
    me_ref, g_ref, w_ref, vec_ref, gp_ref, xh1_ref, xh2_ref, inv_ref, z1m_ref, gm_ref, m_ref, am_ref,
    gr2b_ref, gf_ref, gr1_ref, small_ref, ubg_ref, pack_ref
):
    nb, d, _ = w_ref.shape
    me = me_ref[0]
    gz = g_ref[...]
    xh1 = xh1_ref[...]
    xh2 = xh2_ref[...]
    gr2, gz1, gr1 = back_feed(
        w_ref, me, nb, d, gz, vec_ref, gp_ref, xh1, xh2, inv_ref, gf_ref, ubg_ref
    )
    gr2b_ref[...] = gr2.astype(BF)
    gr1_ref[...] = gr1
    mp, _ = gz.shape
    for y in range(nb // 2):
        pack_ref[y] = gf_ref[2 * y + 1]
        pack_ref[5 + y] = gm_ref[2 * y + 1]
        pack_ref[8, :, y * 4 * HD : (y + 1) * 4 * HD] = am_ref[2 * y + 1]
    pack_ref[8, :, 8 * HD : d] = jnp.zeros((mp, d - 8 * HD), BF)
    pack_ref[2] = gr2.astype(BF)
    pack_ref[3] = gr1.astype(BF)
    pack_ref[4] = z1m_ref[...]
    pack_ref[7] = m_ref[...].astype(BF)
    small_ref[0:1] = colsum(gr1)
    small_ref[1:2] = colsum(gz1 * xh1)
    small_ref[2:3] = colsum(gz1)
    small_ref[3:4] = colsum(gr2)
    small_ref[4:5] = colsum(gz * xh2)
    small_ref[5:6] = colsum(gz)
    small_ref[6:8] = jnp.zeros((2, d), F32)


def last_feed(me, g, w, vec, saved, m, deps=()):
    nb, d, _ = w.shape
    mp = g.shape[0]
    _, _, _, _, am, z1m, gm, gp, xh1, xh2, inv = saved
    sds = jax.ShapeDtypeStruct
    shapes = [
        sds((mp, d), BF),
        sds((nb, mp, d), BF),
        sds((mp, d), F32),
        sds((8, d), F32),
        sds((nb, 1, d), F32),
        sds((9, mp, d), BF),
    ]
    return pl.pallas_call(
        after(last_feed_kernel, 12, len(deps)),
        out_shape=shapes,
        in_specs=[sm_spec()] + [vm_spec()] * 11 + [any_spec()] * len(deps),
        out_specs=[vm_spec()] * len(shapes),
        compiler_params=params(20),
        cost_estimate=pl.CostEstimate(
            flops=2 * mp * d * d * 8, bytes_accessed=16 * d * d, transcendentals=0
        ),
        name="last_feed",
    )(me, g, w, vec, gp, xh1, xh2, inv, z1m, gm, m, am, *deps)


def last_attention_kernel(
    nmem, chains, me_ref, gr1m_ref, k_hbm, v_hbm, w_ref, qm_ref, km_ref, vm_ref, pm_ref, am_ref, gq_ref, gk_ref,
    gv_ref, gr1_ref, sm_ref, smm_ref, ubg_ref, ubgm_ref, z2m_ref, live_ref, small_ref, ge_ref, go_ref,
    ig_ref, kk, vv, one, sem2
):
    nb, d, _ = w_ref.shape
    seg = k_hbm.shape[1]
    mp = gr1m_ref.shape[0]
    keys = seg + mp
    w1 = HPB * HD
    me = me_ref[0]
    kc = pltpu.make_async_copy(k_hbm, kk.at[:, 0:seg, :], sem2.at[0])
    vc = pltpu.make_async_copy(v_hbm, vv.at[:, 0:seg, :], sem2.at[1])
    kc.start()
    vc.start()
    kk[:, seg:keys, :] = km_ref[...]
    vv[:, seg:keys, :] = vm_ref[...]
    gr1 = gr1m_ref[...]
    gr1b = gr1.astype(BF)
    kc.wait()
    vc.wait()
    gabs = []
    for j in range(nb):
        ga = nn(gr1b, w_ref[j ^ me, :, d - 4 * HD : d]).astype(BF)
        gabs.append(jnp.concatenate([ga[:, HD:], jnp.zeros((mp, HD), BF)], axis=1))
    scores = [back_scores(j, gabs[j], am_ref, pm_ref, vv, mp) for j in range(nb)]
    out = gr1
    for j in range(nb):
        gs3, p, gs = scores[j]
        gq = (gather_heads(nn(gs, kk[j])) * 0.125).astype(BF)
        gk = (gk_ref[j] + nn(gs.astype(F32).T.astype(BF), spread(qm_ref[j]))).astype(BF)
        gv = (gv_ref[j] + nn(p.T.astype(BF), gs3)).astype(BF)
        gqt = gq_ref[j]
        o = (ge_ref, go_ref)[j % 2]
        y = j // 2
        o[y, 0:seg, 0:w1] = gqt[:, 0:w1]
        o[y, seg:keys, 0:w1] = gq[:, 0:w1]
        o[y, :, w1 : 2 * w1] = gk[:, 0:w1]
        o[y, :, 2 * w1 : 3 * w1] = gv[:, 0:w1]
        small_ref[8 + j : 9 + j] = ubg_ref[j] + ubgm_ref[j]
        small_ref[12 + j : 13 + j] = jnp.concatenate(
            [
                (colsum(gqt.astype(F32)) + colsum(gq.astype(F32)))[:, 0:w1],
                colsum(gv.astype(F32))[:, 0:w1],
                jnp.zeros((1, d - 2 * w1), F32),
            ],
            axis=1,
        )
        x = nt(o[y, 0:seg, :], w_ref[j ^ me, :, 0 : 3 * w1])
        if j == 0:
            one[...] = gr1_ref[...] + x
        else:
            one[...] += x
        out += nt(o[y, seg:keys, :], w_ref[j ^ me, :, 0 : 3 * w1])
    norm = jnp.sum(z2m_ref[...] * z2m_ref[...]) * (live_ref[0:1, 0:1] / (nmem * d * chains))
    lane = lax.broadcasted_iota(jnp.int32, (1, d), 1)
    small_ref[0:8] = sm_ref[...] + smm_ref[...]
    small_ref[6:7] = jnp.where(lane == me, norm, 0.0)
    small_ref[16:] = jnp.zeros_like(small_ref[16:])
    first = jnp.where(me == 0, 1.0, 0.0)
    each = nmem // nb
    for i in range(nb):
        small_ref[16 + 8 * i : 16 + 8 * i + each, :] = out[i * each : (i + 1) * each] * first
    ig_ref[...] = one[...].astype(BF)


def last_attention(
    me, gr1m, k, v, w, saved, gq, gk, gv, gr1, sm, smm, ubg, ubgm, z2m, live, nmem, chains, deps=()
):
    nb, d, _ = w.shape
    seg = k.shape[1]
    mp = gr1m.shape[0]
    keys = seg + mp
    w1 = HPB * HD
    qm, km, vm, pm, am, _, _, _, _, _, _ = saved
    sds = jax.ShapeDtypeStruct
    shapes = [
        sds((16 + 8 * nb, d), F32),
        sds((nb // 2, keys, 3 * w1), BF),
        sds((nb // 2, keys, 3 * w1), BF),
        sds((seg, d), BF),
    ]
    args = (me, gr1m, k, v, w, qm, km, vm, pm, am, gq, gk, gv, gr1, sm, smm, ubg, ubgm, z2m, live)
    return pl.pallas_call(
        after(functools.partial(last_attention_kernel, nmem, chains), 20, len(deps)),
        out_shape=shapes,
        in_specs=[sm_spec(), vm_spec()]
        + [any_spec()] * 2
        + [vm_spec()] * 16
        + [any_spec()] * len(deps),
        out_specs=[vm_spec()] * len(shapes),
        scratch_shapes=[
            pltpu.VMEM((nb, keys, 4 * HD), BF),
            pltpu.VMEM((nb, keys, 4 * HD), BF),
            pltpu.VMEM((seg, d), F32),
            pltpu.SemaphoreType.DMA((2,)),
        ],
        compiler_params=params(34),
        cost_estimate=pl.CostEstimate(
            flops=2 * seg * d * d * 4, bytes_accessed=30 * d * d, transcendentals=0
        ),
        name="last_attention",
    )(*args, *deps)


def turn(dst, refs):
    at = 0
    for r in refs:
        n = r.shape[0]
        dst[:, at : at + n] = r[...].astype(BF).astype(F32).T.astype(BF)
        at += n


def spread_block(y, xb, sc, n, keep0, send0, keep1, send1, rest=None):
    nz = keep0.shape[1]
    half = keep0.shape[3]
    for z in range(nz):
        for x in range(2):
            at = (2 * z + (x ^ xb)) * n
            part = sc[pl.ds(pl.multiple_of(at, 32), n), 0:half]
            (keep0, send0)[x][y, z, 0:n, :] = part
            (keep1, send1)[y][z, x, 0:n, :] = sc[(2 * z + x) * n : (2 * z + x + 1) * n, half:]
            if rest is not None:
                (keep0, send0)[x][y, z, n:, :] = rest[2 * z + (x ^ xb), :, 0:half]
                (keep1, send1)[y][z, x, n:, :] = rest[2 * z + x, :, half:]


def grad_shapes(n, d):
    sds = jax.ShapeDtypeStruct
    return [sds((2, 4, n, d // 2), BF)] * 2 + [sds((4, 2, n, d // 2), BF)] * 2


def feed_grad_kernel(
    li, ri, me_ref, l_ref, lo_ref, lm_ref, r_ref, ro_ref, rm_ref, pack_ref, keep0, send0, keep1, send1,
    lt, sc
):
    seg, d = l_ref.shape
    turn(lt, (l_ref, lo_ref, lm_ref, pack_ref.at[li]))
    mp = lm_ref.shape[0]
    a, b, c, e = seg, 2 * seg, 2 * seg + mp, 2 * seg + 2 * mp
    for y in range(2):
        acc = nn(lt[:, 0:a], r_ref[y]) + nn(lt[:, a:b], ro_ref[y])
        acc += nn(lt[:, b:c], rm_ref[2 * y]) + nn(lt[:, c:e], pack_ref[ri + y])
        sc[...] = acc.astype(BF)
        spread_block(y, me_ref[1], sc, d // 8, keep0, send0, keep1, send1)


def feed_grad(me, left, left_o, left_m, right, right_o, right_m, pack_o, li, ri, deps=()):
    seg, d = left.shape
    mp = left_m.shape[0]
    args = (me, left, left_o, left_m, right, right_o, right_m, pack_o)
    return pl.pallas_call(
        after(functools.partial(feed_grad_kernel, li, ri), 8, len(deps)),
        out_shape=grad_shapes(d // 8, d),
        in_specs=[sm_spec()] + [vm_spec()] * 7 + [any_spec()] * len(deps),
        out_specs=[vm_spec()] * 4,
        scratch_shapes=[pltpu.VMEM((d, 2 * seg + 2 * mp), BF), pltpu.VMEM((d, d), BF)],
        compiler_params=params(30),
        cost_estimate=pl.CostEstimate(
            flops=8 * seg * d * d, bytes_accessed=16 * d * d, transcendentals=0
        ),
        name="feed_grad",
    )(*args, *deps)


def attention_grad_kernel(
    me_ref, tok_ref, toko_ref, m_ref, ge_ref, go_ref, gr1_ref, gr1o_ref, gr1m_ref, a_ref, ao_ref, am_ref,
    pack_ref, s_ref, so_ref, keep0, send0, keep1, send1, lt0, lt1, sc, rest
):
    seg, d = tok_ref.shape
    mp = m_ref.shape[0]
    keys = seg + mp
    w1 = HPB * HD
    chunk = d // 8
    me = me_ref[0]
    turn(lt0, (tok_ref, m_ref, toko_ref, pack_ref.at[7]))
    turn(lt1, (gr1_ref, gr1o_ref, gr1m_ref, pack_ref.at[3]))
    vecs = s_ref[0:8] + so_ref[0:8]
    a, b, c, e = seg, 2 * seg, 2 * seg + mp, 2 * seg + 2 * mp
    for y in range(2):
        x = nn(lt0[:, 0:keys], ge_ref[y]) + nn(lt0[:, keys:], go_ref[y])
        r = nn(lt1[:, 0:a], a_ref[y]) + nn(lt1[:, a:b], ao_ref[y])
        r += nn(lt1[:, b:c], am_ref[2 * y])
        r += nn(lt1[:, c:e], pack_ref[8, :, y * 4 * HD : (y + 1) * 4 * HD])
        sc[...] = jnp.concatenate([x, r[:, 0:w1]], axis=1).astype(BF)
        j = 2 * y
        bias = s_ref[12 + j : 13 + j] + so_ref[13 + j : 14 + j]
        up = s_ref[8 + j : 9 + j] + so_ref[9 + j : 10 + j]
        second = jnp.concatenate([bias[:, w1 : 2 * w1], vecs[6:7, 0 : d - w1]], axis=1)
        at = pl.multiple_of(16 + 8 * (j ^ me), 8)
        mem = s_ref[pl.ds(at, 8), :] + so_ref[pl.ds(at, 8), :]
        for i in range(8):
            part = [vecs[t : t + 1, i * chunk : (i + 1) * chunk] for t in range(6)]
            top = jnp.concatenate(part + [bias[:, 0:w1]], axis=1)
            rest[i] = jnp.concatenate([top, second, up, mem[0:5]], axis=0).astype(BF)
        spread_block(y, me_ref[1], sc, chunk, keep0, send0, keep1, send1, rest)


def attention_grad(
    me, tok, tok_o, m, ge, go, gr1, gr1_o, gr1m, a, a_o, am, pack_o, small, small_o, deps=()
):
    seg, d = tok.shape
    mp = m.shape[0]
    args = (me, tok, tok_o, m, ge, go, gr1, gr1_o, gr1m, a, a_o, am, pack_o, small, small_o)
    return pl.pallas_call(
        after(attention_grad_kernel, 15, len(deps)),
        out_shape=grad_shapes(d // 8 + 8, d),
        in_specs=[sm_spec()] + [vm_spec()] * 14 + [any_spec()] * len(deps),
        out_specs=[vm_spec()] * 4,
        scratch_shapes=[
            pltpu.VMEM((d, 2 * seg + 2 * mp), BF),
            pltpu.VMEM((d, 2 * seg + 2 * mp), BF),
            pltpu.VMEM((d, d), BF),
            pltpu.VMEM((8, 8, d), BF),
        ],
        compiler_params=params(34),
        cost_estimate=pl.CostEstimate(
            flops=8 * seg * d * d, bytes_accessed=16 * d * d, transcendentals=0
        ),
        name="attention_grad",
    )(*args, *deps)


def plus(a, b):
    return (a.astype(F32) + b.astype(F32)).astype(BF)


def sum_xy_kernel(me_ref, keep0, recv0, keep1, recv1, ak, as_, bk, bs):
    xb = me_ref[1]
    for z in range(4):
        ak[z] = plus(keep0[0, z], recv0[0, z])
        as_[z] = plus(keep0[1, z], recv0[1, z])
        bk[z] = plus(keep1[z, xb], recv1[z, xb])
        bs[z] = plus(keep1[z, 1 - xb], recv1[z, 1 - xb])


def sum_yx_kernel(me_ref, ak, ar, bk, br, *outs):
    z = me_ref[2]
    for i, o in enumerate(outs):
        t = (z + i) % 4
        o[0] = plus(ak[t], ar[t])
        o[1] = plus(bk[t], br[t])


def sum_z(refs):
    halves = []
    for h in range(2):
        t = refs[0][h].astype(F32)
        for r in refs[1:]:
            t = t + r[h].astype(F32)
        halves.append(t)
    return jnp.concatenate(halves, axis=1)


def up_kernel(a, b, c, e, o):
    o[...] = sum_z((a, b, c, e))


def down_kernel(a, b, c, e, o):
    o[...] = sum_z((a, b, c, e)).T


def attention_kernel(a, b, c, e, q, k, v, o, rest):
    t = sum_z((a, b, c, e))
    n, w1 = q.shape
    q[...] = t[0:n, 0:w1]
    k[...] = t[0:n, w1 : 2 * w1]
    v[...] = t[0:n, 2 * w1 : 3 * w1]
    o[...] = t[0:n, 3 * w1 : 4 * w1].T
    rest[...] = t[n:]


def small_call(kernel, shapes, args, name, scalars=False, deps=()):
    return pl.pallas_call(
        after(kernel, len(args), len(deps)),
        out_shape=shapes,
        in_specs=([sm_spec()] if scalars else [])
        + [vm_spec()] * (len(args) - scalars)
        + [any_spec()] * len(deps),
        out_specs=[vm_spec()] * len(shapes),
        compiler_params=params(12),
        name=name,
    )(*args, *deps)


def pack_kernel(q_ref, k_ref, v_ref, o_ref, u_ref, d_ref, out_ref):
    n, w1 = q_ref.shape
    d = u_ref.shape[1]
    for i, r in enumerate((q_ref, k_ref, v_ref)):
        out_ref[:, i * w1 : (i + 1) * w1] = r[...]
    out_ref[:, 3 * w1 : 4 * w1] = o_ref[...].astype(F32).T.astype(BF)
    out_ref[:, d : 2 * d] = u_ref[...]
    out_ref[:, 2 * d : 3 * d] = d_ref[...].astype(F32).T.astype(BF)


def pack(*weights):
    n = weights[0].shape[0]
    d = weights[4].shape[1]
    return pl.pallas_call(
        pack_kernel,
        out_shape=jax.ShapeDtypeStruct((n, 3 * d), BF),
        in_specs=[vm_spec()] * 6,
        out_specs=vm_spec(),
        name="pack",
    )(*weights)


def flip(a, axis, bit):
    return lax.ppermute(a, axis, [(i, i ^ bit) for i in range(lax.axis_size(axis))])


def shift(a, by):
    n = lax.axis_size("dp")
    return lax.ppermute(a, "dp", [(i, (i + by) % n) for i in range(n)])


def pick(a, i, axis):
    return lax.dynamic_index_in_dim(a, i, axis, keepdims=False)


def start_xy(keep0, send0, keep1, send1):
    return keep0, flip(send0, "dp", 1), keep1, flip(send1, "mp", 2)


def middle_xy(place, parts, deps=()):
    _, nz, n, half = parts[0].shape
    shape = jax.ShapeDtypeStruct((nz, n, half), BF)
    ak, as_, bk, bs = small_call(sum_xy_kernel, [shape] * 4, (place, *parts), "sum_xy", True, deps)
    return ak, flip(as_, "mp", 2), bk, flip(bs, "dp", 1)


def start_z(place, parts, deps=()):
    _, n, half = parts[0].shape
    shape = jax.ShapeDtypeStruct((2, n, half), BF)
    own, up, far, down = small_call(sum_yx_kernel, [shape] * 4, (place, *parts), "sum_yx", True, deps)
    return own, shift(far, 4), shift(up, 2), shift(down, -2)


def exchange(x):
    me = lax.axis_index("mp")
    nb = x.shape[0]
    got = [pick(x, me, 0)]
    for i in range(1, nb):
        got.append(flip(pick(x, me ^ i, 0), "mp", i))
    return relative(jnp.stack(got))


def relative(x):
    me = lax.axis_index("mp")
    v = x.reshape((2, 2) + x.shape[1:])
    v = jnp.where(me % 2 == 1, v[:, ::-1], v)
    v = jnp.where(me // 2 == 1, v[::-1], v)
    return v.reshape(x.shape)


def gather_small(x):
    nd = lax.axis_size("dp")
    nb = lax.axis_size("mp")
    if nd != 8:
        return lax.all_gather(x, ("mp", "dp"), axis=0).reshape(nb, nd, -1)
    k = x.shape[0]
    t = x.reshape(1, k)
    me = lax.axis_index("dp")
    b = me % 2
    z = me // 2
    o = flip(t, "mp", 1)
    c = lax.axis_index("mp") % 2
    t = jnp.where(c == 0, jnp.concatenate([t, o]), jnp.concatenate([o, t]))
    o = flip(t, "mp", 2)
    y = lax.axis_index("mp") // 2
    t = jnp.where(y == 0, jnp.concatenate([t, o]), jnp.concatenate([o, t]))
    o = flip(t, "dp", 1)
    t = jnp.where(b == 0, jnp.stack([t, o]), jnp.stack([o, t]))
    up, down, far = shift(t, -2), shift(t, 2), shift(t, 4)
    ring = jnp.stack([t, up, far, down, t, up, far])
    t = lax.dynamic_slice_in_dim(ring, (4 - z) % 4, 4, 0)
    return t.reshape(nd, nb, k).transpose(1, 0, 2)


def body(
    tokens, memory_init, query_weight, query_bias, key_weight, value_weight, value_bias, out_weight,
    out_bias, first_gain, first_shift, up_weight, up_bias, down_weight, down_bias, second_gain,
    second_shift, cotangent, group_segs, chain_group
):
    nd = lax.axis_size("dp")
    nb = lax.axis_size("mp")
    me = lax.axis_index("mp")
    dp = lax.axis_index("dp")
    tuned = nd == 8
    place = [me, dp % 2, dp // 2] if tuned else [me, 0 * me, 0 * me]
    me1 = jnp.stack(place).astype(jnp.int32)
    segments = tokens.shape[1]
    d = tokens.shape[3]
    part = tokens.shape[2]
    seg = part * nb
    nmem = memory_init.shape[0] * nb
    pad = -(-nmem // 16) * 16
    both = ("mp", "dp")
    wl = pack(query_weight, key_weight, value_weight, out_weight, up_weight, down_weight)
    w = lax.all_gather(wl, both, axis=0).reshape(nb, d, 3 * d)
    vecs = (out_bias, first_gain, first_shift, down_bias, second_gain, second_shift)
    small = jnp.concatenate(
        (query_bias, value_bias, up_bias) + vecs + (memory_init.reshape(-1),)
    )
    n1 = query_bias.shape[0]
    n2 = up_bias.shape[0]
    sg = gather_small(small)
    qb = sg[:, :, 0:n1].reshape(nb, 1, -1).astype(F32)
    vb = sg[:, :, n1 : 2 * n1].reshape(nb, 1, -1).astype(F32)
    qkvb = jnp.concatenate([qb, jnp.zeros_like(qb), vb], axis=2)
    ub = sg[:, :, 2 * n1 : 2 * n1 + n2].reshape(nb, 1, -1).astype(F32)
    at = 2 * n1 + n2
    vec = sg[:, :, at : at + 6 * n1].reshape(nb, nd, 6, n1).transpose(2, 1, 0, 3).reshape(6, d)
    vec = jnp.pad(vec.astype(F32), ((0, 2), (0, 0)))
    ml = memory_init.shape[0]
    m0 = sg[:, :, at + 6 * n1 :].reshape(nb, nd, ml, -1).transpose(0, 2, 1, 3).reshape(nmem, d)
    m0 = jnp.pad(m0.astype(F32), ((0, pad - nmem), (0, 0)))
    tok = exchange(tokens[0]).reshape(seg, d)
    ct = exchange(cotangent[0]).reshape(seg, d)
    match = chain_group[:, None] == jnp.arange(group_segs.shape[0], dtype=jnp.int32)[None, :]
    count = jnp.sum(jnp.where(match, group_segs[None, :], 0))
    live = (me < count).astype(F32)
    live2 = jnp.full((8, 128), live, F32)
    q, k, v = qkv_call(me1, tok, w, qkvb)
    m = jnp.where(me == 0, m0, 0.0)
    own = m
    for s in range(segments - 1):
        (z,) = mem_forward(me1, m, k, v, w, qkvb, ub, vec, nmem, False)
        m = lax.ppermute(z, "mp", [(s, s + 1)])
        own = own + m
    (out, z1b, a0, a1, g0, g1, gf0, gf1, gr2b, gr1, gr1b, gq, gk, gv, base, sm, ubg) = token_call(
        me1, tok, ct, live2, own, q, k, v, w, qkvb, ub, vec, nmem
    )
    z2m, *saved = mem_forward(me1, own, k, v, w, qkvb, ub, vec, nmem, True, (base,))
    am, z1m, g_m = saved[4:7]
    layer_out = exchange(out.reshape(nb, part, d))
    send = base
    gin = jnp.zeros_like(base)
    for s in reversed(range(segments - 1)):
        recv = lax.ppermute(send, "mp", [(s + 1, s)])
        gin = gin + recv
        if s == 1:
            recv, layer_out = lax.optimization_barrier((recv, layer_out))
        if s > 0:
            send = mem_backward(me1, recv, k, v, w, vec, base, saved)
    other = lambda x: flip(x, "mp", 1)
    sends, _ = lax.optimization_barrier(((z1b, gf1, gr2b, g1, gr1b, a1), recv))
    z1b_o, gf_o, gr2b_o, g_o, gr1b_o, a_o = [other(x) for x in sends]
    tok_o = other(tok)
    gr2m, gfm, gr1m, smm, ubgm, extra = last_feed(me1, gin, w, vec, saved, own)
    extra_o = other(extra)
    up_g = feed_grad(me1, z1b, z1b_o, z1m, gf0, gf_o, gfm, extra_o, 4, 0)
    down_g = feed_grad(me1, gr2b, gr2b_o, gr2m, g0, g_o, g_m, extra_o, 2, 5, (up_g[0],))
    chains = nd * tokens.shape[0]
    w1 = d // nb
    chunk = d // nd
    small, ge, go, ig = last_attention(
        me1, gr1m, k, v, w, saved, gq, gk, gv, gr1, sm, smm, ubg, ubgm, z2m, live2, nmem, chains,
        (down_g[0],),
    )
    deps = ()
    if tuned:
        up_s = start_xy(*up_g)
        small, ge, go, ig, up_s = lax.optimization_barrier((small, ge, go, ig, up_s))
        up_s = middle_xy(me1, up_s)
        down_s = start_xy(*down_g)
        deps = (up_s[0],)
    att_g = attention_grad(
        me1, tok, tok_o, own, ge, other(go), gr1b, gr1b_o, gr1m, a0, a_o, am, extra_o, small,
        other(small), deps,
    )
    sds = jax.ShapeDtypeStruct
    if tuned:
        up_s, down_s, att_g, ig = lax.optimization_barrier((up_s, down_s, att_g, ig))
        up_s = start_z(me1, up_s)
        down_s = middle_xy(me1, down_s)
        att_s = start_xy(*att_g)
        up_s, down_s, att_s = lax.optimization_barrier((up_s, down_s, att_s))
        att_s = middle_xy(me1, att_s)
        down_s = start_z(me1, down_s)
        (wup,) = small_call(up_kernel, [sds((chunk, d), F32)], up_s, "up_out")
        down_s, att_s, wup, ig = lax.optimization_barrier((down_s, att_s, wup, ig))
        att_s = start_z(me1, att_s)
        input_grad = exchange(ig.reshape(nb, part, d))
        (wdn,) = small_call(down_kernel, [sds((d, chunk), F32)], down_s, "down_out")
        wq, wk, wv, wo, rest = small_call(
            attention_kernel,
            [sds((chunk, w1), F32)] * 3 + [sds((w1, chunk), F32), sds((8, d), F32)],
            att_s,
            "attention_out",
        )
        vg = lax.dynamic_slice(rest[0, 0 : 6 * chunk].reshape(6, chunk), (0, me * n1), (6, n1))
        qbg = lax.dynamic_slice(rest[0, 6 * chunk :], (dp * n1,), (n1,))
        vbg = lax.dynamic_slice(rest[1, 0:w1], (dp * n1,), (n1,))
        ubt = lax.dynamic_slice(rest[2], (dp * n2,), (n2,))
        gmi = lax.dynamic_slice(rest[3 : 3 + ml], (0, dp * chunk), (ml, chunk))
        norms = rest[1, w1 : w1 + segments]
    else:
        input_grad = exchange(ig.reshape(nb, part, d))

        def scatter(keep0, send0, keep1, send1):
            left = jnp.stack([keep0, send0], axis=2)
            right = jnp.stack([keep1, send1])
            x = jnp.concatenate([left, right], axis=4)[:, :, :, 0 : d // 8]
            x = x.reshape(2, nd, chunk, d).astype(F32)
            x = lax.psum_scatter(x, "dp", scatter_dimension=1, tiled=True)
            return (x[0] + flip(x[1], "mp", 2)).reshape(chunk, d)

        wup, wdn, watt = scatter(*up_g), scatter(*down_g).T, scatter(*att_g)
        wq, wk, wv = [watt[:, i * w1 : (i + 1) * w1] for i in range(3)]
        wo = watt[:, 3 * w1 :].T
        rows = jnp.concatenate(
            [small[0:8], relative(small[8:12]), relative(small[12:16]), small[16:]]
        )
        rows = lax.psum(rows, both)
        vg = lax.dynamic_slice(rows, (0, dp * chunk + me * n1), (6, n1))
        qbg = lax.dynamic_slice(rows, (12 + me, dp * n1), (1, n1))[0]
        vbg = lax.dynamic_slice(rows, (12 + me, w1 + dp * n1), (1, n1))[0]
        ubt = lax.dynamic_slice(rows, (8 + me, dp * n2), (1, n2))[0]
        gmi = lax.dynamic_slice(rows, (16 + 8 * me, dp * chunk), (ml, chunk))
        norms = rows[6, 0:segments]
    return (
        layer_out[None],
        input_grad[None],
        gmi,
        wq,
        qbg,
        wk,
        wv,
        vbg,
        wo,
        vg[0],
        vg[1],
        vg[2],
        wup,
        ubt,
        wdn,
        vg[3],
        vg[4],
        vg[5],
        norms,
    )


def solution(mesh):
    rows = P("dp", None, "mp", None)
    md, dm = P(("mp", "dp")), P(("dp", "mp"))
    win, wout = P("dp", "mp"), P("mp", "dp")
    in_specs = (
        rows, wout, win, md, win, win, md, wout, dm, dm, dm, win, md, wout, dm, dm, dm, rows, P(),
        P("dp"),
    )
    out_specs = (
        rows, rows, wout, win, md, win, win, md, wout, dm, dm, dm, win, md, wout, dm, dm, dm, P(),
    )
    return jax.shard_map(body, mesh=mesh, in_specs=in_specs, out_specs=out_specs, check_vma=False)
```

```python
import functools

import jax
import jax.numpy as jnp
from jax import lax
from jax.experimental import pallas as pl
from jax.experimental.pallas import tpu as pltpu
from jax.sharding import PartitionSpec as P

HD = 64
HPB = 3
BF = jnp.bfloat16
F32 = jnp.float32
MIB = 1024 * 1024
NEG = -1e30


def nn(a, b):
    return lax.dot_general(a, b, (((1,), (0,)), ((), ())), preferred_element_type=F32)


def nt(a, b):
    return lax.dot_general(a, b, (((1,), (1,)), ((), ())), preferred_element_type=F32)


def norm_stats(r):
    mean = jnp.mean(r, axis=-1, keepdims=True)
    c = r - mean
    inv = lax.rsqrt(jnp.mean(c * c, axis=-1, keepdims=True) + 1e-05)
    return c * inv, inv


def norm_back(g, xh, inv):
    return inv * (
        g - jnp.mean(g, axis=-1, keepdims=True) - xh * jnp.mean(g * xh, axis=-1, keepdims=True)
    )


def gelu_both(f):
    cdf = 0.5 + 0.5 * lax.erf(f * (0.5**0.5))
    pdf = jnp.exp(-0.5 * f * f) * ((2.0 * jnp.pi) ** -0.5)
    return f * cdf, cdf + f * pdf


def rows_mask(shape, count):
    return lax.broadcasted_iota(jnp.int32, shape, 0) < count


def any_spec():
    return pl.BlockSpec(memory_space=pl.ANY)


def vm_spec():
    return pl.BlockSpec(memory_space=pltpu.VMEM)


def params(mib):
    return pltpu.CompilerParams(vmem_limit_bytes=mib * MIB)


def sm_spec():
    return pl.BlockSpec(memory_space=pltpu.SMEM)


def after(kernel, n_in, n_dep):
    def run(*refs):
        kernel(*refs[:n_in], *refs[n_in + n_dep :])

    return run


def split_qkv(acc):
    w1 = HPB * HD
    zero = jnp.zeros((acc.shape[0], HD), BF)
    q = jnp.concatenate([(acc[:, 0:w1].astype(BF) * 0.125).astype(BF), zero], axis=1)
    k = jnp.concatenate([acc[:, w1 : 2 * w1].astype(BF), zero], axis=1)
    v = jnp.concatenate([acc[:, 2 * w1 : 3 * w1].astype(BF), zero], axis=1)
    return q, k, v


def head_cols(shape, i):
    c = lax.broadcasted_iota(jnp.int32, shape, len(shape) - 1)
    return (c >= i * HD) & (c < (i + 1) * HD)


def spread(x):
    return jnp.concatenate(
        [jnp.where(head_cols(x.shape, i), x, jnp.zeros_like(x)) for i in range(HPB)], axis=0
    )


def gather_heads(x):
    n = x.shape[0] // HPB
    out = jnp.zeros((n, x.shape[1]), x.dtype)
    for i in range(HPB):
        out = jnp.where(head_cols(out.shape, i), x[i * n : (i + 1) * n], out)
    return out


def out_cols(a):
    return jnp.concatenate([jnp.zeros((a.shape[0], HD), a.dtype), a[:, 0 : HPB * HD]], axis=1)


def qkv_kernel(me_ref, tok_ref, w_ref, qkvb_ref, q_ref, k_ref, v_ref):
    nb, d, _ = w_ref.shape
    me = me_ref[0]
    for j in range(nb):
        acc = nn(tok_ref[...], w_ref[j ^ me, :, 0 : 3 * HPB * HD]) + qkvb_ref[j ^ me]
        q, k, v = split_qkv(acc)
        q_ref[j] = q
        k_ref[j] = k
        v_ref[j] = v


def qkv_call(me, tok, w, qkvb):
    nb, d, _ = w.shape
    s = tok.shape[0]
    return pl.pallas_call(
        qkv_kernel,
        out_shape=[jax.ShapeDtypeStruct((nb, s, 4 * HD), BF)] * 3,
        in_specs=[sm_spec(), vm_spec(), vm_spec(), vm_spec()],
        out_specs=[vm_spec()] * 3,
        compiler_params=params(20),
        cost_estimate=pl.CostEstimate(
            flops=2 * s * d * 3 * d, bytes_accessed=8 * d * d, transcendentals=0
        ),
        name="qkv",
    )(me, tok, w, qkvb)


def mem_forward_kernel(
    nmem, step, me_ref, m_ref, k_hbm, v_hbm, w_ref, qkvb_ref, ub_ref, vec_ref, *rest
):
    save = step is not None
    old = ()
    if save and step > 0:
        old, rest = rest[:11], rest[11:]
    kept = rest[1:12]
    if save:
        (
            z2_ref, qm_ref, km_ref, vm_ref, pm_ref, am_ref, z1b_ref, g_ref, gp_ref, xh1_ref,
            xh2_ref, inv_ref,
        ) = rest[:12]
        rest = rest[12:]
    else:
        z2_ref = rest[0]
        rest = rest[1:]
    kk, vv, sc, sem2 = rest
    nb, d, _ = w_ref.shape
    seg = k_hbm.shape[1]
    mp = m_ref.shape[0]
    keys = seg + mp
    w1 = HPB * HD
    me = me_ref[0]
    kc = pltpu.make_async_copy(k_hbm, kk.at[:, 0:seg, :], sem2.at[0])
    vc = pltpu.make_async_copy(v_hbm, vv.at[:, 0:seg, :], sem2.at[1])
    kc.start()
    vc.start()
    mem = m_ref[...]
    mb = mem.astype(BF)
    qs = []
    for j in range(nb):
        acc = nn(mb, w_ref[j ^ me, :, 0 : 3 * w1]) + qkvb_ref[j ^ me]
        q, k, v = split_qkv(acc)
        qs.append(q)
        kk[j, seg:keys, :] = k
        vv[j, seg:keys, :] = v
        if save:
            qm_ref[j] = q
            km_ref[j] = k
            vm_ref[j] = v
    kc.wait()
    vc.wait()
    n = HPB * mp
    for j in range(nb):
        sc[j * n : (j + 1) * n, :] = nt(spread(qs[j]), kk[j])
    keep = lax.broadcasted_iota(jnp.int32, (n, keys), 1) < seg + nmem
    heads = []
    for j in range(nb):
        s = jnp.where(keep, sc[j * n : (j + 1) * n, :], NEG)
        e = jnp.exp(s - jnp.max(s, axis=-1, keepdims=True))
        p = (e / jnp.sum(e, axis=-1, keepdims=True)).astype(BF)
        if save:
            pm_ref[j] = p
        heads.append(p)
    out = jnp.zeros((mp, d), F32)
    for j in range(nb):
        a = gather_heads(nn(heads[j], vv[j])).astype(BF)
        if save:
            am_ref[j] = a
        out += nt(out_cols(a), w_ref[j ^ me, :, d - 4 * HD : d])
    xh1, inv1 = norm_stats(mem + out + vec_ref[0:1])
    z1 = xh1 * vec_ref[1:2] + vec_ref[2:3]
    z1b = z1.astype(BF)
    y = jnp.zeros((mp, d), F32)
    for j in range(nb):
        f = nn(z1b, w_ref[j ^ me, :, d : 2 * d]) + ub_ref[j ^ me]
        g, gp = gelu_both(f)
        g = g.astype(BF)
        if save:
            g_ref[j] = g
            gp_ref[j] = gp
        y += nt(g, w_ref[j ^ me, :, 2 * d : 3 * d])
    xh2, inv2 = norm_stats(z1 + y + vec_ref[3:4])
    z2 = xh2 * vec_ref[4:5] + vec_ref[5:6]
    z2_ref[...] = jnp.where(rows_mask((mp, d), nmem), z2, 0.0)
    if save:
        z1b_ref[...] = z1b
        xh1_ref[...] = xh1
        xh2_ref[...] = xh2
        inv_ref[:, 0:128] = jnp.broadcast_to(inv1, (mp, 128))
        inv_ref[:, 128:256] = jnp.broadcast_to(inv2, (mp, 128))
    if old:

        @pl.when(me != step)
        def _():
            for o, x in zip(kept, old):
                o[...] = x[...]


def mem_forward(me, m, k, v, w, qkvb, ub, vec, nmem, step=None, old=(), deps=()):
    save = step is not None
    nb, d, _ = w.shape
    seg = k.shape[1]
    mp = m.shape[0]
    keys = seg + mp
    sds = jax.ShapeDtypeStruct
    shapes = [sds((mp, d), F32)]
    if save:
        shapes += [sds((nb, mp, 4 * HD), BF)] * 3
        shapes += [
            sds((nb, HPB * mp, keys), BF),
            sds((nb, mp, 4 * HD), BF),
            sds((mp, d), BF),
            sds((nb, mp, d), BF),
            sds((nb, mp, d), F32),
            sds((mp, d), F32),
            sds((mp, d), F32),
            sds((mp, 256), F32),
        ]
    return pl.pallas_call(
        after(functools.partial(mem_forward_kernel, nmem, step), 8 + len(old), len(deps)),
        out_shape=shapes,
        in_specs=[sm_spec(), vm_spec()]
        + [any_spec()] * 2
        + [vm_spec()] * (4 + len(old))
        + [any_spec()] * len(deps),
        out_specs=[vm_spec()] * len(shapes),
        scratch_shapes=[
            pltpu.VMEM((nb, keys, 4 * HD), BF),
            pltpu.VMEM((nb, keys, 4 * HD), BF),
            pltpu.VMEM((nb * HPB * mp, keys), F32),
            pltpu.SemaphoreType.DMA((2,)),
        ],
        compiler_params=params(27),
        cost_estimate=pl.CostEstimate(
            flops=2 * mp * d * d * 12, bytes_accessed=24 * d * d, transcendentals=0
        ),
        name="mem_forward_save" if save else "mem_forward",
    )(me, m, k, v, w, qkvb, ub, vec, *old, *deps)


def colsum(x):
    return jnp.sum(x, axis=0, keepdims=True)


CH = 64


def token_kernel(
    nmem,
    me_ref,
    tok_ref,
    ct_ref,
    live_ref,
    m_ref,
    qq,
    k_hbm,
    v_hbm,
    w_ref,
    qkvb_ref,
    ub_ref,
    vec_ref,
    out_ref,
    z1b_ref,
    a0_ref,
    a1_ref,
    g0_ref,
    g1_ref,
    gf0_ref,
    gf1_ref,
    gr2b_ref,
    gr1_ref,
    g1b,
    gq_ref,
    gk_ref,
    gv_ref,
    base_ref,
    small_ref,
    ubg_ref,
    kk,
    vv,
    probs,
    big,
    one,
    inv,
    sem2,
):
    nb, d, _ = w_ref.shape
    seg = tok_ref.shape[0]
    mp = m_ref.shape[0]
    keys = seg + mp
    w1 = HPB * HD
    steps = seg // CH
    me = me_ref[0]
    loads = [
        pltpu.make_async_copy(k_hbm, kk.at[:, 0:seg, :], sem2.at[1]),
        pltpu.make_async_copy(v_hbm, vv.at[:, 0:seg, :], sem2.at[2]),
    ]
    for c in loads:
        c.start()
    mb = m_ref[...].astype(BF)
    for j in range(nb):
        _, k, v = split_qkv(nn(mb, w_ref[j ^ me, :, 0 : 3 * w1]) + qkvb_ref[j ^ me])
        kk[j, seg:keys, :] = k
        vv[j, seg:keys, :] = v
    for c in loads:
        c.wait()
    one[...] = jnp.zeros_like(one)
    tail = seg + (nmem // 8) * 8

    a_refs = (a0_ref, a1_ref)
    g_refs = (g0_ref, g1_ref)
    gf_refs = (gf0_ref, gf1_ref)

    def attend_one(j, y, c):
        vt = vv[j].astype(F32).T.astype(BF)
        parts = []
        for i in range(HPB):
            cols = slice(i * HD, (i + 1) * HD)
            big[0:keys, 0:seg] = nt(kk[j, :, cols], qq[j, :, cols])
            big[tail:keys, 0:seg] = jnp.where(
                rows_mask((keys - tail, seg), seg + nmem - tail), big[tail:keys, 0:seg], NEG
            )
            for t in range(seg // 128):
                cols = slice(t * 128, (t + 1) * 128)
                s = big[0:keys, cols]
                e = jnp.exp(s - jnp.max(s, axis=0, keepdims=True))
                p = e * (1.0 / jnp.sum(e, axis=0, keepdims=True))
                probs[j * HPB + i, :, cols] = p.astype(BF)
            parts.append(nn(vt[i * HD : (i + 1) * HD], probs[j * HPB + i]))
        parts.append(jnp.zeros((HD, seg), F32))
        a = jnp.concatenate(parts, axis=0).T.astype(BF)
        a_refs[c][y] = a
        one[...] += nt(out_cols(a), w_ref[j ^ me, :, d - 4 * HD : d])

    def attend(y, _):
        for c in range(2):
            attend_one(2 * y + c, y, c)
        return 0

    for y in range(nb // 2):
        attend(y, 0)

    for c in range(steps):
        rows = slice(c * CH, (c + 1) * CH)
        r = tok_ref[rows, :].astype(F32) + one[rows, :] + vec_ref[0:1]
        x, v = norm_stats(r)
        gr1_ref[rows, :] = x
        inv[rows, 0:128] = jnp.broadcast_to(v, (CH, 128))
        z1 = x * vec_ref[1:2] + vec_ref[2:3]
        z1b_ref[rows, :] = z1.astype(BF)
        one[rows, :] = z1 + vec_ref[3:4]

    def feed_one(j, y, c):
        big[0:seg, 0:d] = nn(z1b_ref[...], w_ref[j ^ me, :, d : 2 * d])

        for r in range(seg // 32):
            rows = slice(r * 32, (r + 1) * 32)
            g, p = gelu_both(big[rows, 0:d] + ub_ref[j ^ me])
            g_refs[c][y, rows, :] = g.astype(BF)
            gf_refs[c][y, rows, :] = p.astype(BF)
        one[...] += nt(g_refs[c][y], w_ref[j ^ me, :, 2 * d : 3 * d])

    def feed(y, _):
        for c in range(2):
            feed_one(2 * y + c, y, c)
        return 0

    for y in range(nb // 2):
        feed(y, 0)
    zero = jnp.zeros((1, d), F32)

    sg, ss, sb = zero, zero, zero
    for c in range(steps):
        rows = slice(c * CH, (c + 1) * CH)
        x, v = norm_stats(one[rows, :])
        out_ref[rows, :] = ((x * vec_ref[4:5] + vec_ref[5:6]) * live_ref[0:1, 0:1]).astype(BF)
        gz = ct_ref[rows, :].astype(F32) * live_ref[0:1, 0:1]
        gr = norm_back(gz * vec_ref[4:5], x, v)
        one[rows, :] = gr
        gr2b_ref[rows, :] = gr.astype(BF)
        sg, ss, sb = sg + colsum(gz * x), ss + colsum(gz), sb + colsum(gr)
    small_ref[3:4] = sb
    small_ref[4:5] = sg
    small_ref[5:6] = ss

    def feed_back_one(j, y, c):
        big[0:seg, 0:d] = nn(gr2b_ref[...], w_ref[j ^ me, :, 2 * d : 3 * d])

        total = zero
        for r in range(seg // 64):
            rows = slice(r * 64, (r + 1) * 64)
            gf = (big[rows, 0:d] * gf_refs[c][y, rows, :].astype(F32)).astype(BF)
            gf_refs[c][y, rows, :] = gf
            total = total + colsum(gf.astype(F32))
        ubg_ref[j] = total
        one[...] += nt(gf_refs[c][y], w_ref[j ^ me, :, d : 2 * d])

    def feed_back(y, _):
        for c in range(2):
            feed_back_one(2 * y + c, y, c)
        return 0

    for y in range(nb // 2):
        feed_back(y, 0)

    sg, ss, sb = zero, zero, zero
    for c in range(steps):
        rows = slice(c * CH, (c + 1) * CH)
        gz = one[rows, :]
        x = gr1_ref[rows, :]
        gr = norm_back(gz * vec_ref[1:2], x, inv[rows, 0:1])
        gr1_ref[rows, :] = gr
        g1b[rows, :] = gr.astype(BF)
        sg, ss, sb = sg + colsum(gz * x), ss + colsum(gz), sb + colsum(gr)
    small_ref[0:1] = sb
    small_ref[1:2] = sg
    small_ref[2:3] = ss
    small_ref[6:8] = jnp.zeros((2, d), F32)

    def attend_back_one(j, y, c, base):
        ga = nn(g1b[...], w_ref[j ^ me, :, d - 4 * HD : d])[:, HD:]
        gab = ga.astype(BF)
        delta = (gab.astype(F32) * a_refs[c][y, :, 0:w1].astype(F32)).T
        kt = kk[j].astype(F32).T.astype(BF)
        gqs = []
        gks = []
        gvs = []
        for i in range(HPB):
            cols = slice(i * HD, (i + 1) * HD)
            g = gab[:, cols]
            p = probs[j * HPB + i]
            dl = jnp.sum(delta[cols], axis=0, keepdims=True)
            gvs.append(nn(p, g))
            gs = (p.astype(F32) * (nt(vv[j, :, cols], g) - dl)).astype(BF)
            gks.append(nn(gs, qq[j, :, cols]))
            gqs.append(nn(kt[cols], gs))
        zq = jnp.zeros((HD, seg), F32)
        zk = jnp.zeros((keys, HD), F32)
        gq_ref[j] = (jnp.concatenate(gqs + [zq], axis=0).T * 0.125).astype(BF)
        gk = jnp.concatenate(gks + [zk], axis=1)
        gv = jnp.concatenate(gvs + [zk], axis=1)
        gk_ref[j] = gk.astype(BF)
        gv_ref[j] = gv.astype(BF)
        gm = jnp.concatenate(
            [jnp.zeros((mp, w1), F32), gk[seg:keys, 0:w1], gv[seg:keys, 0:w1]], axis=1
        ).astype(BF)
        return base + nt(gm, w_ref[j ^ me, :, 0 : 3 * w1])

    def attend_back(y, base):
        for c in range(2):
            base = attend_back_one(2 * y + c, y, c, base)
        return base

    total = jnp.zeros((mp, d), F32)
    for y in range(nb // 2):
        total = attend_back(y, total)
    base_ref[...] = total


def token_call(me, tok, ct, live, m, q, k, v, w, qkvb, ub, vec, nmem):
    nb, d, _ = w.shape
    seg = tok.shape[0]
    mp = m.shape[0]
    keys = seg + mp
    sds = jax.ShapeDtypeStruct
    shapes = [
        sds((seg, d), BF),
        sds((seg, d), BF),
        sds((nb // 2, seg, 4 * HD), BF),
        sds((nb // 2, seg, 4 * HD), BF),
        sds((nb // 2, seg, d), BF),
        sds((nb // 2, seg, d), BF),
        sds((nb // 2, seg, d), BF),
        sds((nb // 2, seg, d), BF),
        sds((seg, d), BF),
        sds((seg, d), F32),
        sds((seg, d), BF),
        sds((nb, seg, 4 * HD), BF),
        sds((nb, keys, 4 * HD), BF),
        sds((nb, keys, 4 * HD), BF),
        sds((mp, d), F32),
        sds((8, d), F32),
        sds((nb, 1, d), F32),
    ]
    return pl.pallas_call(
        functools.partial(token_kernel, nmem),
        out_shape=shapes,
        in_specs=[sm_spec()] + [vm_spec()] * 5 + [any_spec()] * 2 + [vm_spec()] * 4,
        out_specs=[vm_spec()] * len(shapes),
        scratch_shapes=[
            pltpu.VMEM((nb, keys, 4 * HD), BF),
            pltpu.VMEM((nb, keys, 4 * HD), BF),
            pltpu.VMEM((nb * HPB, keys, seg), BF),
            pltpu.VMEM((keys, d), F32),
            pltpu.VMEM((seg, d), F32),
            pltpu.VMEM((seg, 128), F32),
            pltpu.SemaphoreType.DMA((3,)),
        ],
        compiler_params=params(43),
        cost_estimate=pl.CostEstimate(
            flops=5 * seg * d * d * 12, bytes_accessed=60 * d * d, transcendentals=0
        ),
        name="token_rows",
    )(me, tok, ct, live, m, q, k, v, w, qkvb, ub, vec)


def back_feed(w_ref, me, nb, d, gz, vec_ref, gp_ref, xh1, xh2, inv_ref, gf_ref=None, ubg_ref=None):
    gr2 = norm_back(gz * vec_ref[4:5], xh2, inv_ref[:, 128:129])
    gr2b = gr2.astype(BF)
    acc = gr2
    for j in range(nb):
        gf = (nn(gr2b, w_ref[j ^ me, :, 2 * d : 3 * d]) * gp_ref[j]).astype(BF)
        if gf_ref is not None:
            gf_ref[j] = gf
            ubg_ref[j] = colsum(gf.astype(F32))
        acc += nt(gf, w_ref[j ^ me, :, d : 2 * d])
    return gr2, acc, norm_back(acc * vec_ref[1:2], xh1, inv_ref[:, 0:1])


def back_scores(j, gab, am_ref, pm_ref, vv, delta_rows):
    n = HPB * delta_rows
    gs3 = spread(gab)
    a3 = jnp.concatenate([am_ref[j]] * HPB, axis=0)
    dl = jnp.sum(gs3.astype(F32) * a3.astype(F32), axis=1, keepdims=True)
    p = pm_ref[j].astype(F32)
    return gs3, p, (p * (nt(gs3, vv[j]) - dl)).astype(BF)


def mem_backward_kernel(
    nmem, me_ref, g_ref, k_hbm, v_hbm, w_ref, vec_ref, base_ref, qm_ref, km_ref, vm_ref, pm_ref,
    am_ref, gp_ref, xh1_ref, xh2_ref, inv_ref, gm_ref, kk, vv, sem2
):
    nb, d, _ = w_ref.shape
    seg = k_hbm.shape[1]
    mp = g_ref.shape[0]
    keys = seg + mp
    w1 = HPB * HD
    me = me_ref[0]
    kc = pltpu.make_async_copy(k_hbm, kk.at[:, 0:seg, :], sem2.at[0])
    vc = pltpu.make_async_copy(v_hbm, vv.at[:, 0:seg, :], sem2.at[1])
    kc.start()
    vc.start()
    kk[:, seg:keys, :] = km_ref[...]
    vv[:, seg:keys, :] = vm_ref[...]
    _, _, gr1 = back_feed(
        w_ref, me, nb, d, g_ref[...], vec_ref, gp_ref, xh1_ref[...], xh2_ref[...], inv_ref
    )
    gr1b = gr1.astype(BF)
    kc.wait()
    vc.wait()
    gabs = []
    for j in range(nb):
        ga = nn(gr1b, w_ref[j ^ me, :, d - 4 * HD : d]).astype(BF)
        gabs.append(jnp.concatenate([ga[:, HD:], jnp.zeros((mp, HD), BF)], axis=1))
    scores = [back_scores(j, gabs[j], am_ref, pm_ref, vv, mp) for j in range(nb)]
    out = gr1 + base_ref[...]
    for j in range(nb):
        gs3, p, gs = scores[j]
        gq = gather_heads(nn(gs, kk[j])) * 0.125
        gk = nn(gs[:, seg:keys].astype(F32).T.astype(BF), spread(qm_ref[j]))
        gv = nn(p[:, seg:keys].T.astype(BF), gs3)
        gm = jnp.concatenate([gq[:, 0:w1], gk[:, 0:w1], gv[:, 0:w1]], axis=1).astype(BF)
        out += nt(gm, w_ref[j ^ me, :, 0 : 3 * w1])
    gm_ref[...] = out


def mem_backward(me, g, k, v, w, vec, base, saved):
    nb, d, _ = w.shape
    seg = k.shape[1]
    mp = g.shape[0]
    keys = seg + mp
    qm, km, vm, pm, am, _, _, gp, xh1, xh2, inv = saved
    args = (me, g, k, v, w, vec, base, qm, km, vm, pm, am, gp, xh1, xh2, inv)
    return pl.pallas_call(
        functools.partial(mem_backward_kernel, 0),
        out_shape=jax.ShapeDtypeStruct((mp, d), F32),
        in_specs=[sm_spec(), vm_spec()] + [any_spec()] * 2 + [vm_spec()] * 12,
        out_specs=vm_spec(),
        scratch_shapes=[
            pltpu.VMEM((nb, keys, 4 * HD), BF),
            pltpu.VMEM((nb, keys, 4 * HD), BF),
            pltpu.SemaphoreType.DMA((2,)),
        ],
        compiler_params=params(24),
        cost_estimate=pl.CostEstimate(
            flops=2 * mp * d * d * 12, bytes_accessed=24 * d * d, transcendentals=0
        ),
        name="mem_backward",
    )(*args)


def last_feed_kernel(
    me_ref, g_ref, w_ref, vec_ref, gp_ref, xh1_ref, xh2_ref, inv_ref, z1m_ref, gm_ref, m_ref, am_ref,
    gr2b_ref, gf_ref, gr1_ref, small_ref, ubg_ref, pack_ref
):
    nb, d, _ = w_ref.shape
    me = me_ref[0]
    gz = g_ref[...]
    xh1 = xh1_ref[...]
    xh2 = xh2_ref[...]
    gr2, gz1, gr1 = back_feed(
        w_ref, me, nb, d, gz, vec_ref, gp_ref, xh1, xh2, inv_ref, gf_ref, ubg_ref
    )
    gr2b_ref[...] = gr2.astype(BF)
    gr1_ref[...] = gr1
    mp, _ = gz.shape
    for y in range(nb // 2):
        pack_ref[y] = gf_ref[2 * y + 1]
        pack_ref[5 + y] = gm_ref[2 * y + 1]
        pack_ref[8, :, y * 4 * HD : (y + 1) * 4 * HD] = am_ref[2 * y + 1]
    pack_ref[8, :, 8 * HD : d] = jnp.zeros((mp, d - 8 * HD), BF)
    pack_ref[2] = gr2.astype(BF)
    pack_ref[3] = gr1.astype(BF)
    pack_ref[4] = z1m_ref[...]
    pack_ref[7] = m_ref[...].astype(BF)
    small_ref[0:1] = colsum(gr1)
    small_ref[1:2] = colsum(gz1 * xh1)
    small_ref[2:3] = colsum(gz1)
    small_ref[3:4] = colsum(gr2)
    small_ref[4:5] = colsum(gz * xh2)
    small_ref[5:6] = colsum(gz)
    small_ref[6:8] = jnp.zeros((2, d), F32)


def last_feed(me, g, w, vec, saved, m, deps=()):
    nb, d, _ = w.shape
    mp = g.shape[0]
    _, _, _, _, am, z1m, gm, gp, xh1, xh2, inv = saved
    sds = jax.ShapeDtypeStruct
    shapes = [
        sds((mp, d), BF),
        sds((nb, mp, d), BF),
        sds((mp, d), F32),
        sds((8, d), F32),
        sds((nb, 1, d), F32),
        sds((9, mp, d), BF),
    ]
    return pl.pallas_call(
        after(last_feed_kernel, 12, len(deps)),
        out_shape=shapes,
        in_specs=[sm_spec()] + [vm_spec()] * 11 + [any_spec()] * len(deps),
        out_specs=[vm_spec()] * len(shapes),
        compiler_params=params(20),
        cost_estimate=pl.CostEstimate(
            flops=2 * mp * d * d * 8, bytes_accessed=16 * d * d, transcendentals=0
        ),
        name="last_feed",
    )(me, g, w, vec, gp, xh1, xh2, inv, z1m, gm, m, am, *deps)


def last_attention_kernel(
    nmem, chains, me_ref, gr1m_ref, k_hbm, v_hbm, w_ref, qm_ref, km_ref, vm_ref, pm_ref, am_ref, gq_ref, gk_ref,
    gv_ref, gr1_ref, sm_ref, smm_ref, ubg_ref, ubgm_ref, z2m_ref, live_ref, small_ref, ge_ref, go_ref,
    ig_ref, kk, vv, one, sem2
):
    nb, d, _ = w_ref.shape
    seg = k_hbm.shape[1]
    mp = gr1m_ref.shape[0]
    keys = seg + mp
    w1 = HPB * HD
    me = me_ref[0]
    kc = pltpu.make_async_copy(k_hbm, kk.at[:, 0:seg, :], sem2.at[0])
    vc = pltpu.make_async_copy(v_hbm, vv.at[:, 0:seg, :], sem2.at[1])
    kc.start()
    vc.start()
    kk[:, seg:keys, :] = km_ref[...]
    vv[:, seg:keys, :] = vm_ref[...]
    gr1 = gr1m_ref[...]
    gr1b = gr1.astype(BF)
    kc.wait()
    vc.wait()
    gabs = []
    for j in range(nb):
        ga = nn(gr1b, w_ref[j ^ me, :, d - 4 * HD : d]).astype(BF)
        gabs.append(jnp.concatenate([ga[:, HD:], jnp.zeros((mp, HD), BF)], axis=1))
    scores = [back_scores(j, gabs[j], am_ref, pm_ref, vv, mp) for j in range(nb)]
    out = gr1
    for j in range(nb):
        gs3, p, gs = scores[j]
        gq = (gather_heads(nn(gs, kk[j])) * 0.125).astype(BF)
        gk = (gk_ref[j] + nn(gs.astype(F32).T.astype(BF), spread(qm_ref[j]))).astype(BF)
        gv = (gv_ref[j] + nn(p.T.astype(BF), gs3)).astype(BF)
        gqt = gq_ref[j]
        o = (ge_ref, go_ref)[j % 2]
        y = j // 2
        o[y, 0:seg, 0:w1] = gqt[:, 0:w1]
        o[y, seg:keys, 0:w1] = gq[:, 0:w1]
        o[y, :, w1 : 2 * w1] = gk[:, 0:w1]
        o[y, :, 2 * w1 : 3 * w1] = gv[:, 0:w1]
        small_ref[8 + j : 9 + j] = ubg_ref[j] + ubgm_ref[j]
        small_ref[12 + j : 13 + j] = jnp.concatenate(
            [
                (colsum(gqt.astype(F32)) + colsum(gq.astype(F32)))[:, 0:w1],
                colsum(gv.astype(F32))[:, 0:w1],
                jnp.zeros((1, d - 2 * w1), F32),
            ],
            axis=1,
        )
        x = nt(o[y, 0:seg, :], w_ref[j ^ me, :, 0 : 3 * w1])
        if j == 0:
            one[...] = gr1_ref[...] + x
        else:
            one[...] += x
        out += nt(o[y, seg:keys, :], w_ref[j ^ me, :, 0 : 3 * w1])
    norm = jnp.sum(z2m_ref[...] * z2m_ref[...]) * (live_ref[0:1, 0:1] / (nmem * d * chains))
    lane = lax.broadcasted_iota(jnp.int32, (1, d), 1)
    small_ref[0:8] = sm_ref[...] + smm_ref[...]
    small_ref[6:7] = jnp.where(lane == me, norm, 0.0)
    small_ref[16:] = jnp.zeros_like(small_ref[16:])
    first = jnp.where(me == 0, 1.0, 0.0)
    each = nmem // nb
    for i in range(nb):
        small_ref[16 + 8 * i : 16 + 8 * i + each, :] = out[i * each : (i + 1) * each] * first
    ig_ref[...] = one[...].astype(BF)


def last_attention(
    me, gr1m, k, v, w, saved, gq, gk, gv, gr1, sm, smm, ubg, ubgm, z2m, live, nmem, chains, deps=()
):
    nb, d, _ = w.shape
    seg = k.shape[1]
    mp = gr1m.shape[0]
    keys = seg + mp
    w1 = HPB * HD
    qm, km, vm, pm, am, _, _, _, _, _, _ = saved
    sds = jax.ShapeDtypeStruct
    shapes = [
        sds((16 + 8 * nb, d), F32),
        sds((nb // 2, keys, 3 * w1), BF),
        sds((nb // 2, keys, 3 * w1), BF),
        sds((seg, d), BF),
    ]
    args = (me, gr1m, k, v, w, qm, km, vm, pm, am, gq, gk, gv, gr1, sm, smm, ubg, ubgm, z2m, live)
    return pl.pallas_call(
        after(functools.partial(last_attention_kernel, nmem, chains), 20, len(deps)),
        out_shape=shapes,
        in_specs=[sm_spec(), vm_spec()]
        + [any_spec()] * 2
        + [vm_spec()] * 16
        + [any_spec()] * len(deps),
        out_specs=[vm_spec()] * len(shapes),
        scratch_shapes=[
            pltpu.VMEM((nb, keys, 4 * HD), BF),
            pltpu.VMEM((nb, keys, 4 * HD), BF),
            pltpu.VMEM((seg, d), F32),
            pltpu.SemaphoreType.DMA((2,)),
        ],
        compiler_params=params(34),
        cost_estimate=pl.CostEstimate(
            flops=2 * seg * d * d * 4, bytes_accessed=30 * d * d, transcendentals=0
        ),
        name="last_attention",
    )(*args, *deps)


def turn(dst, refs):
    at = 0
    for r in refs:
        n = r.shape[0]
        dst[:, at : at + n] = r[...].astype(BF).astype(F32).T.astype(BF)
        at += n


def spread_block(y, xb, sc, n, keep0, send0, keep1, send1, rest=None):
    nz = keep0.shape[1]
    half = keep0.shape[3]
    for z in range(nz):
        for x in range(2):
            at = (2 * z + (x ^ xb)) * n
            part = sc[pl.ds(pl.multiple_of(at, 32), n), 0:half]
            (keep0, send0)[x][y, z, 0:n, :] = part
            (keep1, send1)[y][z, x, 0:n, :] = sc[(2 * z + x) * n : (2 * z + x + 1) * n, half:]
            if rest is not None:
                (keep0, send0)[x][y, z, n:, :] = rest[2 * z + (x ^ xb), :, 0:half]
                (keep1, send1)[y][z, x, n:, :] = rest[2 * z + x, :, half:]


def grad_shapes(n, d):
    sds = jax.ShapeDtypeStruct
    return [sds((2, 4, n, d // 2), BF)] * 2 + [sds((4, 2, n, d // 2), BF)] * 2


def feed_grad_kernel(
    li, ri, me_ref, l_ref, lo_ref, lm_ref, r_ref, ro_ref, rm_ref, pack_ref, keep0, send0, keep1, send1,
    lt, sc
):
    seg, d = l_ref.shape
    turn(lt, (l_ref, lo_ref, lm_ref, pack_ref.at[li]))
    mp = lm_ref.shape[0]
    a, b, c, e = seg, 2 * seg, 2 * seg + mp, 2 * seg + 2 * mp
    for y in range(2):
        acc = nn(lt[:, 0:a], r_ref[y]) + nn(lt[:, a:b], ro_ref[y])
        acc += nn(lt[:, b:c], rm_ref[2 * y]) + nn(lt[:, c:e], pack_ref[ri + y])
        sc[...] = acc.astype(BF)
        spread_block(y, me_ref[1], sc, d // 8, keep0, send0, keep1, send1)


def feed_grad(me, left, left_o, left_m, right, right_o, right_m, pack_o, li, ri, deps=()):
    seg, d = left.shape
    mp = left_m.shape[0]
    args = (me, left, left_o, left_m, right, right_o, right_m, pack_o)
    return pl.pallas_call(
        after(functools.partial(feed_grad_kernel, li, ri), 8, len(deps)),
        out_shape=grad_shapes(d // 8, d),
        in_specs=[sm_spec()] + [vm_spec()] * 7 + [any_spec()] * len(deps),
        out_specs=[vm_spec()] * 4,
        scratch_shapes=[pltpu.VMEM((d, 2 * seg + 2 * mp), BF), pltpu.VMEM((d, d), BF)],
        compiler_params=params(30),
        cost_estimate=pl.CostEstimate(
            flops=8 * seg * d * d, bytes_accessed=16 * d * d, transcendentals=0
        ),
        name="feed_grad",
    )(*args, *deps)


def attention_grad_kernel(
    me_ref, tok_ref, toko_ref, m_ref, ge_ref, go_ref, gr1_ref, gr1o_ref, gr1m_ref, a_ref, ao_ref, am_ref,
    pack_ref, s_ref, so_ref, keep0, send0, keep1, send1, lt0, lt1, sc, rest
):
    seg, d = tok_ref.shape
    mp = m_ref.shape[0]
    keys = seg + mp
    w1 = HPB * HD
    chunk = d // 8
    me = me_ref[0]
    turn(lt0, (tok_ref, m_ref, toko_ref, pack_ref.at[7]))
    turn(lt1, (gr1_ref, gr1o_ref, gr1m_ref, pack_ref.at[3]))
    vecs = s_ref[0:8] + so_ref[0:8]
    a, b, c, e = seg, 2 * seg, 2 * seg + mp, 2 * seg + 2 * mp
    for y in range(2):
        x = nn(lt0[:, 0:keys], ge_ref[y]) + nn(lt0[:, keys:], go_ref[y])
        r = nn(lt1[:, 0:a], a_ref[y]) + nn(lt1[:, a:b], ao_ref[y])
        r += nn(lt1[:, b:c], am_ref[2 * y])
        r += nn(lt1[:, c:e], pack_ref[8, :, y * 4 * HD : (y + 1) * 4 * HD])
        sc[...] = jnp.concatenate([x, r[:, 0:w1]], axis=1).astype(BF)
        j = 2 * y
        bias = s_ref[12 + j : 13 + j] + so_ref[13 + j : 14 + j]
        up = s_ref[8 + j : 9 + j] + so_ref[9 + j : 10 + j]
        second = jnp.concatenate([bias[:, w1 : 2 * w1], vecs[6:7, 0 : d - w1]], axis=1)
        at = pl.multiple_of(16 + 8 * (j ^ me), 8)
        mem = s_ref[pl.ds(at, 8), :] + so_ref[pl.ds(at, 8), :]
        for i in range(8):
            part = [vecs[t : t + 1, i * chunk : (i + 1) * chunk] for t in range(6)]
            top = jnp.concatenate(part + [bias[:, 0:w1]], axis=1)
            rest[i] = jnp.concatenate([top, second, up, mem[0:5]], axis=0).astype(BF)
        spread_block(y, me_ref[1], sc, chunk, keep0, send0, keep1, send1, rest)


def attention_grad(
    me, tok, tok_o, m, ge, go, gr1, gr1_o, gr1m, a, a_o, am, pack_o, small, small_o, deps=()
):
    seg, d = tok.shape
    mp = m.shape[0]
    args = (me, tok, tok_o, m, ge, go, gr1, gr1_o, gr1m, a, a_o, am, pack_o, small, small_o)
    return pl.pallas_call(
        after(attention_grad_kernel, 15, len(deps)),
        out_shape=grad_shapes(d // 8 + 8, d),
        in_specs=[sm_spec()] + [vm_spec()] * 14 + [any_spec()] * len(deps),
        out_specs=[vm_spec()] * 4,
        scratch_shapes=[
            pltpu.VMEM((d, 2 * seg + 2 * mp), BF),
            pltpu.VMEM((d, 2 * seg + 2 * mp), BF),
            pltpu.VMEM((d, d), BF),
            pltpu.VMEM((8, 8, d), BF),
        ],
        compiler_params=params(34),
        cost_estimate=pl.CostEstimate(
            flops=8 * seg * d * d, bytes_accessed=16 * d * d, transcendentals=0
        ),
        name="attention_grad",
    )(*args, *deps)


def plus(a, b):
    return (a.astype(F32) + b.astype(F32)).astype(BF)


def sum_xy_kernel(me_ref, keep0, recv0, keep1, recv1, ak, as_, bk, bs):
    xb = me_ref[1]
    for z in range(4):
        ak[z] = plus(keep0[0, z], recv0[0, z])
        as_[z] = plus(keep0[1, z], recv0[1, z])
        bk[z] = plus(keep1[z, xb], recv1[z, xb])
        bs[z] = plus(keep1[z, 1 - xb], recv1[z, 1 - xb])


def sum_yx_kernel(me_ref, ak, ar, bk, br, *outs):
    z = me_ref[2]
    for i, o in enumerate(outs):
        t = (z + i) % 4
        o[0] = plus(ak[t], ar[t])
        o[1] = plus(bk[t], br[t])


def sum_z(refs):
    halves = []
    for h in range(2):
        t = refs[0][h].astype(F32)
        for r in refs[1:]:
            t = t + r[h].astype(F32)
        halves.append(t)
    return jnp.concatenate(halves, axis=1)


def up_kernel(a, b, c, e, o):
    o[...] = sum_z((a, b, c, e))


def down_kernel(a, b, c, e, o):
    o[...] = sum_z((a, b, c, e)).T


def attention_kernel(a, b, c, e, q, k, v, o, rest):
    t = sum_z((a, b, c, e))
    n, w1 = q.shape
    q[...] = t[0:n, 0:w1]
    k[...] = t[0:n, w1 : 2 * w1]
    v[...] = t[0:n, 2 * w1 : 3 * w1]
    o[...] = t[0:n, 3 * w1 : 4 * w1].T
    rest[...] = t[n:]


def small_call(kernel, shapes, args, name, scalars=False, deps=()):
    return pl.pallas_call(
        after(kernel, len(args), len(deps)),
        out_shape=shapes,
        in_specs=([sm_spec()] if scalars else [])
        + [vm_spec()] * (len(args) - scalars)
        + [any_spec()] * len(deps),
        out_specs=[vm_spec()] * len(shapes),
        compiler_params=params(12),
        name=name,
    )(*args, *deps)


def pack_kernel(q_ref, k_ref, v_ref, o_ref, u_ref, d_ref, out_ref):
    n, w1 = q_ref.shape
    d = u_ref.shape[1]
    for i, r in enumerate((q_ref, k_ref, v_ref)):
        out_ref[:, i * w1 : (i + 1) * w1] = r[...]
    out_ref[:, 3 * w1 : 4 * w1] = o_ref[...].astype(F32).T.astype(BF)
    out_ref[:, d : 2 * d] = u_ref[...]
    out_ref[:, 2 * d : 3 * d] = d_ref[...].astype(F32).T.astype(BF)


def pack(*weights):
    n = weights[0].shape[0]
    d = weights[4].shape[1]
    return pl.pallas_call(
        pack_kernel,
        out_shape=jax.ShapeDtypeStruct((n, 3 * d), BF),
        in_specs=[vm_spec()] * 6,
        out_specs=vm_spec(),
        name="pack",
    )(*weights)


def flip(a, axis, bit):
    return lax.ppermute(a, axis, [(i, i ^ bit) for i in range(lax.axis_size(axis))])


def shift(a, by):
    n = lax.axis_size("dp")
    return lax.ppermute(a, "dp", [(i, (i + by) % n) for i in range(n)])


def pick(a, i, axis):
    return lax.dynamic_index_in_dim(a, i, axis, keepdims=False)


def start_xy(keep0, send0, keep1, send1):
    return keep0, flip(send0, "dp", 1), keep1, flip(send1, "mp", 2)


def middle_xy(place, parts, deps=()):
    _, nz, n, half = parts[0].shape
    shape = jax.ShapeDtypeStruct((nz, n, half), BF)
    ak, as_, bk, bs = small_call(sum_xy_kernel, [shape] * 4, (place, *parts), "sum_xy", True, deps)
    return ak, flip(as_, "mp", 2), bk, flip(bs, "dp", 1)


def start_z(place, parts, deps=()):
    _, n, half = parts[0].shape
    shape = jax.ShapeDtypeStruct((2, n, half), BF)
    own, up, far, down = small_call(sum_yx_kernel, [shape] * 4, (place, *parts), "sum_yx", True, deps)
    return own, shift(far, 4), shift(up, 2), shift(down, -2)


def exchange(x):
    me = lax.axis_index("mp")
    nb = x.shape[0]
    got = [pick(x, me, 0)]
    for i in range(1, nb):
        got.append(flip(pick(x, me ^ i, 0), "mp", i))
    return relative(jnp.stack(got))


def relative(x):
    me = lax.axis_index("mp")
    v = x.reshape((2, 2) + x.shape[1:])
    v = jnp.where(me % 2 == 1, v[:, ::-1], v)
    v = jnp.where(me // 2 == 1, v[::-1], v)
    return v.reshape(x.shape)


def gather_small(x):
    nd = lax.axis_size("dp")
    nb = lax.axis_size("mp")
    if nd != 8:
        return lax.all_gather(x, ("mp", "dp"), axis=0).reshape(nb, nd, -1)
    k = x.shape[0]
    t = x.reshape(1, k)
    me = lax.axis_index("dp")
    b = me % 2
    z = me // 2
    o = flip(t, "mp", 1)
    c = lax.axis_index("mp") % 2
    t = jnp.where(c == 0, jnp.concatenate([t, o]), jnp.concatenate([o, t]))
    o = flip(t, "mp", 2)
    y = lax.axis_index("mp") // 2
    t = jnp.where(y == 0, jnp.concatenate([t, o]), jnp.concatenate([o, t]))
    o = flip(t, "dp", 1)
    t = jnp.where(b == 0, jnp.stack([t, o]), jnp.stack([o, t]))
    up, down, far = shift(t, -2), shift(t, 2), shift(t, 4)
    ring = jnp.stack([t, up, far, down, t, up, far])
    t = lax.dynamic_slice_in_dim(ring, (4 - z) % 4, 4, 0)
    return t.reshape(nd, nb, k).transpose(1, 0, 2)


def body(
    tokens, memory_init, query_weight, query_bias, key_weight, value_weight, value_bias, out_weight,
    out_bias, first_gain, first_shift, up_weight, up_bias, down_weight, down_bias, second_gain,
    second_shift, cotangent, group_segs, chain_group
):
    nd = lax.axis_size("dp")
    nb = lax.axis_size("mp")
    me = lax.axis_index("mp")
    dp = lax.axis_index("dp")
    tuned = nd == 8
    place = [me, dp % 2, dp // 2] if tuned else [me, 0 * me, 0 * me]
    me1 = jnp.stack(place).astype(jnp.int32)
    segments = tokens.shape[1]
    d = tokens.shape[3]
    part = tokens.shape[2]
    seg = part * nb
    nmem = memory_init.shape[0] * nb
    pad = -(-nmem // 16) * 16
    both = ("mp", "dp")
    wl = pack(query_weight, key_weight, value_weight, out_weight, up_weight, down_weight)
    w = lax.all_gather(wl, both, axis=0).reshape(nb, d, 3 * d)
    vecs = (out_bias, first_gain, first_shift, down_bias, second_gain, second_shift)
    small = jnp.concatenate(
        (query_bias, value_bias, up_bias) + vecs + (memory_init.reshape(-1),)
    )
    n1 = query_bias.shape[0]
    n2 = up_bias.shape[0]
    sg = gather_small(small)
    qb = sg[:, :, 0:n1].reshape(nb, 1, -1).astype(F32)
    vb = sg[:, :, n1 : 2 * n1].reshape(nb, 1, -1).astype(F32)
    qkvb = jnp.concatenate([qb, jnp.zeros_like(qb), vb], axis=2)
    ub = sg[:, :, 2 * n1 : 2 * n1 + n2].reshape(nb, 1, -1).astype(F32)
    at = 2 * n1 + n2
    vec = sg[:, :, at : at + 6 * n1].reshape(nb, nd, 6, n1).transpose(2, 1, 0, 3).reshape(6, d)
    vec = jnp.pad(vec.astype(F32), ((0, 2), (0, 0)))
    ml = memory_init.shape[0]
    m0 = sg[:, :, at + 6 * n1 :].reshape(nb, nd, ml, -1).transpose(0, 2, 1, 3).reshape(nmem, d)
    m0 = jnp.pad(m0.astype(F32), ((0, pad - nmem), (0, 0)))
    tok = exchange(tokens[0]).reshape(seg, d)
    ct = exchange(cotangent[0]).reshape(seg, d)
    match = chain_group[:, None] == jnp.arange(group_segs.shape[0], dtype=jnp.int32)[None, :]
    count = jnp.sum(jnp.where(match, group_segs[None, :], 0))
    live = (me < count).astype(F32)
    live2 = jnp.full((8, 128), live, F32)
    q, k, v = qkv_call(me1, tok, w, qkvb)
    m = jnp.where(me == 0, m0, 0.0)
    own = m
    saved = ()
    for s in range(segments - 1):
        z, *saved = mem_forward(me1, m, k, v, w, qkvb, ub, vec, nmem, s, saved)
        m = lax.ppermute(z, "mp", [(s, s + 1)])
        own = own + m
    (out, z1b, a0, a1, g0, g1, gf0, gf1, gr2b, gr1, gr1b, gq, gk, gv, base, sm, ubg) = token_call(
        me1, tok, ct, live2, own, q, k, v, w, qkvb, ub, vec, nmem
    )
    am, z1m, g_m = saved[4:7]
    send = base
    gin = jnp.zeros_like(base)
    for s in reversed(range(segments - 1)):
        recv = lax.ppermute(send, "mp", [(s + 1, s)])
        gin = gin + recv
        if s > 0:
            send = mem_backward(me1, recv, k, v, w, vec, base, saved)
    (z2m,) = mem_forward(me1, own, k, v, w, qkvb, ub, vec, nmem, None, (), (send,))
    other = lambda x: flip(x, "mp", 1)
    sends, _ = lax.optimization_barrier(((z1b, gf1, gr2b, g1, gr1b, a1), (recv, z2m)))
    z1b_o, gf_o, gr2b_o, g_o, gr1b_o, a_o = [other(x) for x in sends]
    tok_o = other(tok)
    gr2m, gfm, gr1m, smm, ubgm, extra = last_feed(me1, gin, w, vec, saved, own, (z2m,))
    extra_o = other(extra)
    up_g = feed_grad(me1, z1b, z1b_o, z1m, gf0, gf_o, gfm, extra_o, 4, 0)
    down_g = feed_grad(me1, gr2b, gr2b_o, gr2m, g0, g_o, g_m, extra_o, 2, 5, (up_g[0],))
    chains = nd * tokens.shape[0]
    w1 = d // nb
    chunk = d // nd
    small, ge, go, ig = last_attention(
        me1, gr1m, k, v, w, saved, gq, gk, gv, gr1, sm, smm, ubg, ubgm, z2m, live2, nmem, chains,
        (down_g[0],),
    )
    deps = ()
    if tuned:
        up_s = start_xy(*up_g)
        small, ge, go, ig, up_s = lax.optimization_barrier((small, ge, go, ig, up_s))
        up_s = middle_xy(me1, up_s)
        down_s = start_xy(*down_g)
        deps = (up_s[0],)
    att_g = attention_grad(
        me1, tok, tok_o, own, ge, other(go), gr1b, gr1b_o, gr1m, a0, a_o, am, extra_o, small,
        other(small), deps,
    )
    sds = jax.ShapeDtypeStruct
    if tuned:
        up_s, down_s, att_g, ig = lax.optimization_barrier((up_s, down_s, att_g, ig))
        up_s = start_z(me1, up_s)
        down_s = middle_xy(me1, down_s)
        att_s = start_xy(*att_g)
        up_s, down_s, att_s, out = lax.optimization_barrier((up_s, down_s, att_s, out))
        att_s = middle_xy(me1, att_s)
        down_s = start_z(me1, down_s)
        layer_out = exchange(out.reshape(nb, part, d))
        (wup,) = small_call(up_kernel, [sds((chunk, d), F32)], up_s, "up_out")
        down_s, att_s, wup, ig = lax.optimization_barrier((down_s, att_s, wup, ig))
        att_s = start_z(me1, att_s)
        input_grad = exchange(ig.reshape(nb, part, d))
        (wdn,) = small_call(down_kernel, [sds((d, chunk), F32)], down_s, "down_out")
        wq, wk, wv, wo, rest = small_call(
            attention_kernel,
            [sds((chunk, w1), F32)] * 3 + [sds((w1, chunk), F32), sds((8, d), F32)],
            att_s,
            "attention_out",
        )
        vg = lax.dynamic_slice(rest[0, 0 : 6 * chunk].reshape(6, chunk), (0, me * n1), (6, n1))
        qbg = lax.dynamic_slice(rest[0, 6 * chunk :], (dp * n1,), (n1,))
        vbg = lax.dynamic_slice(rest[1, 0:w1], (dp * n1,), (n1,))
        ubt = lax.dynamic_slice(rest[2], (dp * n2,), (n2,))
        gmi = lax.dynamic_slice(rest[3 : 3 + ml], (0, dp * chunk), (ml, chunk))
        norms = rest[1, w1 : w1 + segments]
    else:
        layer_out = exchange(out.reshape(nb, part, d))
        input_grad = exchange(ig.reshape(nb, part, d))

        def scatter(keep0, send0, keep1, send1):
            left = jnp.stack([keep0, send0], axis=2)
            right = jnp.stack([keep1, send1])
            x = jnp.concatenate([left, right], axis=4)[:, :, :, 0 : d // 8]
            x = x.reshape(2, nd, chunk, d).astype(F32)
            x = lax.psum_scatter(x, "dp", scatter_dimension=1, tiled=True)
            return (x[0] + flip(x[1], "mp", 2)).reshape(chunk, d)

        wup, wdn, watt = scatter(*up_g), scatter(*down_g).T, scatter(*att_g)
        wq, wk, wv = [watt[:, i * w1 : (i + 1) * w1] for i in range(3)]
        wo = watt[:, 3 * w1 :].T
        rows = jnp.concatenate(
            [small[0:8], relative(small[8:12]), relative(small[12:16]), small[16:]]
        )
        rows = lax.psum(rows, both)
        vg = lax.dynamic_slice(rows, (0, dp * chunk + me * n1), (6, n1))
        qbg = lax.dynamic_slice(rows, (12 + me, dp * n1), (1, n1))[0]
        vbg = lax.dynamic_slice(rows, (12 + me, w1 + dp * n1), (1, n1))[0]
        ubt = lax.dynamic_slice(rows, (8 + me, dp * n2), (1, n2))[0]
        gmi = lax.dynamic_slice(rows, (16 + 8 * me, dp * chunk), (ml, chunk))
        norms = rows[6, 0:segments]
    return (
        layer_out[None],
        input_grad[None],
        gmi,
        wq,
        qbg,
        wk,
        wv,
        vbg,
        wo,
        vg[0],
        vg[1],
        vg[2],
        wup,
        ubt,
        wdn,
        vg[3],
        vg[4],
        vg[5],
        norms,
    )


def solution(mesh):
    rows = P("dp", None, "mp", None)
    md, dm = P(("mp", "dp")), P(("dp", "mp"))
    win, wout = P("dp", "mp"), P("mp", "dp")
    in_specs = (
        rows, wout, win, md, win, win, md, wout, dm, dm, dm, win, md, wout, dm, dm, dm, rows, P(),
        P("dp"),
    )
    out_specs = (
        rows, rows, wout, win, md, win, win, md, wout, dm, dm, dm, win, md, wout, dm, dm, dm, P(),
    )
    return jax.shard_map(body, mesh=mesh, in_specs=in_specs, out_specs=out_specs, check_vma=False)
```

```python
import functools

import jax
import jax.numpy as jnp
from jax import lax
from jax.experimental import pallas as pl
from jax.experimental.pallas import tpu as pltpu
from jax.sharding import PartitionSpec as P

HD = 64
HPB = 3
BF = jnp.bfloat16
F32 = jnp.float32
MIB = 1024 * 1024
NEG = -1e30


def nn(a, b):
    return lax.dot_general(a, b, (((1,), (0,)), ((), ())), preferred_element_type=F32)


def nt(a, b):
    return lax.dot_general(a, b, (((1,), (1,)), ((), ())), preferred_element_type=F32)


def norm_stats(r):
    mean = jnp.mean(r, axis=-1, keepdims=True)
    c = r - mean
    inv = lax.rsqrt(jnp.mean(c * c, axis=-1, keepdims=True) + 1e-05)
    return c * inv, inv


def norm_back(g, xh, inv):
    return inv * (
        g - jnp.mean(g, axis=-1, keepdims=True) - xh * jnp.mean(g * xh, axis=-1, keepdims=True)
    )


def gelu_both(f):
    cdf = 0.5 + 0.5 * lax.erf(f * (0.5**0.5))
    pdf = jnp.exp(-0.5 * f * f) * ((2.0 * jnp.pi) ** -0.5)
    return f * cdf, cdf + f * pdf


def rows_mask(shape, count):
    return lax.broadcasted_iota(jnp.int32, shape, 0) < count


def any_spec():
    return pl.BlockSpec(memory_space=pl.ANY)


def vm_spec():
    return pl.BlockSpec(memory_space=pltpu.VMEM)


def params(mib):
    return pltpu.CompilerParams(vmem_limit_bytes=mib * MIB)


def sm_spec():
    return pl.BlockSpec(memory_space=pltpu.SMEM)


def after(kernel, n_in, n_dep):
    def run(*refs):
        kernel(*refs[:n_in], *refs[n_in + n_dep :])

    return run


def split_qkv(acc):
    w1 = HPB * HD
    zero = jnp.zeros((acc.shape[0], HD), BF)
    q = jnp.concatenate([(acc[:, 0:w1].astype(BF) * 0.125).astype(BF), zero], axis=1)
    k = jnp.concatenate([acc[:, w1 : 2 * w1].astype(BF), zero], axis=1)
    v = jnp.concatenate([acc[:, 2 * w1 : 3 * w1].astype(BF), zero], axis=1)
    return q, k, v


def head_cols(shape, i):
    c = lax.broadcasted_iota(jnp.int32, shape, len(shape) - 1)
    return (c >= i * HD) & (c < (i + 1) * HD)


def spread(x):
    return jnp.concatenate(
        [jnp.where(head_cols(x.shape, i), x, jnp.zeros_like(x)) for i in range(HPB)], axis=0
    )


def gather_heads(x):
    n = x.shape[0] // HPB
    out = jnp.zeros((n, x.shape[1]), x.dtype)
    for i in range(HPB):
        out = jnp.where(head_cols(out.shape, i), x[i * n : (i + 1) * n], out)
    return out


def out_cols(a):
    return jnp.concatenate([jnp.zeros((a.shape[0], HD), a.dtype), a[:, 0 : HPB * HD]], axis=1)


def qkv_kernel(me_ref, tok_ref, w_ref, qkvb_ref, q_ref, k_ref, v_ref):
    nb, d, _ = w_ref.shape
    me = me_ref[0]
    for j in range(nb):
        acc = nn(tok_ref[...], w_ref[j ^ me, :, 0 : 3 * HPB * HD]) + qkvb_ref[j ^ me]
        q, k, v = split_qkv(acc)
        q_ref[j] = q
        k_ref[j] = k
        v_ref[j] = v


def qkv_call(me, tok, w, qkvb):
    nb, d, _ = w.shape
    s = tok.shape[0]
    return pl.pallas_call(
        qkv_kernel,
        out_shape=[jax.ShapeDtypeStruct((nb, s, 4 * HD), BF)] * 3,
        in_specs=[sm_spec(), vm_spec(), vm_spec(), vm_spec()],
        out_specs=[vm_spec()] * 3,
        compiler_params=params(20),
        cost_estimate=pl.CostEstimate(
            flops=2 * s * d * 3 * d, bytes_accessed=8 * d * d, transcendentals=0
        ),
        name="qkv",
    )(me, tok, w, qkvb)


def mem_forward_kernel(
    nmem, step, me_ref, m_ref, k_hbm, v_hbm, w_ref, qkvb_ref, ub_ref, vec_ref, *rest
):
    save = step is not None
    old = ()
    if save and step > 0:
        old, rest = rest[:12], rest[12:]
    kept = rest[1:13]
    if save:
        (
            z2_ref, qm_ref, km_ref, vm_ref, pm_ref, am_ref, z1b_ref, g_ref, gp_ref, xh1_ref,
            xh2_ref, inv_ref, own_ref,
        ) = rest[:13]
        rest = rest[13:]
    else:
        z2_ref = rest[0]
        rest = rest[1:]
    kk, vv, sc, sem2 = rest
    nb, d, _ = w_ref.shape
    seg = k_hbm.shape[1]
    mp = m_ref.shape[0]
    keys = seg + mp
    w1 = HPB * HD
    me = me_ref[0]
    kc = pltpu.make_async_copy(k_hbm, kk.at[:, 0:seg, :], sem2.at[0])
    vc = pltpu.make_async_copy(v_hbm, vv.at[:, 0:seg, :], sem2.at[1])
    kc.start()
    vc.start()
    mem = m_ref[...]
    mb = mem.astype(BF)
    qs = []
    for j in range(nb):
        acc = nn(mb, w_ref[j ^ me, :, 0 : 3 * w1]) + qkvb_ref[j ^ me]
        q, k, v = split_qkv(acc)
        qs.append(q)
        kk[j, seg:keys, :] = k
        vv[j, seg:keys, :] = v
        if save:
            qm_ref[j] = q
            km_ref[j] = k
            vm_ref[j] = v
    kc.wait()
    vc.wait()
    n = HPB * mp
    for j in range(nb):
        sc[j * n : (j + 1) * n, :] = nt(spread(qs[j]), kk[j])
    keep = lax.broadcasted_iota(jnp.int32, (n, keys), 1) < seg + nmem
    heads = []
    for j in range(nb):
        s = jnp.where(keep, sc[j * n : (j + 1) * n, :], NEG)
        e = jnp.exp(s - jnp.max(s, axis=-1, keepdims=True))
        p = (e / jnp.sum(e, axis=-1, keepdims=True)).astype(BF)
        if save:
            pm_ref[j] = p
        heads.append(p)
    out = jnp.zeros((mp, d), F32)
    for j in range(nb):
        a = gather_heads(nn(heads[j], vv[j])).astype(BF)
        if save:
            am_ref[j] = a
        out += nt(out_cols(a), w_ref[j ^ me, :, d - 4 * HD : d])
    xh1, inv1 = norm_stats(mem + out + vec_ref[0:1])
    z1 = xh1 * vec_ref[1:2] + vec_ref[2:3]
    z1b = z1.astype(BF)
    y = jnp.zeros((mp, d), F32)
    for j in range(nb):
        f = nn(z1b, w_ref[j ^ me, :, d : 2 * d]) + ub_ref[j ^ me]
        g, gp = gelu_both(f)
        g = g.astype(BF)
        if save:
            g_ref[j] = g
            gp_ref[j] = gp
        y += nt(g, w_ref[j ^ me, :, 2 * d : 3 * d])
    xh2, inv2 = norm_stats(z1 + y + vec_ref[3:4])
    z2 = xh2 * vec_ref[4:5] + vec_ref[5:6]
    z2_ref[...] = jnp.where(rows_mask((mp, d), nmem), z2, 0.0)
    if save:
        z1b_ref[...] = z1b
        xh1_ref[...] = xh1
        xh2_ref[...] = xh2
        inv_ref[:, 0:128] = jnp.broadcast_to(inv1, (mp, 128))
        inv_ref[:, 128:256] = jnp.broadcast_to(inv2, (mp, 128))
        own_ref[...] = z2_ref[...]
    if old:

        @pl.when(me != step)
        def _():
            for o, x in zip(kept, old):
                o[...] = x[...]


def mem_forward(me, m, k, v, w, qkvb, ub, vec, nmem, step=None, old=(), deps=(), first=()):
    save = step is not None
    if first:
        kernel = functools.partial(mem_last_kernel, nmem)
    else:
        kernel = functools.partial(mem_forward_kernel, nmem, step)
    nb, d, _ = w.shape
    seg = k.shape[1]
    mp = m.shape[0]
    keys = seg + mp
    sds = jax.ShapeDtypeStruct
    shapes = [sds((mp, d), F32)]
    if save:
        shapes += [sds((nb, mp, 4 * HD), BF)] * 3
        shapes += [
            sds((nb, HPB * mp, keys), BF),
            sds((nb, mp, 4 * HD), BF),
            sds((mp, d), BF),
            sds((nb, mp, d), BF),
            sds((nb, mp, d), F32),
            sds((mp, d), F32),
            sds((mp, d), F32),
            sds((mp, 256), F32),
            sds((mp, d), F32),
        ]
    return pl.pallas_call(
        after(kernel, 8 + len(old) + len(first), len(deps)),
        out_shape=shapes,
        in_specs=[sm_spec(), vm_spec()]
        + [vm_spec()] * len(first)
        + [any_spec()] * 2
        + [vm_spec()] * (4 + len(old))
        + [any_spec()] * len(deps),
        out_specs=[vm_spec()] * len(shapes),
        scratch_shapes=[
            pltpu.VMEM((nb, keys, 4 * HD), BF),
            pltpu.VMEM((nb, keys, 4 * HD), BF),
            pltpu.VMEM((nb * HPB * mp, keys), F32),
            pltpu.SemaphoreType.DMA((2,)),
        ],
        compiler_params=params(24),
        cost_estimate=pl.CostEstimate(
            flops=2 * mp * d * d * 12, bytes_accessed=24 * d * d, transcendentals=0
        ),
        name="mem_forward_save" if save else "mem_forward",
    )(me, *first, m, k, v, w, qkvb, ub, vec, *old, *deps)


def mem_last_kernel(nmem, me_ref, own_ref, *rest):
    ins, out, scratch = rest[:7], rest[7], rest[8:]
    me = me_ref[0]
    last = ins[3].shape[0] - 1

    @pl.when(me == last)
    def _():
        mem_forward_kernel(nmem, None, me_ref, *ins, out, *scratch)

    @pl.when(me != last)
    def _():
        out[...] = own_ref[...]


def colsum(x):
    return jnp.sum(x, axis=0, keepdims=True)


CH = 64


def token_kernel(
    nmem,
    me_ref,
    tok_ref,
    ct_ref,
    live_ref,
    m_ref,
    qq,
    k_hbm,
    v_hbm,
    w_ref,
    qkvb_ref,
    ub_ref,
    vec_ref,
    out_ref,
    z1b_ref,
    a0_ref,
    a1_ref,
    g0_ref,
    g1_ref,
    gf0_ref,
    gf1_ref,
    gr2b_ref,
    gr1_ref,
    g1b,
    gq_ref,
    gk_ref,
    gv_ref,
    base_ref,
    small_ref,
    ubg_ref,
    kk,
    vv,
    probs,
    big,
    one,
    inv,
    sem2,
):
    nb, d, _ = w_ref.shape
    seg = tok_ref.shape[0]
    mp = m_ref.shape[0]
    keys = seg + mp
    w1 = HPB * HD
    steps = seg // CH
    me = me_ref[0]
    loads = [
        pltpu.make_async_copy(k_hbm, kk.at[:, 0:seg, :], sem2.at[1]),
        pltpu.make_async_copy(v_hbm, vv.at[:, 0:seg, :], sem2.at[2]),
    ]
    for c in loads:
        c.start()
    mb = m_ref[...].astype(BF)
    for j in range(nb):
        _, k, v = split_qkv(nn(mb, w_ref[j ^ me, :, 0 : 3 * w1]) + qkvb_ref[j ^ me])
        kk[j, seg:keys, :] = k
        vv[j, seg:keys, :] = v
    for c in loads:
        c.wait()
    one[...] = jnp.zeros_like(one)
    tail = seg + (nmem // 8) * 8

    a_refs = (a0_ref, a1_ref)
    g_refs = (g0_ref, g1_ref)
    gf_refs = (gf0_ref, gf1_ref)

    def attend_one(j, y, c):
        vt = vv[j].astype(F32).T.astype(BF)
        parts = []
        for i in range(HPB):
            cols = slice(i * HD, (i + 1) * HD)
            big[0:keys, 0:seg] = nt(kk[j, :, cols], qq[j, :, cols])
            big[tail:keys, 0:seg] = jnp.where(
                rows_mask((keys - tail, seg), seg + nmem - tail), big[tail:keys, 0:seg], NEG
            )
            for t in range(seg // 128):
                cols = slice(t * 128, (t + 1) * 128)
                s = big[0:keys, cols]
                e = jnp.exp(s - jnp.max(s, axis=0, keepdims=True))
                p = e * (1.0 / jnp.sum(e, axis=0, keepdims=True))
                probs[j * HPB + i, :, cols] = p.astype(BF)
            parts.append(nn(vt[i * HD : (i + 1) * HD], probs[j * HPB + i]))
        parts.append(jnp.zeros((HD, seg), F32))
        a = jnp.concatenate(parts, axis=0).T.astype(BF)
        a_refs[c][y] = a
        one[...] += nt(out_cols(a), w_ref[j ^ me, :, d - 4 * HD : d])

    def attend(y, _):
        for c in range(2):
            attend_one(2 * y + c, y, c)
        return 0

    for y in range(nb // 2):
        attend(y, 0)

    for c in range(steps):
        rows = slice(c * CH, (c + 1) * CH)
        r = tok_ref[rows, :].astype(F32) + one[rows, :] + vec_ref[0:1]
        x, v = norm_stats(r)
        gr1_ref[rows, :] = x
        inv[rows, 0:128] = jnp.broadcast_to(v, (CH, 128))
        z1 = x * vec_ref[1:2] + vec_ref[2:3]
        z1b_ref[rows, :] = z1.astype(BF)
        one[rows, :] = z1 + vec_ref[3:4]

    def feed_one(j, y, c):
        big[0:seg, 0:d] = nn(z1b_ref[...], w_ref[j ^ me, :, d : 2 * d])

        for r in range(seg // 32):
            rows = slice(r * 32, (r + 1) * 32)
            g, p = gelu_both(big[rows, 0:d] + ub_ref[j ^ me])
            g_refs[c][y, rows, :] = g.astype(BF)
            gf_refs[c][y, rows, :] = p.astype(BF)
        one[...] += nt(g_refs[c][y], w_ref[j ^ me, :, 2 * d : 3 * d])

    def feed(y, _):
        for c in range(2):
            feed_one(2 * y + c, y, c)
        return 0

    for y in range(nb // 2):
        feed(y, 0)
    zero = jnp.zeros((1, d), F32)

    sg, ss, sb = zero, zero, zero
    for c in range(steps):
        rows = slice(c * CH, (c + 1) * CH)
        x, v = norm_stats(one[rows, :])
        out_ref[rows, :] = ((x * vec_ref[4:5] + vec_ref[5:6]) * live_ref[0:1, 0:1]).astype(BF)
        gz = ct_ref[rows, :].astype(F32) * live_ref[0:1, 0:1]
        gr = norm_back(gz * vec_ref[4:5], x, v)
        one[rows, :] = gr
        gr2b_ref[rows, :] = gr.astype(BF)
        sg, ss, sb = sg + colsum(gz * x), ss + colsum(gz), sb + colsum(gr)
    small_ref[3:4] = sb
    small_ref[4:5] = sg
    small_ref[5:6] = ss

    def feed_back_one(j, y, c):
        big[0:seg, 0:d] = nn(gr2b_ref[...], w_ref[j ^ me, :, 2 * d : 3 * d])

        total = zero
        for r in range(seg // 64):
            rows = slice(r * 64, (r + 1) * 64)
            gf = (big[rows, 0:d] * gf_refs[c][y, rows, :].astype(F32)).astype(BF)
            gf_refs[c][y, rows, :] = gf
            total = total + colsum(gf.astype(F32))
        ubg_ref[j] = total
        one[...] += nt(gf_refs[c][y], w_ref[j ^ me, :, d : 2 * d])

    def feed_back(y, _):
        for c in range(2):
            feed_back_one(2 * y + c, y, c)
        return 0

    for y in range(nb // 2):
        feed_back(y, 0)

    sg, ss, sb = zero, zero, zero
    for c in range(steps):
        rows = slice(c * CH, (c + 1) * CH)
        gz = one[rows, :]
        x = gr1_ref[rows, :]
        gr = norm_back(gz * vec_ref[1:2], x, inv[rows, 0:1])
        gr1_ref[rows, :] = gr
        g1b[rows, :] = gr.astype(BF)
        sg, ss, sb = sg + colsum(gz * x), ss + colsum(gz), sb + colsum(gr)
    small_ref[0:1] = sb
    small_ref[1:2] = sg
    small_ref[2:3] = ss
    small_ref[6:8] = jnp.zeros((2, d), F32)

    def attend_back_one(j, y, c, base):
        ga = nn(g1b[...], w_ref[j ^ me, :, d - 4 * HD : d])[:, HD:]
        gab = ga.astype(BF)
        delta = (gab.astype(F32) * a_refs[c][y, :, 0:w1].astype(F32)).T
        kt = kk[j].astype(F32).T.astype(BF)
        gqs = []
        gks = []
        gvs = []
        for i in range(HPB):
            cols = slice(i * HD, (i + 1) * HD)
            g = gab[:, cols]
            p = probs[j * HPB + i]
            dl = jnp.sum(delta[cols], axis=0, keepdims=True)
            gvs.append(nn(p, g))
            gs = (p.astype(F32) * (nt(vv[j, :, cols], g) - dl)).astype(BF)
            gks.append(nn(gs, qq[j, :, cols]))
            gqs.append(nn(kt[cols], gs))
        zq = jnp.zeros((HD, seg), F32)
        zk = jnp.zeros((keys, HD), F32)
        gq_ref[j] = (jnp.concatenate(gqs + [zq], axis=0).T * 0.125).astype(BF)
        gk = jnp.concatenate(gks + [zk], axis=1)
        gv = jnp.concatenate(gvs + [zk], axis=1)
        gk_ref[j] = gk.astype(BF)
        gv_ref[j] = gv.astype(BF)
        gm = jnp.concatenate(
            [jnp.zeros((mp, w1), F32), gk[seg:keys, 0:w1], gv[seg:keys, 0:w1]], axis=1
        ).astype(BF)
        return base + nt(gm, w_ref[j ^ me, :, 0 : 3 * w1])

    def attend_back(y, base):
        for c in range(2):
            base = attend_back_one(2 * y + c, y, c, base)
        return base

    total = jnp.zeros((mp, d), F32)
    for y in range(nb // 2):
        total = attend_back(y, total)
    base_ref[...] = total


def token_call(me, tok, ct, live, m, q, k, v, w, qkvb, ub, vec, nmem):
    nb, d, _ = w.shape
    seg = tok.shape[0]
    mp = m.shape[0]
    keys = seg + mp
    sds = jax.ShapeDtypeStruct
    shapes = [
        sds((seg, d), BF),
        sds((seg, d), BF),
        sds((nb // 2, seg, 4 * HD), BF),
        sds((nb // 2, seg, 4 * HD), BF),
        sds((nb // 2, seg, d), BF),
        sds((nb // 2, seg, d), BF),
        sds((nb // 2, seg, d), BF),
        sds((nb // 2, seg, d), BF),
        sds((seg, d), BF),
        sds((seg, d), F32),
        sds((seg, d), BF),
        sds((nb, seg, 4 * HD), BF),
        sds((nb, keys, 4 * HD), BF),
        sds((nb, keys, 4 * HD), BF),
        sds((mp, d), F32),
        sds((8, d), F32),
        sds((nb, 1, d), F32),
    ]
    return pl.pallas_call(
        functools.partial(token_kernel, nmem),
        out_shape=shapes,
        in_specs=[sm_spec()] + [vm_spec()] * 5 + [any_spec()] * 2 + [vm_spec()] * 4,
        out_specs=[vm_spec()] * len(shapes),
        scratch_shapes=[
            pltpu.VMEM((nb, keys, 4 * HD), BF),
            pltpu.VMEM((nb, keys, 4 * HD), BF),
            pltpu.VMEM((nb * HPB, keys, seg), BF),
            pltpu.VMEM((keys, d), F32),
            pltpu.VMEM((seg, d), F32),
            pltpu.VMEM((seg, 128), F32),
            pltpu.SemaphoreType.DMA((3,)),
        ],
        compiler_params=params(43),
        cost_estimate=pl.CostEstimate(
            flops=5 * seg * d * d * 12, bytes_accessed=60 * d * d, transcendentals=0
        ),
        name="token_rows",
    )(me, tok, ct, live, m, q, k, v, w, qkvb, ub, vec)


def back_feed(w_ref, me, nb, d, gz, vec_ref, gp_ref, xh1, xh2, inv_ref, gf_ref=None, ubg_ref=None):
    gr2 = norm_back(gz * vec_ref[4:5], xh2, inv_ref[:, 128:129])
    gr2b = gr2.astype(BF)
    acc = gr2
    for j in range(nb):
        gf = (nn(gr2b, w_ref[j ^ me, :, 2 * d : 3 * d]) * gp_ref[j]).astype(BF)
        if gf_ref is not None:
            gf_ref[j] = gf
            ubg_ref[j] = colsum(gf.astype(F32))
        acc += nt(gf, w_ref[j ^ me, :, d : 2 * d])
    return gr2, acc, norm_back(acc * vec_ref[1:2], xh1, inv_ref[:, 0:1])


def back_scores(j, gab, am_ref, pm_ref, vv, delta_rows):
    n = HPB * delta_rows
    gs3 = spread(gab)
    a3 = jnp.concatenate([am_ref[j]] * HPB, axis=0)
    dl = jnp.sum(gs3.astype(F32) * a3.astype(F32), axis=1, keepdims=True)
    p = pm_ref[j].astype(F32)
    return gs3, p, (p * (nt(gs3, vv[j]) - dl)).astype(BF)


def mem_backward_kernel(
    nmem, me_ref, g_ref, k_hbm, v_hbm, w_ref, vec_ref, base_ref, qm_ref, km_ref, vm_ref, pm_ref,
    am_ref, gp_ref, xh1_ref, xh2_ref, inv_ref, gm_ref, kk, vv, sem2
):
    nb, d, _ = w_ref.shape
    seg = k_hbm.shape[1]
    mp = g_ref.shape[0]
    keys = seg + mp
    w1 = HPB * HD
    me = me_ref[0]
    kc = pltpu.make_async_copy(k_hbm, kk.at[:, 0:seg, :], sem2.at[0])
    vc = pltpu.make_async_copy(v_hbm, vv.at[:, 0:seg, :], sem2.at[1])
    kc.start()
    vc.start()
    kk[:, seg:keys, :] = km_ref[...]
    vv[:, seg:keys, :] = vm_ref[...]
    _, _, gr1 = back_feed(
        w_ref, me, nb, d, g_ref[...], vec_ref, gp_ref, xh1_ref[...], xh2_ref[...], inv_ref
    )
    gr1b = gr1.astype(BF)
    kc.wait()
    vc.wait()
    gabs = []
    for j in range(nb):
        ga = nn(gr1b, w_ref[j ^ me, :, d - 4 * HD : d]).astype(BF)
        gabs.append(jnp.concatenate([ga[:, HD:], jnp.zeros((mp, HD), BF)], axis=1))
    scores = [back_scores(j, gabs[j], am_ref, pm_ref, vv, mp) for j in range(nb)]
    out = gr1 + base_ref[...]
    for j in range(nb):
        gs3, p, gs = scores[j]
        gq = gather_heads(nn(gs, kk[j])) * 0.125
        gk = nn(gs[:, seg:keys].astype(F32).T.astype(BF), spread(qm_ref[j]))
        gv = nn(p[:, seg:keys].T.astype(BF), gs3)
        gm = jnp.concatenate([gq[:, 0:w1], gk[:, 0:w1], gv[:, 0:w1]], axis=1).astype(BF)
        out += nt(gm, w_ref[j ^ me, :, 0 : 3 * w1])
    gm_ref[...] = out


def mem_backward(me, g, k, v, w, vec, base, saved):
    nb, d, _ = w.shape
    seg = k.shape[1]
    mp = g.shape[0]
    keys = seg + mp
    qm, km, vm, pm, am, _, _, gp, xh1, xh2, inv, _ = saved
    args = (me, g, k, v, w, vec, base, qm, km, vm, pm, am, gp, xh1, xh2, inv)
    return pl.pallas_call(
        functools.partial(mem_backward_kernel, 0),
        out_shape=jax.ShapeDtypeStruct((mp, d), F32),
        in_specs=[sm_spec(), vm_spec()] + [any_spec()] * 2 + [vm_spec()] * 12,
        out_specs=vm_spec(),
        scratch_shapes=[
            pltpu.VMEM((nb, keys, 4 * HD), BF),
            pltpu.VMEM((nb, keys, 4 * HD), BF),
            pltpu.SemaphoreType.DMA((2,)),
        ],
        compiler_params=params(24),
        cost_estimate=pl.CostEstimate(
            flops=2 * mp * d * d * 12, bytes_accessed=24 * d * d, transcendentals=0
        ),
        name="mem_backward",
    )(*args)


def last_feed_kernel(
    me_ref, g_ref, w_ref, vec_ref, gp_ref, xh1_ref, xh2_ref, inv_ref, z1m_ref, gm_ref, m_ref, am_ref,
    gr2b_ref, gf_ref, gr1_ref, small_ref, ubg_ref, pack_ref
):
    nb, d, _ = w_ref.shape
    me = me_ref[0]
    gz = g_ref[...]
    xh1 = xh1_ref[...]
    xh2 = xh2_ref[...]
    gr2, gz1, gr1 = back_feed(
        w_ref, me, nb, d, gz, vec_ref, gp_ref, xh1, xh2, inv_ref, gf_ref, ubg_ref
    )
    gr2b_ref[...] = gr2.astype(BF)
    gr1_ref[...] = gr1
    mp, _ = gz.shape
    for y in range(nb // 2):
        pack_ref[y] = gf_ref[2 * y + 1]
        pack_ref[5 + y] = gm_ref[2 * y + 1]
        pack_ref[8, :, y * 4 * HD : (y + 1) * 4 * HD] = am_ref[2 * y + 1]
    pack_ref[8, :, 8 * HD : d] = jnp.zeros((mp, d - 8 * HD), BF)
    pack_ref[2] = gr2.astype(BF)
    pack_ref[3] = gr1.astype(BF)
    pack_ref[4] = z1m_ref[...]
    pack_ref[7] = m_ref[...].astype(BF)
    small_ref[0:1] = colsum(gr1)
    small_ref[1:2] = colsum(gz1 * xh1)
    small_ref[2:3] = colsum(gz1)
    small_ref[3:4] = colsum(gr2)
    small_ref[4:5] = colsum(gz * xh2)
    small_ref[5:6] = colsum(gz)
    small_ref[6:8] = jnp.zeros((2, d), F32)


def last_feed(me, g, w, vec, saved, m, deps=()):
    nb, d, _ = w.shape
    mp = g.shape[0]
    _, _, _, _, am, z1m, gm, gp, xh1, xh2, inv, _ = saved
    sds = jax.ShapeDtypeStruct
    shapes = [
        sds((mp, d), BF),
        sds((nb, mp, d), BF),
        sds((mp, d), F32),
        sds((8, d), F32),
        sds((nb, 1, d), F32),
        sds((9, mp, d), BF),
    ]
    return pl.pallas_call(
        after(last_feed_kernel, 12, len(deps)),
        out_shape=shapes,
        in_specs=[sm_spec()] + [vm_spec()] * 11 + [any_spec()] * len(deps),
        out_specs=[vm_spec()] * len(shapes),
        compiler_params=params(20),
        cost_estimate=pl.CostEstimate(
            flops=2 * mp * d * d * 8, bytes_accessed=16 * d * d, transcendentals=0
        ),
        name="last_feed",
    )(me, g, w, vec, gp, xh1, xh2, inv, z1m, gm, m, am, *deps)


def last_attention_kernel(
    nmem, chains, me_ref, gr1m_ref, k_hbm, v_hbm, w_ref, qm_ref, km_ref, vm_ref, pm_ref, am_ref, gq_ref, gk_ref,
    gv_ref, gr1_ref, sm_ref, smm_ref, ubg_ref, ubgm_ref, z2m_ref, live_ref, small_ref, ge_ref, go_ref,
    ig_ref, kk, vv, one, sem2
):
    nb, d, _ = w_ref.shape
    seg = k_hbm.shape[1]
    mp = gr1m_ref.shape[0]
    keys = seg + mp
    w1 = HPB * HD
    me = me_ref[0]
    kc = pltpu.make_async_copy(k_hbm, kk.at[:, 0:seg, :], sem2.at[0])
    vc = pltpu.make_async_copy(v_hbm, vv.at[:, 0:seg, :], sem2.at[1])
    kc.start()
    vc.start()
    kk[:, seg:keys, :] = km_ref[...]
    vv[:, seg:keys, :] = vm_ref[...]
    gr1 = gr1m_ref[...]
    gr1b = gr1.astype(BF)
    kc.wait()
    vc.wait()
    gabs = []
    for j in range(nb):
        ga = nn(gr1b, w_ref[j ^ me, :, d - 4 * HD : d]).astype(BF)
        gabs.append(jnp.concatenate([ga[:, HD:], jnp.zeros((mp, HD), BF)], axis=1))
    scores = [back_scores(j, gabs[j], am_ref, pm_ref, vv, mp) for j in range(nb)]
    out = gr1
    for j in range(nb):
        gs3, p, gs = scores[j]
        gq = (gather_heads(nn(gs, kk[j])) * 0.125).astype(BF)
        gk = (gk_ref[j] + nn(gs.astype(F32).T.astype(BF), spread(qm_ref[j]))).astype(BF)
        gv = (gv_ref[j] + nn(p.T.astype(BF), gs3)).astype(BF)
        gqt = gq_ref[j]
        o = (ge_ref, go_ref)[j % 2]
        y = j // 2
        o[y, 0:seg, 0:w1] = gqt[:, 0:w1]
        o[y, seg:keys, 0:w1] = gq[:, 0:w1]
        o[y, :, w1 : 2 * w1] = gk[:, 0:w1]
        o[y, :, 2 * w1 : 3 * w1] = gv[:, 0:w1]
        small_ref[8 + j : 9 + j] = ubg_ref[j] + ubgm_ref[j]
        small_ref[12 + j : 13 + j] = jnp.concatenate(
            [
                (colsum(gqt.astype(F32)) + colsum(gq.astype(F32)))[:, 0:w1],
                colsum(gv.astype(F32))[:, 0:w1],
                jnp.zeros((1, d - 2 * w1), F32),
            ],
            axis=1,
        )
        x = nt(o[y, 0:seg, :], w_ref[j ^ me, :, 0 : 3 * w1])
        if j == 0:
            one[...] = gr1_ref[...] + x
        else:
            one[...] += x
        out += nt(o[y, seg:keys, :], w_ref[j ^ me, :, 0 : 3 * w1])
    norm = jnp.sum(z2m_ref[...] * z2m_ref[...]) * (live_ref[0:1, 0:1] / (nmem * d * chains))
    lane = lax.broadcasted_iota(jnp.int32, (1, d), 1)
    small_ref[0:8] = sm_ref[...] + smm_ref[...]
    small_ref[6:7] = jnp.where(lane == me, norm, 0.0)
    small_ref[16:] = jnp.zeros_like(small_ref[16:])
    first = jnp.where(me == 0, 1.0, 0.0)
    each = nmem // nb
    for i in range(nb):
        small_ref[16 + 8 * i : 16 + 8 * i + each, :] = out[i * each : (i + 1) * each] * first
    ig_ref[...] = one[...].astype(BF)


def last_attention(
    me, gr1m, k, v, w, saved, gq, gk, gv, gr1, sm, smm, ubg, ubgm, z2m, live, nmem, chains, deps=()
):
    nb, d, _ = w.shape
    seg = k.shape[1]
    mp = gr1m.shape[0]
    keys = seg + mp
    w1 = HPB * HD
    qm, km, vm, pm, am, _, _, _, _, _, _, _ = saved
    sds = jax.ShapeDtypeStruct
    shapes = [
        sds((16 + 8 * nb, d), F32),
        sds((nb // 2, keys, 3 * w1), BF),
        sds((nb // 2, keys, 3 * w1), BF),
        sds((seg, d), BF),
    ]
    args = (me, gr1m, k, v, w, qm, km, vm, pm, am, gq, gk, gv, gr1, sm, smm, ubg, ubgm, z2m, live)
    return pl.pallas_call(
        after(functools.partial(last_attention_kernel, nmem, chains), 20, len(deps)),
        out_shape=shapes,
        in_specs=[sm_spec(), vm_spec()]
        + [any_spec()] * 2
        + [vm_spec()] * 16
        + [any_spec()] * len(deps),
        out_specs=[vm_spec()] * len(shapes),
        scratch_shapes=[
            pltpu.VMEM((nb, keys, 4 * HD), BF),
            pltpu.VMEM((nb, keys, 4 * HD), BF),
            pltpu.VMEM((seg, d), F32),
            pltpu.SemaphoreType.DMA((2,)),
        ],
        compiler_params=params(34),
        cost_estimate=pl.CostEstimate(
            flops=2 * seg * d * d * 4, bytes_accessed=30 * d * d, transcendentals=0
        ),
        name="last_attention",
    )(*args, *deps)


def turn(dst, refs):
    at = 0
    for r in refs:
        n = r.shape[0]
        dst[:, at : at + n] = r[...].astype(BF).astype(F32).T.astype(BF)
        at += n


def spread_block(y, xb, sc, n, keep0, send0, keep1, send1, rest=None):
    nz = keep0.shape[1]
    half = keep0.shape[3]
    for z in range(nz):
        for x in range(2):
            at = (2 * z + (x ^ xb)) * n
            part = sc[pl.ds(pl.multiple_of(at, 32), n), 0:half]
            (keep0, send0)[x][y, z, 0:n, :] = part
            (keep1, send1)[y][z, x, 0:n, :] = sc[(2 * z + x) * n : (2 * z + x + 1) * n, half:]
            if rest is not None:
                (keep0, send0)[x][y, z, n:, :] = rest[2 * z + (x ^ xb), :, 0:half]
                (keep1, send1)[y][z, x, n:, :] = rest[2 * z + x, :, half:]


def grad_shapes(n, d):
    sds = jax.ShapeDtypeStruct
    return [sds((2, 4, n, d // 2), BF)] * 2 + [sds((4, 2, n, d // 2), BF)] * 2


def feed_grad_kernel(
    li, ri, me_ref, l_ref, lo_ref, lm_ref, r_ref, ro_ref, rm_ref, pack_ref, keep0, send0, keep1, send1,
    lt, sc
):
    seg, d = l_ref.shape
    turn(lt, (l_ref, lo_ref, lm_ref, pack_ref.at[li]))
    mp = lm_ref.shape[0]
    a, b, c, e = seg, 2 * seg, 2 * seg + mp, 2 * seg + 2 * mp
    for y in range(2):
        acc = nn(lt[:, 0:a], r_ref[y]) + nn(lt[:, a:b], ro_ref[y])
        acc += nn(lt[:, b:c], rm_ref[2 * y]) + nn(lt[:, c:e], pack_ref[ri + y])
        sc[...] = acc.astype(BF)
        spread_block(y, me_ref[1], sc, d // 8, keep0, send0, keep1, send1)


def feed_grad(me, left, left_o, left_m, right, right_o, right_m, pack_o, li, ri, deps=()):
    seg, d = left.shape
    mp = left_m.shape[0]
    args = (me, left, left_o, left_m, right, right_o, right_m, pack_o)
    return pl.pallas_call(
        after(functools.partial(feed_grad_kernel, li, ri), 8, len(deps)),
        out_shape=grad_shapes(d // 8, d),
        in_specs=[sm_spec()] + [vm_spec()] * 7 + [any_spec()] * len(deps),
        out_specs=[vm_spec()] * 4,
        scratch_shapes=[pltpu.VMEM((d, 2 * seg + 2 * mp), BF), pltpu.VMEM((d, d), BF)],
        compiler_params=params(30),
        cost_estimate=pl.CostEstimate(
            flops=8 * seg * d * d, bytes_accessed=16 * d * d, transcendentals=0
        ),
        name="feed_grad",
    )(*args, *deps)


def attention_grad_kernel(
    me_ref, tok_ref, toko_ref, m_ref, ge_ref, go_ref, gr1_ref, gr1o_ref, gr1m_ref, a_ref, ao_ref, am_ref,
    pack_ref, s_ref, so_ref, keep0, send0, keep1, send1, lt0, lt1, sc, rest
):
    seg, d = tok_ref.shape
    mp = m_ref.shape[0]
    keys = seg + mp
    w1 = HPB * HD
    chunk = d // 8
    me = me_ref[0]
    turn(lt0, (tok_ref, m_ref, toko_ref, pack_ref.at[7]))
    turn(lt1, (gr1_ref, gr1o_ref, gr1m_ref, pack_ref.at[3]))
    vecs = s_ref[0:8] + so_ref[0:8]
    a, b, c, e = seg, 2 * seg, 2 * seg + mp, 2 * seg + 2 * mp
    for y in range(2):
        x = nn(lt0[:, 0:keys], ge_ref[y]) + nn(lt0[:, keys:], go_ref[y])
        r = nn(lt1[:, 0:a], a_ref[y]) + nn(lt1[:, a:b], ao_ref[y])
        r += nn(lt1[:, b:c], am_ref[2 * y])
        r += nn(lt1[:, c:e], pack_ref[8, :, y * 4 * HD : (y + 1) * 4 * HD])
        sc[...] = jnp.concatenate([x, r[:, 0:w1]], axis=1).astype(BF)
        j = 2 * y
        bias = s_ref[12 + j : 13 + j] + so_ref[13 + j : 14 + j]
        up = s_ref[8 + j : 9 + j] + so_ref[9 + j : 10 + j]
        second = jnp.concatenate([bias[:, w1 : 2 * w1], vecs[6:7, 0 : d - w1]], axis=1)
        at = pl.multiple_of(16 + 8 * (j ^ me), 8)
        mem = s_ref[pl.ds(at, 8), :] + so_ref[pl.ds(at, 8), :]
        for i in range(8):
            part = [vecs[t : t + 1, i * chunk : (i + 1) * chunk] for t in range(6)]
            top = jnp.concatenate(part + [bias[:, 0:w1]], axis=1)
            rest[i] = jnp.concatenate([top, second, up, mem[0:5]], axis=0).astype(BF)
        spread_block(y, me_ref[1], sc, chunk, keep0, send0, keep1, send1, rest)


def attention_grad(
    me, tok, tok_o, m, ge, go, gr1, gr1_o, gr1m, a, a_o, am, pack_o, small, small_o, deps=()
):
    seg, d = tok.shape
    mp = m.shape[0]
    args = (me, tok, tok_o, m, ge, go, gr1, gr1_o, gr1m, a, a_o, am, pack_o, small, small_o)
    return pl.pallas_call(
        after(attention_grad_kernel, 15, len(deps)),
        out_shape=grad_shapes(d // 8 + 8, d),
        in_specs=[sm_spec()] + [vm_spec()] * 14 + [any_spec()] * len(deps),
        out_specs=[vm_spec()] * 4,
        scratch_shapes=[
            pltpu.VMEM((d, 2 * seg + 2 * mp), BF),
            pltpu.VMEM((d, 2 * seg + 2 * mp), BF),
            pltpu.VMEM((d, d), BF),
            pltpu.VMEM((8, 8, d), BF),
        ],
        compiler_params=params(34),
        cost_estimate=pl.CostEstimate(
            flops=8 * seg * d * d, bytes_accessed=16 * d * d, transcendentals=0
        ),
        name="attention_grad",
    )(*args, *deps)


def plus(a, b):
    return (a.astype(F32) + b.astype(F32)).astype(BF)


def sum_xy_kernel(me_ref, keep0, recv0, keep1, recv1, ak, as_, bk, bs):
    xb = me_ref[1]
    for z in range(4):
        ak[z] = plus(keep0[0, z], recv0[0, z])
        as_[z] = plus(keep0[1, z], recv0[1, z])
        bk[z] = plus(keep1[z, xb], recv1[z, xb])
        bs[z] = plus(keep1[z, 1 - xb], recv1[z, 1 - xb])


def sum_yx_kernel(me_ref, ak, ar, bk, br, *outs):
    z = me_ref[2]
    for i, o in enumerate(outs):
        t = (z + i) % 4
        o[0] = plus(ak[t], ar[t])
        o[1] = plus(bk[t], br[t])


def sum_z(refs):
    halves = []
    for h in range(2):
        t = refs[0][h].astype(F32)
        for r in refs[1:]:
            t = t + r[h].astype(F32)
        halves.append(t)
    return jnp.concatenate(halves, axis=1)


def up_kernel(a, b, c, e, o):
    o[...] = sum_z((a, b, c, e))


def attention_kernel(a, b, c, e, q, k, v, o, rest):
    t = sum_z((a, b, c, e))
    n, w1 = q.shape
    q[...] = t[0:n, 0:w1]
    k[...] = t[0:n, w1 : 2 * w1]
    v[...] = t[0:n, 2 * w1 : 3 * w1]
    o[...] = t[0:n, 3 * w1 : 4 * w1].T
    rest[...] = t[n:]


def small_call(kernel, shapes, args, name, scalars=False, deps=()):
    return pl.pallas_call(
        after(kernel, len(args), len(deps)),
        out_shape=shapes,
        in_specs=([sm_spec()] if scalars else [])
        + [vm_spec()] * (len(args) - scalars)
        + [any_spec()] * len(deps),
        out_specs=[vm_spec()] * len(shapes),
        compiler_params=params(12),
        name=name,
    )(*args, *deps)


def pack_kernel(q_ref, k_ref, v_ref, o_ref, u_ref, d_ref, out_ref):
    n, w1 = q_ref.shape
    d = u_ref.shape[1]
    for i, r in enumerate((q_ref, k_ref, v_ref)):
        out_ref[:, i * w1 : (i + 1) * w1] = r[...]
    out_ref[:, 3 * w1 : 4 * w1] = o_ref[...].astype(F32).T.astype(BF)
    out_ref[:, d : 2 * d] = u_ref[...]
    out_ref[:, 2 * d : 3 * d] = d_ref[...].astype(F32).T.astype(BF)


def pack(*weights):
    n = weights[0].shape[0]
    d = weights[4].shape[1]
    return pl.pallas_call(
        pack_kernel,
        out_shape=jax.ShapeDtypeStruct((n, 3 * d), BF),
        in_specs=[vm_spec()] * 6,
        out_specs=vm_spec(),
        name="pack",
    )(*weights)


def flip(a, axis, bit):
    return lax.ppermute(a, axis, [(i, i ^ bit) for i in range(lax.axis_size(axis))])


def shift(a, by):
    n = lax.axis_size("dp")
    return lax.ppermute(a, "dp", [(i, (i + by) % n) for i in range(n)])


def pick(a, i, axis):
    return lax.dynamic_index_in_dim(a, i, axis, keepdims=False)


def start_xy(keep0, send0, keep1, send1):
    return keep0, flip(send0, "dp", 1), keep1, flip(send1, "mp", 2)


def middle_xy(place, parts, deps=()):
    _, nz, n, half = parts[0].shape
    shape = jax.ShapeDtypeStruct((nz, n, half), BF)
    ak, as_, bk, bs = small_call(sum_xy_kernel, [shape] * 4, (place, *parts), "sum_xy", True, deps)
    return ak, flip(as_, "mp", 2), bk, flip(bs, "dp", 1)


def start_z(place, parts, deps=()):
    _, n, half = parts[0].shape
    shape = jax.ShapeDtypeStruct((2, n, half), BF)
    own, up, far, down = small_call(sum_yx_kernel, [shape] * 4, (place, *parts), "sum_yx", True, deps)
    return own, shift(far, 4), shift(up, 2), shift(down, -2)


def exchange(x):
    me = lax.axis_index("mp")
    nb = x.shape[0]
    got = [pick(x, me, 0)]
    for i in range(1, nb):
        got.append(flip(pick(x, me ^ i, 0), "mp", i))
    return relative(jnp.stack(got))


def relative(x):
    me = lax.axis_index("mp")
    v = x.reshape((2, 2) + x.shape[1:])
    v = jnp.where(me % 2 == 1, v[:, ::-1], v)
    v = jnp.where(me // 2 == 1, v[::-1], v)
    return v.reshape(x.shape)


def gather_small(x):
    nd = lax.axis_size("dp")
    nb = lax.axis_size("mp")
    if nd != 8:
        return lax.all_gather(x, ("mp", "dp"), axis=0).reshape(nb, nd, -1)
    k = x.shape[0]
    t = x.reshape(1, k)
    me = lax.axis_index("dp")
    b = me % 2
    z = me // 2
    o = flip(t, "mp", 1)
    c = lax.axis_index("mp") % 2
    t = jnp.where(c == 0, jnp.concatenate([t, o]), jnp.concatenate([o, t]))
    o = flip(t, "mp", 2)
    y = lax.axis_index("mp") // 2
    t = jnp.where(y == 0, jnp.concatenate([t, o]), jnp.concatenate([o, t]))
    o = flip(t, "dp", 1)
    t = jnp.where(b == 0, jnp.stack([t, o]), jnp.stack([o, t]))
    up, down, far = shift(t, -2), shift(t, 2), shift(t, 4)
    ring = jnp.stack([t, up, far, down, t, up, far])
    t = lax.dynamic_slice_in_dim(ring, (4 - z) % 4, 4, 0)
    return t.reshape(nd, nb, k).transpose(1, 0, 2)


def body(
    tokens, memory_init, query_weight, query_bias, key_weight, value_weight, value_bias, out_weight,
    out_bias, first_gain, first_shift, up_weight, up_bias, down_weight, down_bias, second_gain,
    second_shift, cotangent, group_segs, chain_group
):
    nd = lax.axis_size("dp")
    nb = lax.axis_size("mp")
    me = lax.axis_index("mp")
    dp = lax.axis_index("dp")
    tuned = nd == 8
    place = [me, dp % 2, dp // 2] if tuned else [me, 0 * me, 0 * me]
    me1 = jnp.stack(place).astype(jnp.int32)
    segments = tokens.shape[1]
    d = tokens.shape[3]
    part = tokens.shape[2]
    seg = part * nb
    nmem = memory_init.shape[0] * nb
    pad = -(-nmem // 16) * 16
    both = ("mp", "dp")
    wl = pack(query_weight, key_weight, value_weight, out_weight, up_weight, down_weight)
    w = lax.all_gather(wl, both, axis=0).reshape(nb, d, 3 * d)
    vecs = (out_bias, first_gain, first_shift, down_bias, second_gain, second_shift)
    small = jnp.concatenate(
        (query_bias, value_bias, up_bias) + vecs + (memory_init.reshape(-1),)
    )
    n1 = query_bias.shape[0]
    n2 = up_bias.shape[0]
    sg = gather_small(small)
    qb = sg[:, :, 0:n1].reshape(nb, 1, -1).astype(F32)
    vb = sg[:, :, n1 : 2 * n1].reshape(nb, 1, -1).astype(F32)
    qkvb = jnp.concatenate([qb, jnp.zeros_like(qb), vb], axis=2)
    ub = sg[:, :, 2 * n1 : 2 * n1 + n2].reshape(nb, 1, -1).astype(F32)
    at = 2 * n1 + n2
    vec = sg[:, :, at : at + 6 * n1].reshape(nb, nd, 6, n1).transpose(2, 1, 0, 3).reshape(6, d)
    vec = jnp.pad(vec.astype(F32), ((0, 2), (0, 0)))
    ml = memory_init.shape[0]
    m0 = sg[:, :, at + 6 * n1 :].reshape(nb, nd, ml, -1).transpose(0, 2, 1, 3).reshape(nmem, d)
    m0 = jnp.pad(m0.astype(F32), ((0, pad - nmem), (0, 0)))
    tok = exchange(tokens[0]).reshape(seg, d)
    ct = exchange(cotangent[0]).reshape(seg, d)
    match = chain_group[:, None] == jnp.arange(group_segs.shape[0], dtype=jnp.int32)[None, :]
    count = jnp.sum(jnp.where(match, group_segs[None, :], 0))
    live = (me < count).astype(F32)
    live2 = jnp.full((8, 128), live, F32)
    q, k, v = qkv_call(me1, tok, w, qkvb)
    m = jnp.where(me == 0, m0, 0.0)
    own = m
    saved = ()
    for s in range(segments - 1):
        z, *saved = mem_forward(me1, m, k, v, w, qkvb, ub, vec, nmem, s, saved)
        m = lax.ppermute(z, "mp", [(s, s + 1)])
        own = own + m
    (out, z1b, a0, a1, g0, g1, gf0, gf1, gr2b, gr1, gr1b, gq, gk, gv, base, sm, ubg) = token_call(
        me1, tok, ct, live2, own, q, k, v, w, qkvb, ub, vec, nmem
    )
    am, z1m, g_m = saved[4:7]
    send = base
    gin = jnp.zeros_like(base)
    for s in reversed(range(segments - 1)):
        recv = lax.ppermute(send, "mp", [(s + 1, s)])
        gin = gin + recv
        if s > 0:
            send = mem_backward(me1, recv, k, v, w, vec, base, saved)
    (z2m,) = mem_forward(
        me1, own, k, v, w, qkvb, ub, vec, nmem, None, (), (send,), (saved[11],)
    )
    other = lambda x: flip(x, "mp", 1)
    sends, _ = lax.optimization_barrier(((z1b, gf1, gr2b, g1, gr1b, a1), (recv, z2m)))
    z1b_o, gf_o, gr2b_o, g_o, gr1b_o, a_o = [other(x) for x in sends]
    tok_o = other(tok)
    gr2m, gfm, gr1m, smm, ubgm, extra = last_feed(me1, gin, w, vec, saved, own, (z2m,))
    extra_o = other(extra)
    up_g = feed_grad(me1, z1b, z1b_o, z1m, gf0, gf_o, gfm, extra_o, 4, 0)
    down_g = feed_grad(me1, gr2b, gr2b_o, gr2m, g0, g_o, g_m, extra_o, 2, 5, (up_g[0],))
    chains = nd * tokens.shape[0]
    w1 = d // nb
    chunk = d // nd
    small, ge, go, ig = last_attention(
        me1, gr1m, k, v, w, saved, gq, gk, gv, gr1, sm, smm, ubg, ubgm, z2m, live2, nmem, chains,
        (down_g[0],),
    )
    deps = ()
    if tuned:
        up_s = start_xy(*up_g)
        small, ge, go, ig, up_s = lax.optimization_barrier((small, ge, go, ig, up_s))
        up_s = middle_xy(me1, up_s)
        down_s = start_xy(*down_g)
        deps = (up_s[0],)
    att_g = attention_grad(
        me1, tok, tok_o, own, ge, other(go), gr1b, gr1b_o, gr1m, a0, a_o, am, extra_o, small,
        other(small), deps,
    )
    sds = jax.ShapeDtypeStruct
    if tuned:
        up_s, down_s, att_g, ig = lax.optimization_barrier((up_s, down_s, att_g, ig))
        up_s = start_z(me1, up_s)
        down_s = middle_xy(me1, down_s)
        att_s = start_xy(*att_g)
        up_s, down_s, att_s, out = lax.optimization_barrier((up_s, down_s, att_s, out))
        att_s = middle_xy(me1, att_s)
        down_s = start_z(me1, down_s)
        layer_out = exchange(out.reshape(nb, part, d))
        (wup,) = small_call(up_kernel, [sds((chunk, d), F32)], up_s, "up_out")
        down_s, att_s, wup, ig = lax.optimization_barrier((down_s, att_s, wup, ig))
        att_s = start_z(me1, att_s)
        input_grad = exchange(ig.reshape(nb, part, d))
        (wdn,) = small_call(up_kernel, [sds((chunk, d), F32)], down_s, "down_out")
        wdn = wdn.T
        wq, wk, wv, wo, rest = small_call(
            attention_kernel,
            [sds((chunk, w1), F32)] * 3 + [sds((w1, chunk), F32), sds((8, d), F32)],
            att_s,
            "attention_out",
        )
        vg = lax.dynamic_slice(rest[0, 0 : 6 * chunk].reshape(6, chunk), (0, me * n1), (6, n1))
        qbg = lax.dynamic_slice(rest[0, 6 * chunk :], (dp * n1,), (n1,))
        vbg = lax.dynamic_slice(rest[1, 0:w1], (dp * n1,), (n1,))
        ubt = lax.dynamic_slice(rest[2], (dp * n2,), (n2,))
        gmi = lax.dynamic_slice(rest[3 : 3 + ml], (0, dp * chunk), (ml, chunk))
        norms = rest[1, w1 : w1 + segments]
    else:
        layer_out = exchange(out.reshape(nb, part, d))
        input_grad = exchange(ig.reshape(nb, part, d))

        def scatter(keep0, send0, keep1, send1):
            left = jnp.stack([keep0, send0], axis=2)
            right = jnp.stack([keep1, send1])
            x = jnp.concatenate([left, right], axis=4)[:, :, :, 0 : d // 8]
            x = x.reshape(2, nd, chunk, d).astype(F32)
            x = lax.psum_scatter(x, "dp", scatter_dimension=1, tiled=True)
            return (x[0] + flip(x[1], "mp", 2)).reshape(chunk, d)

        wup, wdn, watt = scatter(*up_g), scatter(*down_g).T, scatter(*att_g)
        wq, wk, wv = [watt[:, i * w1 : (i + 1) * w1] for i in range(3)]
        wo = watt[:, 3 * w1 :].T
        rows = jnp.concatenate(
            [small[0:8], relative(small[8:12]), relative(small[12:16]), small[16:]]
        )
        rows = lax.psum(rows, both)
        vg = lax.dynamic_slice(rows, (0, dp * chunk + me * n1), (6, n1))
        qbg = lax.dynamic_slice(rows, (12 + me, dp * n1), (1, n1))[0]
        vbg = lax.dynamic_slice(rows, (12 + me, w1 + dp * n1), (1, n1))[0]
        ubt = lax.dynamic_slice(rows, (8 + me, dp * n2), (1, n2))[0]
        gmi = lax.dynamic_slice(rows, (16 + 8 * me, dp * chunk), (ml, chunk))
        norms = rows[6, 0:segments]
    return (
        layer_out[None],
        input_grad[None],
        gmi,
        wq,
        qbg,
        wk,
        wv,
        vbg,
        wo,
        vg[0],
        vg[1],
        vg[2],
        wup,
        ubt,
        wdn,
        vg[3],
        vg[4],
        vg[5],
        norms,
    )


def solution(mesh):
    rows = P("dp", None, "mp", None)
    md, dm = P(("mp", "dp")), P(("dp", "mp"))
    win, wout = P("dp", "mp"), P("mp", "dp")
    in_specs = (
        rows, wout, win, md, win, win, md, wout, dm, dm, dm, win, md, wout, dm, dm, dm, rows, P(),
        P("dp"),
    )
    out_specs = (
        rows, rows, wout, win, md, win, win, md, wout, dm, dm, dm, win, md, wout, dm, dm, dm, P(),
    )
    return jax.shard_map(body, mesh=mesh, in_specs=in_specs, out_specs=out_specs, check_vma=False)
```
